32 devices in a mesh: ctx: 16 (over z, y, x), fsdp: 2 (over core).
Axes of the slice: x: 2, y: 2, z: 4, core: 2. Of those that a mesh axis runs over, the one named last changes fastest.
Arguments:
- tokens: bfloat16 [2, 2048, 2304], P('fsdp', 'ctx'), may hold values from -6 to 6
- cotangent: bfloat16 [2, 2048, 2304], P('fsdp', 'ctx'), may hold values from -6 to 6
- pair_table: int32 [16], replicated, may hold values from 0 to 15, each once
- query_weight: bfloat16 [2304, 2048], P(None, ('ctx', 'fsdp')), may hold values from -0.20833333 to 0.20833333
- key_weight: bfloat16 [2304, 1024], P(None, ('ctx', 'fsdp')), may hold values from -0.20833333 to 0.20833333
- value_weight: bfloat16 [2304, 1024], P(None, ('ctx', 'fsdp')), may hold values from -0.125 to 0.125
- output_weight: bfloat16 [2048, 2304], P(('ctx', 'fsdp')), may hold values from -0.125 to 0.125
- gate_weight: bfloat16 [2304, 9216], P(None, ('ctx', 'fsdp')), may hold values from -0.125 to 0.125
- up_weight: bfloat16 [2304, 9216], P(None, ('ctx', 'fsdp')), may hold values from -0.125 to 0.125
- down_weight: bfloat16 [9216, 2304], P(('ctx', 'fsdp')), may hold values from -0.0625 to 0.0625
- norm_scales: bfloat16 [4, 2304], replicated, may hold values from 0.099609375 to 1.8984375
Outputs:
- output: bfloat16 [2, 2048, 2304], P('fsdp', 'ctx')
- input_grad: bfloat16 [2, 2048, 2304], P('fsdp', 'ctx')
- query_weight_grad: float32 [2304, 2048], P(None, ('ctx', 'fsdp'))
- key_weight_grad: float32 [2304, 1024], P(None, ('ctx', 'fsdp'))
- value_weight_grad: float32 [2304, 1024], P(None, ('ctx', 'fsdp'))
- output_weight_grad: float32 [2048, 2304], P(('ctx', 'fsdp'))
- gate_weight_grad: float32 [2304, 9216], P(None, ('ctx', 'fsdp'))
- up_weight_grad: float32 [2304, 9216], P(None, ('ctx', 'fsdp'))
- down_weight_grad: float32 [9216, 2304], P(('ctx', 'fsdp'))
- scale_grad: float32 [4, 2304], P(None, ('ctx', 'fsdp'))
The draws below stay inside these ranges and needn't reach their ends.
Inputs may be any that keep to these rules, and one draw needn't show every extreme that they name: Each index of ctx holds position blocks pair_table[index] and 31 - pair_table[index]; every value appears once.
All inputs are finite; a program needn't handle non-finite values.
Results may differ from the reference program's by a relative error of at most 0.019.
The reference program's roundings to bfloat16 on the way count: a program that leaves them out, or rounds other values in their place, can miss the bound.
Values may be sent and summed in bfloat16 or wider, within the bound.
No kernel may reach another device: no remote copies, remote signals or barrier semaphores. Data moves between devices by JAX's collectives and lax.ppermute only.
A program may use at most 640 MiB of HBM per device.

```python
import jax
import jax.numpy as jnp
from jax import lax

D = 2304
HEADS = 8
KV_HEADS = 4
HEAD = 256
FF = 9216
TOK_DEV = 128
SEQS = 2
SEQ_LEN = 2048
BLK = 64
BLOCKS = 32
N_CTX = 16


def chosen_head(key):
    return jax.random.randint(jax.random.fold_in(key, 97), (), 0, KV_HEADS)


def draw_projection(key, columns, group_size, chosen):
    values = jnp.clip(jax.random.normal(key, (D, columns), jnp.float32), -4.0, 4.0)
    owners = jnp.arange(columns, dtype=jnp.int32) // HEAD // group_size
    factor = jnp.where(owners == chosen, 2.5, 1.0).astype(jnp.float32)
    return values * factor[None, :] * float(D) ** (-0.5)


def draw_query_weight(key, part):
    chosen = chosen_head(key)
    key = jax.random.fold_in(key, 11)
    return draw_projection(key, HEADS * HEAD, HEADS // KV_HEADS, chosen).astype(jnp.bfloat16)


def draw_key_weight(key, part):
    chosen = chosen_head(key)
    key = jax.random.fold_in(key, 23)
    return draw_projection(key, KV_HEADS * HEAD, 1, chosen).astype(jnp.bfloat16)


def shard_levels(rng, dims, shards, low, largest):
    loudness, own = 1.0, jax.random.fold_in(rng, 6)
    for dim, shards_of in shards:
        heights = jnp.exp(jax.random.uniform(jax.random.fold_in(own, dim), (shards_of,), jnp.float32, low / len(shards), largest / len(shards)))
        loudness = loudness * jnp.repeat(heights, dims[dim] // shards_of).reshape([-1 if axis == dim else 1 for axis in range(len(dims))])
    return loudness


def noise(rng, dims, deviation, most, pieces=(), kind=jnp.bfloat16):
    drawn = deviation * jax.random.normal(rng, dims, jnp.float32)
    if pieces:
        drawn = drawn * shard_levels(rng, dims, pieces, -0.22, 0.18)
    return jnp.clip(drawn, -most, most).astype(kind)


def setup_inputs(seed: int = 0) -> dict:
    key_list = jax.random.split(jax.random.key(seed), 12)
    tokens = noise(key_list[0], (SEQS, SEQ_LEN, D), 1.0, 6.0, ((0, 2), (1, 16)))
    cotangent = noise(key_list[1], (SEQS, SEQ_LEN, D), 1.0, 6.0, ((0, 2), (1, 16)))
    pair_table = jax.random.permutation(key_list[2], N_CTX).astype(jnp.int32)
    query_weight = draw_query_weight(jax.random.fold_in(key_list[11], 71), 0)
    key_weight = draw_key_weight(jax.random.fold_in(key_list[11], 71), 0)
    value_weight = noise(key_list[5], (D, KV_HEADS * HEAD), D ** -0.5, 0.125, ((1, 32),))
    output_weight = noise(key_list[6], (HEADS * HEAD, D), (HEADS * HEAD) ** -0.5, 0.125, ((0, 32),))
    gate_weight = noise(key_list[7], (D, FF), D ** -0.5, 0.125, ((1, 32),))
    up_weight = noise(key_list[8], (D, FF), D ** -0.5, 0.125, ((1, 32),))
    down_weight = noise(key_list[9], (FF, D), FF ** -0.5, 0.0625, ((0, 32),))
    norm_scales = jnp.clip(1.0 + 0.18 * jax.random.normal(key_list[10], (4, D), jnp.float32), 0.099609375, 1.8984375).astype(jnp.bfloat16)
    return dict(tokens=tokens, cotangent=cotangent, pair_table=pair_table, query_weight=query_weight, key_weight=key_weight, value_weight=value_weight, output_weight=output_weight, gate_weight=gate_weight, up_weight=up_weight, down_weight=down_weight, norm_scales=norm_scales)


EPSILON = 1e-06
SOFT_CAP = 50.0
QUERY_SCALE = 0.0625

@jax.custom_vjp
def low(v):
    return lax.optimization_barrier(v.astype(jnp.bfloat16)).astype(jnp.float32)

@jax.custom_vjp
def low_back(v):
    return v

def low_keep(v):
    return (low(v), None)

def low_pass(kept, grad):
    return (grad,)

def back_keep(v):
    return (v, None)

def back_low(kept, grad):
    return (low(grad),)
low.defvjp(low_keep, low_pass)
low_back.defvjp(back_keep, back_low)

def matmul_high(left, right):
    return jnp.dot(left, right, precision=lax.Precision.HIGHEST, preferred_element_type=jnp.float32)

def rms_norm(vector_in, scale_row):
    return vector_in * lax.rsqrt(lax.optimization_barrier(jnp.mean(vector_in * vector_in, axis=-1, keepdims=True)) + EPSILON) * scale_row

def rotate(matrix_in, positions, head_count):
    half_size = HEAD // 2
    frequency = 10000.0 ** (-jnp.arange(half_size, dtype=jnp.float32) * 2.0 / HEAD)
    angles = positions.astype(jnp.float32)[:, None] * frequency[None, :]
    cosine = jnp.cos(angles)[:, None, :]
    sine_table = jnp.sin(angles)[:, None, :]
    shaped = matrix_in.reshape(matrix_in.shape[0], head_count, HEAD)
    first_half = shaped[..., :half_size]
    second_half = shaped[..., half_size:]
    turned = jnp.concatenate([first_half * cosine - second_half * sine_table, second_half * cosine + first_half * sine_table], axis=-1)
    return turned.reshape(matrix_in.shape[0], head_count * HEAD)

def places(pair_table):
    row_ids = jnp.arange(SEQ_LEN, dtype=jnp.int32)
    owners = row_ids // TOK_DEV
    within = row_ids % TOK_DEV
    chosen = pair_table[owners]
    return jnp.where(within < BLK, chosen * BLK + within, (BLOCKS - 1 - chosen) * BLK + within - BLK).astype(jnp.int32)

def attend(queries, key_rows, value_rows, positions):
    group_size = HEADS // KV_HEADS
    query_block = min(512, SEQ_LEN)
    keys_shaped = key_rows.reshape(SEQ_LEN, KV_HEADS, HEAD)
    values_shaped = value_rows.reshape(SEQ_LEN, KV_HEADS, HEAD)
    query_blocks = queries.reshape(SEQ_LEN // query_block, query_block, KV_HEADS, group_size, HEAD)
    place_blocks = positions.reshape(SEQ_LEN // query_block, query_block)

    @jax.checkpoint
    def block_attend(operands):
        query_part, place_part = operands
        raw_scores = low_back(jnp.einsum('bgjd,kgd->gjbk', query_part, keys_shaped, precision=lax.Precision.HIGHEST))
        capped = SOFT_CAP * jnp.tanh(raw_scores / SOFT_CAP)
        allowed = positions[None, None, None, :] <= place_part[None, None, :, None]
        capped = jnp.where(allowed, capped, -1e+30)
        weights_soft = jax.nn.softmax(capped, axis=-1)
        return jnp.einsum('gjbk,kgd->bgjd', low(weights_soft), values_shaped, precision=lax.Precision.HIGHEST)
    outputs = lax.map(block_attend, (query_blocks, place_blocks))
    return outputs.reshape(SEQ_LEN, HEADS * HEAD)

def layer_forward(params, inputs, positions):
    query_weight, key_weight, value_weight, output_weight, gate_weight, up_weight, down_weight, scales = params
    normed_first = low(rms_norm(inputs, scales[0]))
    queries = low(rotate(low_back(matmul_high(normed_first, query_weight)), positions, HEADS) * QUERY_SCALE)
    key_rows = low(rotate(low_back(matmul_high(normed_first, key_weight)), positions, KV_HEADS))
    value_rows = low(low_back(matmul_high(normed_first, value_weight)))
    attn_out = low(low_back(attend(queries, key_rows, value_rows, positions)))
    branch_out = low_back(matmul_high(attn_out, output_weight))
    hidden = inputs + rms_norm(branch_out, scales[1])
    normed_second = low(rms_norm(hidden, scales[2]))
    gate_out = low_back(matmul_high(normed_second, gate_weight))
    up_out = low_back(matmul_high(normed_second, up_weight))
    mixed = low(jax.nn.gelu(gate_out, approximate=True) * up_out)
    ffn_out = low_back(matmul_high(mixed, down_weight))
    return hidden + rms_norm(ffn_out, scales[3])

def reference(tokens, cotangent, pair_table, query_weight, key_weight, value_weight, output_weight, gate_weight, up_weight, down_weight, norm_scales):
    positions = places(pair_table)
    params = tuple((weight_item.astype(jnp.float32) for weight_item in (query_weight, key_weight, value_weight, output_weight, gate_weight, up_weight, down_weight, norm_scales)))
    inputs = tokens.astype(jnp.float32)

    def forward(param_set, input_set):
        return lax.map(lambda sequence: layer_forward(param_set, sequence, positions), input_set)
    result, pull = jax.vjp(forward, params, inputs)
    param_grads, input_grads = pull(cotangent.astype(jnp.float32))
    return (result.astype(jnp.bfloat16), input_grads.astype(jnp.bfloat16), param_grads[0], param_grads[1], param_grads[2], param_grads[3], param_grads[4], param_grads[5], param_grads[6], param_grads[7])
```

```python
import jax
import jax.numpy as jnp
from jax import lax
from jax.sharding import Mesh, PartitionSpec as P

HEADS = 8
KV_HEADS = 4
HEAD = 256

EPSILON = 1e-06
SOFT_CAP = 50.0
QUERY_SCALE = 0.0625

LOW = jnp.bfloat16
WIDE = jnp.float32

EVERY = ("line", "plane", "fsdp")


def contract(left, right, left_dim, right_dim):
    return lax.dot_general(
        left, right, (((left_dim,), (right_dim,)), ((), ())), preferred_element_type=WIDE
    )


def inverse_root(matrix_in):
    return lax.rsqrt(jnp.mean(matrix_in * matrix_in, axis=-1, keepdims=True) + EPSILON)


def norm_back(matrix_in, inverse, scale_row, upstream):
    weighted = upstream * scale_row
    inner = jnp.mean(matrix_in * weighted, axis=-1, keepdims=True)
    back = inverse * weighted - matrix_in * (inverse * inverse * inverse) * inner
    return (back, jnp.sum(upstream * matrix_in * inverse, axis=0))


def rope_tables(positions):
    half_size = HEAD // 2
    frequency = 10000.0 ** (-jnp.arange(half_size, dtype=WIDE) * 2.0 / HEAD)
    angles = positions.astype(WIDE)[:, None] * frequency[None, :]
    return (jnp.cos(angles)[:, None, :], jnp.sin(angles)[:, None, :])


def rotate(matrix_in, cosine, sine_table, head_count, direction):
    row_count = matrix_in.shape[0]
    half_size = HEAD // 2
    shaped = matrix_in.reshape(row_count, head_count, HEAD)
    first_half = shaped[..., :half_size]
    second_half = shaped[..., half_size:]
    return jnp.concatenate(
        [
            first_half * cosine - direction * second_half * sine_table,
            second_half * cosine + direction * first_half * sine_table,
        ],
        axis=-1,
    )


def line_gather(block):
    count = lax.axis_size("line")
    place = lax.axis_index("line")
    up, down = block, block
    ups, downs = {}, {}
    for step in range(1, count):
        up = lax.ppermute(up, "line", [(z, z + 1) for z in range(step - 1, count - 1)])
        down = lax.ppermute(down, "line", [(z, z - 1) for z in range(1, count - step + 1)])
        ups[step], downs[step] = up, down
    slots = [block]
    for turn in range(1, count):
        slots.append(jnp.where(place + turn < count, downs[turn], ups[count - turn]))
    return jnp.concatenate(slots, axis=0)


def line_scatter(parts):
    count = lax.axis_size("line")
    up = parts[count - 1].astype(LOW)
    down = parts[1].astype(LOW)
    for step in range(1, count):
        up = lax.ppermute(up, "line", [(z, z + 1) for z in range(0, step)])
        down = lax.ppermute(down, "line", [(z, z - 1) for z in range(count - step, count)])
        if step < count - 1:
            up = (parts[count - 1 - step] + up.astype(WIDE)).astype(LOW)
            down = (parts[1 + step] + down.astype(WIDE)).astype(LOW)
            up, down = lax.optimization_barrier((up, down))
    return parts[0] + up.astype(WIDE) + down.astype(WIDE)


def swap(value, bits):
    count = lax.axis_size("plane")
    return lax.ppermute(value, "plane", [(b, b ^ bits) for b in range(count)])


def plane_order():
    count = lax.axis_size("plane")
    if count == 4:
        own = lax.axis_index("plane")
        return [own, own ^ 1, own ^ 2, own ^ 3]
    return list(range(count))


def plane_gather(block):
    if lax.axis_size("plane") != 4:
        return lax.all_gather(block, "plane", axis=0, tiled=True)
    half = block.shape[0] // 2
    one, two = swap(block, 1), swap(block, 2)
    first, second = swap(two[:half], 1), swap(one[half:], 2)
    return jnp.concatenate([block, one, two, first, second], axis=0)


def plane_scatter(total):
    count = lax.axis_size("plane")
    if count != 4:
        return lax.psum_scatter(total, "plane", scatter_dimension=0, tiled=True)
    rows = total.shape[0] // count
    half = rows // 2
    own, one, two, far = [total[i * rows : (i + 1) * rows] for i in range(count)]
    low_far = far.astype(LOW)
    for_two = swap(low_far[:half], 1).astype(WIDE)
    for_one = swap(low_far[half:], 2).astype(WIDE)
    send_one = jnp.concatenate([one[:half], one[half:] + for_one], axis=0).astype(LOW)
    send_two = jnp.concatenate([two[:half] + for_two, two[half:]], axis=0).astype(LOW)
    return own + swap(send_one, 1).astype(WIDE) + swap(send_two, 2).astype(WIDE)


def sibling(value):
    return lax.ppermute(value, "fsdp", [(0, 1), (1, 0)])


def shards(
    tokens,
    cotangent,
    pair_table,
    query_weight,
    key_weight,
    value_weight,
    output_weight,
    gate_weight,
    up_weight,
    down_weight,
    norm_scales,
):
    line_count = lax.axis_size("line")
    plane_count = lax.axis_size("plane")
    fsdp_count = lax.axis_size("fsdp")
    sharers = plane_count * fsdp_count
    line_place = lax.axis_index("line")
    plane_place = lax.axis_index("plane")
    core = lax.axis_index("fsdp")
    devices = line_count * plane_count
    model = tokens.shape[2]
    row_count = tokens.shape[1]
    half_rows = row_count // 2
    span = line_count * row_count
    group_size = HEADS // KV_HEADS
    query_local = query_weight.shape[1]
    key_local = key_weight.shape[1]
    output_local = output_weight.shape[0]
    ff_local = gate_weight.shape[1]
    query_width = query_local * sharers
    key_width = key_local * sharers

    tokens_own = tokens[0]
    tokens_line = line_gather(tokens_own)

    attn_local = jnp.concatenate(
        [jnp.concatenate([query_weight, key_weight, value_weight], axis=1).T, output_weight], axis=0
    )
    attn_all = lax.all_gather(attn_local, ("plane", "fsdp"), axis=0, tiled=False)
    paired_local = jnp.concatenate([gate_weight.T, up_weight.T], axis=0)
    paired_all = lax.all_gather(paired_local, ("fsdp", "plane"), axis=0, tiled=True)
    down_all = lax.all_gather(down_weight, ("fsdp", "plane"), axis=0, tiled=True)

    edge_one = query_local
    edge_two = edge_one + key_local
    edge_three = edge_two + key_local
    projection = jnp.concatenate(
        [
            attn_all[:, :edge_one].reshape(-1, model),
            attn_all[:, edge_one:edge_two].reshape(-1, model),
            attn_all[:, edge_two:edge_three].reshape(-1, model),
        ],
        axis=0,
    )
    output_all = attn_all[:, edge_three:].reshape(-1, model)

    offsets = jnp.arange(row_count, dtype=jnp.int32)

    def place_rows(line_index, plane_index):
        pair = pair_table[line_index * plane_count + plane_index]
        return jnp.where(
            offsets < half_rows,
            pair * half_rows + offsets,
            (2 * devices - 1 - pair) * half_rows + offsets - half_rows,
        )

    line_order = [(line_place + turn) % line_count for turn in range(line_count)]
    positions = jnp.concatenate([place_rows(line, plane_place) for line in line_order])
    key_positions = jnp.concatenate(
        [place_rows(line, plane) for plane in plane_order() for line in line_order]
    )
    cosine, sine_table = rope_tables(positions)
    scales = norm_scales.astype(WIDE)

    wide_line = tokens_line.astype(WIDE)
    inverse_line = inverse_root(wide_line)
    unit_line = wide_line * inverse_line
    normed_first = (unit_line * scales[0]).astype(LOW)

    raw = contract(normed_first, projection, 1, 1)
    queries = (
        rotate(raw[:, :query_width], cosine, sine_table, group_size, 1.0) * QUERY_SCALE
    ).astype(LOW)
    key_rows = rotate(raw[:, query_width : query_width + key_width], cosine, sine_table, 1, 1.0)
    value_rows = raw[:, query_width + key_width :]
    both = jnp.concatenate([key_rows[:, 0].astype(LOW), value_rows.astype(LOW)], axis=1)
    both_all = plane_gather(both)
    keys_all = both_all[:, :key_width]
    values_all = both_all[:, key_width:]

    allowed = key_positions[None, :] <= positions[:, None]
    stacked = queries.transpose(1, 0, 2).reshape(group_size * span, HEAD)
    bounded = jnp.tanh(contract(stacked, keys_all, 1, 1) * (1.0 / SOFT_CAP))
    allowed_all = jnp.concatenate([allowed] * group_size, axis=0)
    grown = jnp.where(allowed_all, jnp.exp(SOFT_CAP * bounded), 0.0)
    weights_soft = grown * (1.0 / jnp.sum(grown, axis=-1, keepdims=True))
    weights_low = weights_soft.astype(LOW)
    slope = weights_soft * (1.0 - bounded * bounded)
    attn_full = contract(weights_low, values_all, 1, 0)
    attn_low = (
        attn_full.astype(LOW).reshape(group_size, span, HEAD).transpose(1, 0, 2).reshape(span, -1)
    )

    branch_out = line_scatter(
        contract(attn_low, output_all, 1, 0).reshape(line_count, row_count, model)
    )

    inputs = tokens_own.astype(WIDE)
    inverse_two = inverse_root(branch_out)
    hidden = inputs + branch_out * inverse_two * scales[1]
    inverse_three = inverse_root(hidden)
    normed_second = line_gather((hidden * inverse_three * scales[2]).astype(LOW))

    pair_out = contract(paired_all, normed_second, 1, 1).reshape(sharers, 2 * ff_local, span)

    def mix(gate_in, up_in):
        return jax.nn.gelu(gate_in, approximate=True) * up_in

    gate_out = pair_out[:, :ff_local]
    up_out = pair_out[:, ff_local:]
    mixed = mix(gate_out, up_out).astype(LOW).reshape(sharers * ff_local, span)
    ffn_out = line_scatter(contract(mixed, down_all, 0, 0).reshape(line_count, row_count, model))

    inverse_four = inverse_root(ffn_out)
    result = hidden + ffn_out * inverse_four * scales[3]
    upstream = cotangent[0].astype(WIDE)
    ffn_grad, scale_four = norm_back(ffn_out, inverse_four, scales[3], upstream)
    ffn_grad_low = line_gather(ffn_grad.astype(LOW))

    mixed_grad = contract(down_all, ffn_grad_low, 1, 1).reshape(sharers, ff_local, span)
    _, gelu_pull = jax.vjp(mix, gate_out, up_out)
    gate_grad, up_grad = gelu_pull(mixed_grad)
    pair_grad = jnp.concatenate([gate_grad.astype(LOW), up_grad.astype(LOW)], axis=1).reshape(
        sharers * 2 * ff_local, span
    )
    second_grad = line_scatter(
        contract(pair_grad, paired_all, 0, 0).reshape(line_count, row_count, model)
    )

    def both_cores(value):
        amount = value.shape[0] // fsdp_count
        own = lax.dynamic_slice_in_dim(value, core * amount, amount, 0)
        away = lax.dynamic_slice_in_dim(value, (1 - core) * amount, amount, 0)
        return jnp.concatenate([own, sibling(away)], axis=1)

    down_grad = contract(
        both_cores(mixed), jnp.concatenate([ffn_grad_low, sibling(ffn_grad_low)], axis=0), 1, 0
    )
    down_share = lax.psum_scatter(
        down_grad.astype(LOW), "plane", scatter_dimension=0, tiled=True
    ).astype(WIDE)
    paired_weight_grad = contract(
        both_cores(pair_grad),
        jnp.concatenate([normed_second, sibling(normed_second)], axis=0),
        1,
        0,
    )
    paired_share = lax.psum_scatter(
        paired_weight_grad.astype(LOW), "plane", scatter_dimension=0, tiled=True
    ).astype(WIDE)

    hidden_part, scale_three = norm_back(hidden, inverse_three, scales[2], second_grad)
    hidden_grad = upstream + hidden_part
    branch_grad, scale_two = norm_back(branch_out, inverse_two, scales[1], hidden_grad)
    branch_grad_low = line_gather(branch_grad.astype(LOW))

    attn_grad = contract(branch_grad_low, output_all, 1, 1).astype(LOW)
    output_weight_grad = contract(attn_low, branch_grad_low, 0, 0)
    attn_grad = (
        attn_grad.reshape(span, group_size, HEAD)
        .transpose(1, 0, 2)
        .reshape(group_size * span, HEAD)
    )
    row_inner = jnp.sum(attn_grad.astype(WIDE) * attn_full, axis=-1, keepdims=True)
    weight_grad = contract(attn_grad, values_all, 1, 1)
    score_grad = (slope * (weight_grad - row_inner)).astype(LOW)
    key_grad = contract(score_grad, stacked, 0, 0)
    value_grad = contract(weights_low, attn_grad, 0, 0)
    query_grad = contract(score_grad, keys_all, 1, 0)
    own_grad = plane_scatter(jnp.concatenate([key_grad, value_grad], axis=1))

    query_grad = query_grad.reshape(group_size, span, HEAD).transpose(1, 0, 2)
    query_raw_low = (
        (rotate(query_grad, cosine, sine_table, group_size, -1.0) * QUERY_SCALE)
        .astype(LOW)
        .reshape(span, query_width)
    )
    key_raw_low = rotate(own_grad[:, :key_width], cosine, sine_table, 1, -1.0)[:, 0].astype(LOW)
    raw_low = jnp.concatenate([query_raw_low, key_raw_low, own_grad[:, key_width:].astype(LOW)], 1)
    first_part = contract(raw_low, projection, 1, 0)
    scale_one = jnp.sum(first_part * unit_line, axis=0)
    first_grad = line_scatter(first_part.reshape(line_count, row_count, model))

    projection_grad = contract(raw_low, normed_first, 0, 0).astype(LOW)
    attn_weight_grad = jnp.concatenate(
        [
            projection_grad[:query_width].reshape(sharers, query_local, model),
            projection_grad[query_width : query_width + key_width].reshape(
                sharers, key_local, model
            ),
            projection_grad[query_width + key_width :].reshape(sharers, key_local, model),
            output_weight_grad.astype(LOW).reshape(sharers, output_local, model),
        ],
        axis=1,
    )
    attn_share = lax.psum_scatter(
        attn_weight_grad.reshape(-1, model), ("plane", "fsdp"), scatter_dimension=0, tiled=True
    ).astype(WIDE)

    input_part, _ = norm_back(inputs, inverse_root(inputs), scales[0], first_grad)
    input_grad = hidden_grad + input_part

    scale_grads = jnp.stack([scale_one, scale_two, scale_three, scale_four], axis=0)
    all_count = devices * fsdp_count
    scale_cut = scale_grads.reshape(4, all_count, -1).transpose(1, 0, 2).reshape(all_count, -1)
    scale_share = jnp.sum(lax.all_to_all(scale_cut, EVERY, 0, 0, tiled=True), axis=0).reshape(4, -1)

    return (
        result.astype(LOW)[None],
        input_grad.astype(LOW)[None],
        attn_share[:edge_one].T,
        attn_share[edge_one:edge_two].T,
        attn_share[edge_two:edge_three].T,
        attn_share[edge_three:],
        paired_share[:ff_local].T,
        paired_share[ff_local:].T,
        down_share,
        scale_share,
    )


def solution(mesh):
    devices, fsdp_count = mesh.devices.shape
    inner = Mesh(
        mesh.devices.reshape(KV_HEADS, devices // KV_HEADS, fsdp_count), EVERY
    )
    rows = P("fsdp", ("line", "plane"), None)
    return jax.shard_map(
        shards,
        mesh=inner,
        in_specs=(
            rows,
            rows,
            P(),
            P(None, EVERY),
            P(None, EVERY),
            P(None, EVERY),
            P(EVERY, None),
            P(None, EVERY),
            P(None, EVERY),
            P(EVERY, None),
            P(),
        ),
        out_specs=(
            rows,
            rows,
            P(None, EVERY),
            P(None, EVERY),
            P(None, EVERY),
            P(EVERY, None),
            P(None, EVERY),
            P(None, EVERY),
            P(EVERY, None),
            P(None, EVERY),
        ),
        check_vma=False,
    )
```

```python
import functools

import jax
import jax.numpy as jnp
from jax import lax
from jax.experimental import pallas as pl
from jax.experimental.pallas import tpu as pltpu
from jax.sharding import Mesh, PartitionSpec as P

HEADS = 8
KV_HEADS = 4
HEAD = 256

EPSILON = 1e-06
SOFT_CAP = 50.0
QUERY_SCALE = 0.0625

LOW = jnp.bfloat16
WIDE = jnp.float32

EVERY = ("line", "plane", "fsdp")


def contract(left, right, left_dim, right_dim):
    return lax.dot_general(
        left, right, (((left_dim,), (right_dim,)), ((), ())), preferred_element_type=WIDE
    )


def inverse_root(matrix_in):
    return lax.rsqrt(jnp.mean(matrix_in * matrix_in, axis=-1, keepdims=True) + EPSILON)


def norm_back(matrix_in, inverse, scale_row, upstream):
    weighted = upstream * scale_row
    inner = jnp.mean(matrix_in * weighted, axis=-1, keepdims=True)
    return inverse * weighted - matrix_in * (inverse * inverse * inverse) * inner


def rope_tables(positions):
    half_size = HEAD // 2
    frequency = 10000.0 ** (-jnp.arange(half_size, dtype=WIDE) * 2.0 / HEAD)
    angles = positions.astype(WIDE)[:, None] * frequency[None, :]
    return (jnp.cos(angles), jnp.sin(angles))


VMEM_LIMIT = 56 * 1024 * 1024
COST = pl.CostEstimate(flops=0, bytes_accessed=64 * 1024 * 1024, transcendentals=0)


def params():
    return pltpu.CompilerParams(vmem_limit_bytes=VMEM_LIMIT)


def project_kernel(
    rows_ref, weight_ref, scale_ref, cos_ref, sin_ref, normed_ref, query_ref, pair_ref, *scratch
):
    key_width = pair_ref.shape[1] // 2
    query_width = query_ref.shape[0] // rows_ref.shape[0] * HEAD
    span = rows_ref.shape[0]
    packed = weight_ref
    if scratch:
        packed = scratch[0]
        sharers = weight_ref.shape[0]
        query_local, key_local = query_width // sharers, key_width // sharers
        for j in range(sharers):
            packed[j * query_local : (j + 1) * query_local] = weight_ref[j, :query_local]
            at = query_width + j * key_local
            from_row = query_local
            for _ in range(2):
                packed[at : at + key_local] = weight_ref[j, from_row : from_row + key_local]
                at += key_width
                from_row += key_local
    rows = rows_ref[...].astype(WIDE)
    inverse = lax.rsqrt(jnp.mean(rows * rows, axis=-1, keepdims=True) + EPSILON)
    normed = (rows * inverse * scale_ref[...]).astype(LOW)
    normed_ref[...] = normed
    cosine, sine_table = cos_ref[...], sin_ref[...]
    half = HEAD // 2

    def turn(raw):
        first, second = raw[:, :half], raw[:, half:]
        return first * cosine - second * sine_table, second * cosine + first * sine_table

    for head in range(query_width // HEAD):
        raw = contract(normed, packed[head * HEAD : (head + 1) * HEAD], 1, 1)
        first, second = turn(raw)
        query_ref[head * span : (head + 1) * span, :half] = (first * QUERY_SCALE).astype(LOW)
        query_ref[head * span : (head + 1) * span, half:] = (second * QUERY_SCALE).astype(LOW)
    raw = contract(normed, packed[query_width:], 1, 1)
    first, second = turn(raw[:, :key_width])
    pair_ref[:, :half] = first.astype(LOW)
    pair_ref[:, half:key_width] = second.astype(LOW)
    pair_ref[:, key_width:] = raw[:, key_width:].astype(LOW)


def project_call(rows, weights, scale_row, cosine, sine_table, query_width, key_width):
    span, model = rows.shape
    heads = query_width // HEAD
    return pl.pallas_call(
        project_kernel,
        out_shape=(
            jax.ShapeDtypeStruct((span, model), LOW),
            jax.ShapeDtypeStruct((heads * span, HEAD), LOW),
            jax.ShapeDtypeStruct((span, 2 * key_width), LOW),
        ),
        scratch_shapes=[pltpu.VMEM((query_width + 2 * key_width, model), LOW)]
        if weights.ndim == 3
        else [],
        compiler_params=params(),
        cost_estimate=COST,
    )(rows, weights, scale_row, cosine, sine_table)


KEY_BLOCK = 2048


def as_row(column):
    return jnp.broadcast_to(column, (column.shape[0], 128)).T[:1]


def attend_kernel(query_ref, pair_ref, place_ref, key_place_ref, out_ref, low_ref, inverse_ref):
    keys = pair_ref[:, :HEAD]
    values = pair_ref[:, HEAD:]
    bounded = jnp.tanh(contract(query_ref[...], keys, 1, 1) * (1.0 / SOFT_CAP))
    allowed = key_place_ref[...] <= place_ref[...]
    grown = jnp.where(allowed, jnp.exp(SOFT_CAP * bounded), 0.0)
    inverse = 1.0 / jnp.sum(grown, axis=-1, keepdims=True)
    weights = (grown * inverse).astype(LOW)
    out = contract(weights, values, 1, 0)
    out_ref[...] = out
    low_ref[...] = out.astype(LOW)
    inverse_ref[...] = as_row(inverse)


def attend_call(queries, pair, places_column, key_places_row, group_size):
    count = queries.shape[0]
    span = count // group_size
    keys = pair.shape[0]
    by_head = pl.BlockSpec((span, HEAD), lambda h: (0, h))
    return pl.pallas_call(
        attend_kernel,
        grid=(group_size,),
        in_specs=[
            pl.BlockSpec((span, HEAD), lambda h: (h, 0)),
            pl.BlockSpec((keys, 2 * HEAD), lambda h: (0, 0)),
            pl.BlockSpec((span, 1), lambda h: (0, 0)),
            pl.BlockSpec((1, keys), lambda h: (0, 0)),
        ],
        out_specs=[by_head, by_head, pl.BlockSpec((1, span), lambda h: (0, h))],
        out_shape=(
            jax.ShapeDtypeStruct((span, group_size * HEAD), WIDE),
            jax.ShapeDtypeStruct((span, group_size * HEAD), LOW),
            jax.ShapeDtypeStruct((1, count), WIDE),
        ),
        compiler_params=params(),
        cost_estimate=COST,
    )(queries, pair, places_column, key_places_row)


def attend_back_kernel(*refs):
    query_ref, grad_ref, out_ref, pair_ref, inverse_ref, place_ref, key_place_ref = refs[:7]
    cos_ref, sin_ref, *prior_refs, query_grad_ref, pair_grad_ref, total_ref, held_ref = refs[7:]
    part, head = pl.program_id(0), pl.program_id(1)
    keys = pair_ref[:, :HEAD]
    values = pair_ref[:, HEAD:]
    queries = query_ref[...]
    grads = grad_ref[...]
    inner = as_row(jnp.sum(grads.astype(WIDE) * out_ref[...], axis=-1, keepdims=True))
    bounded = jnp.tanh(contract(keys, queries, 1, 1) * (1.0 / SOFT_CAP))
    allowed = key_place_ref[...] <= place_ref[...]
    weights = jnp.where(allowed, jnp.exp(SOFT_CAP * bounded) * inverse_ref[...], 0.0)
    weight_grad = contract(values, grads, 1, 1)
    score_grad = (weights * (weight_grad - inner) * (1.0 - bounded * bounded)).astype(LOW)
    query_part = contract(score_grad, keys, 0, 0)

    @pl.when(part == 0)
    def _():
        held_ref[head] = query_part

    @pl.when(part > 0)
    def _():
        held_ref[head] += query_part

    query_grad = held_ref[head]
    half = HEAD // 2
    first, second = query_grad[:, :half], query_grad[:, half:]
    cosine, sine_table = cos_ref[...], sin_ref[...]
    query_grad_ref[:, :half] = ((first * cosine + second * sine_table) * QUERY_SCALE).astype(LOW)
    query_grad_ref[:, half:] = ((second * cosine - first * sine_table) * QUERY_SCALE).astype(LOW)
    key_grad = contract(score_grad, queries, 1, 0)
    value_grad = contract(weights.astype(LOW), grads, 1, 0)

    @pl.when(head == 0)
    def _():
        if prior_refs:
            total_ref[:, :HEAD] = prior_refs[0][:, :HEAD] + key_grad
            total_ref[:, HEAD:] = prior_refs[0][:, HEAD:] + value_grad
        else:
            total_ref[:, :HEAD] = key_grad
            total_ref[:, HEAD:] = value_grad

    @pl.when(head > 0)
    def _():
        total_ref[:, :HEAD] += key_grad
        total_ref[:, HEAD:] += value_grad

    @pl.when(head == pl.num_programs(1) - 1)
    def _():
        pair_grad_ref[...] = total_ref[...].astype(pair_grad_ref.dtype)


def attend_back_call(
    queries, grads, out, pair, inverse, places_row, key_places_column, cosine, sine_table, prior, group_size
):
    count = queries.shape[0]
    span = count // group_size
    keys = pair.shape[0]
    block = min(keys, KEY_BLOCK)
    by_head = pl.BlockSpec((span, HEAD), lambda k, h: (0, h))
    by_keys = pl.BlockSpec((block, 2 * HEAD), lambda k, h: (k, 0))
    table = pl.BlockSpec((span, HEAD // 2), lambda k, h: (0, 0))
    extra = [] if prior is None else [prior]
    return pl.pallas_call(
        attend_back_kernel,
        grid=(keys // block, group_size),
        in_specs=[
            pl.BlockSpec((span, HEAD), lambda k, h: (h, 0)),
            by_head,
            by_head,
            by_keys,
            pl.BlockSpec((1, span), lambda k, h: (0, h)),
            pl.BlockSpec((1, span), lambda k, h: (0, 0)),
            pl.BlockSpec((block, 1), lambda k, h: (k, 0)),
            table,
            table,
        ]
        + [by_keys] * len(extra),
        out_specs=[by_head, by_keys],
        out_shape=(
            jax.ShapeDtypeStruct((span, group_size * HEAD), LOW),
            jax.ShapeDtypeStruct((keys, 2 * HEAD), WIDE if prior is None else LOW),
        ),
        scratch_shapes=[
            pltpu.VMEM((block, 2 * HEAD), WIDE),
            pltpu.VMEM((group_size, span, HEAD), WIDE),
        ],
        compiler_params=params(),
        cost_estimate=COST,
    )(queries, grads, out, pair, inverse, places_row, key_places_column, cosine, sine_table, *extra)


def project_back_kernel(
    query_ref, own_ref, one_ref, two_ref, weight_ref, cos_ref, sin_ref, raw_ref, part_ref
):
    query_width = query_ref.shape[1]
    total = own_ref[...].astype(WIDE) + one_ref[...].astype(WIDE) + two_ref[...].astype(WIDE)
    half = HEAD // 2
    first, second = total[:, :half], total[:, half:HEAD]
    cosine, sine_table = cos_ref[...], sin_ref[...]
    raw_ref[:, :query_width] = query_ref[...]
    raw_ref[:, query_width : query_width + half] = (first * cosine + second * sine_table).astype(LOW)
    raw_ref[:, query_width + half : query_width + HEAD] = (
        second * cosine - first * sine_table
    ).astype(LOW)
    raw_ref[:, query_width + HEAD :] = total[:, HEAD:].astype(LOW)
    part_ref[...] = contract(raw_ref[...], weight_ref[...], 1, 0)


def project_back_call(query_grad, own, one, two, weights, cosine, sine_table):
    span = query_grad.shape[0]
    width, model = weights.shape
    return pl.pallas_call(
        project_back_kernel,
        out_shape=(
            jax.ShapeDtypeStruct((span, width), LOW),
            jax.ShapeDtypeStruct((span, model), WIDE),
        ),
        compiler_params=params(),
        cost_estimate=COST,
    )(query_grad, own, one, two, weights, cosine, sine_table)


GELU_ROOT = 0.7978845608028654
GELU_CUBE = 0.044715


STEPS = 4


def blocks_of(value, count, first):
    rows = value.shape[0] // (2 * count)
    return jnp.concatenate(
        [value[(2 * p + first) * rows : (2 * p + first + 1) * rows] for p in range(count)], axis=0
    )


def widen_kernel(
    parts, core_ref, rows_ref, weight_ref, mixed_ref, away_ref, bent_ref, slope_ref
):
    step = pl.program_id(0)
    both = contract(weight_ref[...], rows_ref[...], 1, 1)
    gate, up = blocks_of(both, parts, 0), blocks_of(both, parts, 1)
    square = gate * gate
    curve = jnp.tanh(GELU_ROOT * gate * (1.0 + GELU_CUBE * square))
    rise = 0.5 * (1.0 + curve)
    bent = gate * rise
    mixed = (bent * up).astype(LOW)
    mixed_ref[...] = mixed
    bent_ref[...] = bent
    steep = GELU_ROOT * (1.0 + 3.0 * GELU_CUBE * square)
    slope_ref[...] = up * (rise + 0.5 * gate * (1.0 - curve * curve) * steep)

    @pl.when(step // (STEPS // 2) != core_ref[0])
    def _():
        away_ref[...] = mixed


def away_block(step, core_ref):
    first = (1 - core_ref[0]) * (STEPS // 2)
    return (jnp.clip(step - first, 0, STEPS // 2 - 1), 0)


def widen_call(rows, weights, core, sharers):
    span, model = rows.shape
    amount = weights.shape[0] // 2
    block = amount // STEPS
    by_step = pl.BlockSpec((block, span), lambda j, core_ref: (j, 0))
    return pl.pallas_call(
        functools.partial(widen_kernel, sharers // STEPS),
        grid_spec=pltpu.PrefetchScalarGridSpec(
            num_scalar_prefetch=1,
            grid=(STEPS,),
            in_specs=[
                pl.BlockSpec((span, model), lambda j, core_ref: (0, 0)),
                pl.BlockSpec((2 * block, model), lambda j, core_ref: (j, 0)),
            ],
            out_specs=[by_step, pl.BlockSpec((block, span), away_block), by_step, by_step],
        ),
        out_shape=(
            jax.ShapeDtypeStruct((amount, span), LOW),
            jax.ShapeDtypeStruct((amount // 2, span), LOW),
            jax.ShapeDtypeStruct((amount, span), WIDE),
            jax.ShapeDtypeStruct((amount, span), WIDE),
        ),
        compiler_params=params(),
        cost_estimate=COST,
    )(core, rows, weights)


def narrow_back_kernel(
    parts, core_ref, rows_ref, weight_ref, bent_ref, slope_ref, grad_ref, away_ref
):
    step = pl.program_id(0)
    mixed_grad = contract(weight_ref[...], rows_ref[...], 1, 1)
    gate, up = mixed_grad * slope_ref[...], mixed_grad * bent_ref[...]
    rows = gate.shape[0] // parts
    grad = jnp.concatenate(
        [part[p * rows : (p + 1) * rows] for p in range(parts) for part in (gate, up)], axis=0
    ).astype(LOW)
    grad_ref[...] = grad

    @pl.when(step // (STEPS // 2) != core_ref[0])
    def _():
        away_ref[...] = grad


def narrow_back_call(rows, weights, bent, slope, core, sharers):
    span, model = rows.shape
    amount = weights.shape[0]
    block = amount // STEPS
    by_step = pl.BlockSpec((block, span), lambda j, core_ref: (j, 0))
    return pl.pallas_call(
        functools.partial(narrow_back_kernel, sharers // STEPS),
        grid_spec=pltpu.PrefetchScalarGridSpec(
            num_scalar_prefetch=1,
            grid=(STEPS,),
            in_specs=[
                pl.BlockSpec((span, model), lambda j, core_ref: (0, 0)),
                pl.BlockSpec((block, model), lambda j, core_ref: (j, 0)),
                by_step,
                by_step,
            ],
            out_specs=[
                pl.BlockSpec((2 * block, span), lambda j, core_ref: (j, 0)),
                pl.BlockSpec((2 * block, span), away_block),
            ],
        ),
        out_shape=(
            jax.ShapeDtypeStruct((2 * amount, span), LOW),
            jax.ShapeDtypeStruct((amount, span), LOW),
        ),
        compiler_params=params(),
        cost_estimate=COST,
    )(core, rows, weights, bent, slope)


def weight_grad_kernel(core_ref, *refs):
    *pairs, out_ref = refs
    half = len(pairs) // 2
    total = contract(pairs[0][...], pairs[half][...], 1, 0)
    for left, right in zip(pairs[1:half], pairs[half + 1 :]):
        total += contract(left[...], right[...], 1, 0)
    out_ref[...] = total.astype(LOW)


def weight_grad_call(own, away, rows, core):
    span, model = rows[0].shape
    amount = own[0].shape[0] // 2
    block = amount // STEPS
    mine = pl.BlockSpec((block, span), lambda j, core_ref: (core_ref[0] * STEPS + j, 0))
    theirs = pl.BlockSpec((block, span), lambda j, core_ref: (j, 0))
    whole = pl.BlockSpec((span, model), lambda j, core_ref: (0, 0))
    return pl.pallas_call(
        weight_grad_kernel,
        grid_spec=pltpu.PrefetchScalarGridSpec(
            num_scalar_prefetch=1,
            grid=(STEPS,),
            in_specs=[mine] * len(own) + [theirs] * len(away) + [whole] * len(rows),
            out_specs=pl.BlockSpec((block, model), lambda j, core_ref: (j, 0)),
        ),
        out_shape=jax.ShapeDtypeStruct((amount, model), LOW),
        compiler_params=params(),
        cost_estimate=COST,
    )(core, *own, *away, *rows)


def shard_grad_kernel(parts, place_ref, *refs):
    *pairs, near_ref, away_ref, total_ref = refs
    half = len(pairs) // 2
    total = contract(pairs[0][...], pairs[half][...], 0, 0)
    for left, right in zip(pairs[1:half], pairs[half + 1 :]):
        total += contract(left[...], right[...], 0, 0)
    total_ref[...] = total.astype(LOW)
    own, core = place_ref[0], place_ref[1]
    planes = near_ref.shape[0]
    for plane in range(planes):
        for side in range(2):
            to_row = 0
            for first, rows in parts:
                block = total_ref[pl.ds(first + (2 * plane + side) * rows, rows)]

                @pl.when(core == side)
                def _():
                    near_ref[plane ^ own, pl.ds(to_row, rows)] = block

                @pl.when(core != side)
                def _():
                    away_ref[plane ^ own, pl.ds(to_row, rows)] = block

                to_row += rows


def shard_grad_call(left, right, parts, place, planes):
    width, model = left[0].shape[1], right[0].shape[1]
    rows = sum(part[1] for part in parts)
    shape = jax.ShapeDtypeStruct((planes, rows, model), LOW)
    return pl.pallas_call(
        functools.partial(shard_grad_kernel, parts),
        in_specs=[pl.BlockSpec(memory_space=pltpu.SMEM)]
        + [pl.BlockSpec(memory_space=pltpu.VMEM)] * (len(left) + len(right)),
        out_specs=[pl.BlockSpec(memory_space=pltpu.VMEM)] * 2,
        out_shape=(shape, shape),
        scratch_shapes=[pltpu.VMEM((width, model), LOW)],
        compiler_params=params(),
        cost_estimate=COST,
    )(place, *left, *right)


def tie(value, *others):
    return lax.optimization_barrier((value, others))[0]


def choose(flag, one, two):
    return jnp.where(flag, one, two)


def nothing(*others):
    return ()


def line_gather(block, work, while_first=nothing, while_last=nothing):
    place = lax.axis_index("line")
    up = lax.ppermute(block, "line", [(0, 1), (1, 2), (2, 3)])
    down = lax.ppermute(block, "line", [(1, 0), (2, 1), (3, 2)])
    done = while_first(lambda value: tie(value, block))
    up, down, done_first = lax.optimization_barrier((up, down, done))
    up_two = lax.ppermute(up, "line", [(1, 2), (2, 3)])
    down_two = lax.ppermute(down, "line", [(1, 0), (2, 1)])
    first = work(0, jnp.concatenate([block, choose(place >= 1, up, down)], axis=0))
    up_two, down_two = tie((up_two, down_two), first)
    up_three = lax.ppermute(up_two, "line", [(2, 3)])
    down_three = lax.ppermute(down_two, "line", [(1, 0)])
    done = while_last(lambda value: tie(value, up_two, down_two))
    up_three, down_three, done_last = lax.optimization_barrier((up_three, down_three, done))
    third = choose(place >= 2, up_two, down_two)
    fourth = choose(place == 0, down_three, choose(place == 3, up_three, down))
    second = work(1, jnp.concatenate([third, fourth], axis=0))
    return first, second, done_first, done_last


def line_order():
    place = lax.axis_index("line")
    return jnp.stack(
        [
            place,
            choose(place >= 1, place - 1, 1),
            lax.rem(place + 2, 4),
            choose(place >= 1, lax.rem(place + 1, 4), 3),
        ]
    ).astype(jnp.int32)


def line_scatter(late, work, while_second=nothing, while_last=nothing):
    place = lax.axis_index("line")
    rows = late.shape[0] // 2
    third, fourth = late[:rows], late[rows:]
    low_fourth = fourth.astype(LOW)
    up = lax.ppermute(low_fourth, "line", [(0, 1)])
    down = lax.ppermute(low_fourth, "line", [(3, 2)])
    up, down, (early, done_first) = lax.optimization_barrier((up, down, work()))
    own, second = early[:rows], early[rows:]
    up = (third + up.astype(WIDE)).astype(LOW)
    down = (third + down.astype(WIDE)).astype(LOW)
    sent_up, sent_down = lax.optimization_barrier((up, down))
    up = lax.ppermute(sent_up, "line", [(0, 1), (1, 2)])
    down = lax.ppermute(sent_down, "line", [(3, 2), (2, 1)])
    done = while_second(lambda value: tie(value, sent_up, sent_down), done_first)
    up, down, done_second = lax.optimization_barrier((up, down, done))
    up = (choose(place == 0, second, fourth) + up.astype(WIDE)).astype(LOW)
    down = (second + down.astype(WIDE)).astype(LOW)
    sent_up, sent_down = lax.optimization_barrier((up, down))
    up = lax.ppermute(sent_up, "line", [(0, 1), (1, 2), (2, 3)])
    down = lax.ppermute(sent_down, "line", [(3, 2), (2, 1), (1, 0)])
    done = while_last(lambda value: tie(value, sent_up, sent_down), done_second)
    up, down, done_last = lax.optimization_barrier((up, down, done))
    return own + up.astype(WIDE) + down.astype(WIDE), done_first, done_second, done_last


def swap(value, bits):
    count = lax.axis_size("plane")
    return lax.ppermute(value, "plane", [(b, b ^ bits) for b in range(count)])


def plane_order():
    count = lax.axis_size("plane")
    if count == 4:
        own = lax.axis_index("plane")
        return [own, own ^ 1, own ^ 2, own ^ 3]
    return list(range(count))


def plane_gather(block):
    if lax.axis_size("plane") != 4:
        return lax.all_gather(block, "plane", axis=0, tiled=True)
    half = block.shape[0] // 2
    one, two = swap(block, 1), swap(block, 2)
    first, second = swap(two[:half], 1), swap(one[half:], 2)
    return jnp.concatenate([block, one, two, first, second], axis=0)


def plane_scatter_far(total):
    count = lax.axis_size("plane")
    rows = total.shape[0] // count
    half = rows // 2
    own, one, two, far = [total[i * rows : (i + 1) * rows] for i in range(count)]
    one, two = one.astype(WIDE), two.astype(WIDE)
    low_far = far.astype(LOW)
    for_two = swap(low_far[:half], 1).astype(WIDE)
    for_one = swap(low_far[half:], 2).astype(WIDE)
    send_one = jnp.concatenate([one[:half], one[half:] + for_one], axis=0).astype(LOW)
    send_two = jnp.concatenate([two[:half] + for_two, two[half:]], axis=0).astype(LOW)
    return own, send_one, send_two


def plane_scatter(total):
    if lax.axis_size("plane") != 4:
        summed = lax.psum_scatter(total, "plane", scatter_dimension=0, tiled=True)
        empty = jnp.zeros(summed.shape, LOW)
        return summed, empty, empty
    own, send_one, send_two = plane_scatter_far(total)
    return own, swap(send_one, 1), swap(send_two, 2)


def sibling(value):
    return lax.ppermute(value, "fsdp", [(0, 1), (1, 0)])


def shards(
    tokens,
    cotangent,
    pair_table,
    query_weight,
    key_weight,
    value_weight,
    output_weight,
    gate_weight,
    up_weight,
    down_weight,
    norm_scales,
):
    line_count = lax.axis_size("line")
    plane_count = lax.axis_size("plane")
    fsdp_count = lax.axis_size("fsdp")
    sharers = plane_count * fsdp_count
    line_place = lax.axis_index("line")
    plane_place = lax.axis_index("plane")
    core = lax.axis_index("fsdp")
    devices = line_count * plane_count
    model = tokens.shape[2]
    row_count = tokens.shape[1]
    half_rows = row_count // 2
    span = 2 * row_count
    group_size = HEADS // KV_HEADS
    query_local = query_weight.shape[1]
    key_local = key_weight.shape[1]
    ff_local = gate_weight.shape[1]
    query_width = query_local * sharers
    key_width = key_local * sharers
    chunks = range(2)

    attn_local = jnp.concatenate(
        [jnp.concatenate([query_weight, key_weight, value_weight], axis=1).T, output_weight], axis=0
    )
    attn_flat = lax.all_gather(attn_local, ("plane", "fsdp"), axis=0, tiled=False)
    core_ref = core.astype(jnp.int32)[None]
    place_ref = jnp.stack([plane_place, core]).astype(jnp.int32)
    paired_local = jnp.concatenate([gate_weight.T, up_weight.T], axis=0)
    paired_all = lax.all_gather(paired_local, ("fsdp", "plane"), axis=0, tiled=True)
    down_all = lax.all_gather(down_weight, ("fsdp", "plane"), axis=0, tiled=True)

    edge_one = query_local
    edge_two = edge_one + key_local
    edge_three = edge_two + key_local
    edge_four = edge_three + output_weight.shape[0]
    pair_ids = jnp.arange(devices, dtype=jnp.int32)
    order = line_order()

    def places(members, chunk):
        lines = order[2 * chunk : 2 * chunk + 2]
        index = (lines[None, :] * plane_count + members[:, None]).reshape(-1)
        pair = jnp.sum(
            jnp.where(index[:, None] == pair_ids[None, :], pair_table[None, :], 0), axis=1
        )
        offsets = jnp.arange(row_count, dtype=jnp.int32)
        return jnp.where(
            offsets[None, :] < half_rows,
            pair[:, None] * half_rows + offsets[None, :],
            (2 * devices - 1 - pair[:, None]) * half_rows + offsets[None, :] - half_rows,
        ).reshape(-1)

    members = jnp.stack([jnp.asarray(member, jnp.int32) for member in plane_order()])
    positions = [places(plane_place[None], c) for c in chunks]
    key_positions = jnp.concatenate([places(members, c) for c in chunks])
    tables = [rope_tables(positions[c]) for c in chunks]
    scales = norm_scales.astype(WIDE)

    tokens_own = tokens[0]
    tokens_line, normed_first, queries = [None] * 2, [None] * 2, [None] * 2

    def packed(held):
        return jnp.concatenate(
            [
                held[:, :edge_one].reshape(-1, model),
                held[:, edge_one:edge_two].reshape(-1, model),
                held[:, edge_two:edge_three].reshape(-1, model),
            ],
            axis=0,
        )

    def project(c, rows):
        tokens_line[c] = rows
        weights = attn_flat if plane_count == 4 else packed(attn_flat)
        normed_first[c], queries[c], both = project_call(
            rows, weights, scales[0:1], *tables[c], query_width, key_width
        )
        return plane_gather(both)

    pair_all = jnp.concatenate(line_gather(tokens_own, project)[:2], axis=0)
    attn_held = tie(attn_flat, queries[1])
    output_all = attn_held[:, edge_three:].reshape(-1, model)

    attn_full, attn_low, inverse_sums = [None] * 2, [None] * 2, [None] * 2

    def attend(c):
        attn_full[c], attn_low[c], inverse_sums[c] = attend_call(
            queries[c], pair_all, positions[c][:, None], key_positions[None, :], group_size
        )
        return contract(attn_low[c], output_all, 1, 0)

    def reorder(gate, _):
        return packed(gate(attn_flat))

    branch_out, _, projection, _ = line_scatter(
        attend(1), lambda: (attend(0), ()), while_second=reorder
    )

    inputs = tokens_own.astype(WIDE)
    inverse_two = inverse_root(branch_out)
    hidden = inputs + branch_out * inverse_two * scales[1]
    inverse_three = inverse_root(hidden)

    normed_second, mixed, mixed_away = [None] * 2, [None] * 2, [None] * 2
    bent, slope = [None] * 2, [None] * 2

    def widen(c, rows):
        normed_second[c] = rows
        mixed[c], mixed_away[c], bent[c], slope[c] = widen_call(rows, paired_all, core_ref, sharers)
        return mixed[c]

    line_gather((hidden * inverse_three * scales[2]).astype(LOW), widen)

    def keep_mixed(gate, _):
        return [sibling(gate(part)) for part in mixed_away]

    def keep_second(gate, _):
        return [sibling(gate(part)) for part in normed_second]

    ffn_out, _, mixed_theirs, second_theirs = line_scatter(
        contract(mixed[1], down_all, 0, 0),
        lambda: (contract(mixed[0], down_all, 0, 0), ()),
        while_second=keep_mixed,
        while_last=keep_second,
    )

    inverse_four = inverse_root(ffn_out)
    result = hidden + ffn_out * inverse_four * scales[3]
    upstream = cotangent[0].astype(WIDE)
    ffn_grad = norm_back(ffn_out, inverse_four, scales[3], upstream)

    ffn_grad_low, pair_grad, pair_away = [None] * 2, [None] * 2, [None] * 2

    def narrow_back(c, rows):
        ffn_grad_low[c] = rows
        pair_grad[c], pair_away[c] = narrow_back_call(
            rows, down_all, bent[c], slope[c], core_ref, sharers
        )
        return pair_grad[c]

    line_gather(ffn_grad.astype(LOW), narrow_back)

    def give_rows():
        theirs = [sibling(part) for part in pair_away], [sibling(part) for part in ffn_grad_low]
        return contract(pair_grad[0], paired_all, 0, 0), theirs

    def give_down(gate, theirs):
        return weight_grad_call(
            [gate(part) for part in mixed], mixed_theirs, ffn_grad_low + theirs[1], core_ref
        )

    second_grad, (pair_theirs, _), down_grad, _ = line_scatter(
        contract(pair_grad[1], paired_all, 0, 0), give_rows, while_second=give_down
    )
    down_share = lax.psum_scatter(down_grad, "plane", scatter_dimension=0, tiled=True)

    def give_paired(gate):
        return weight_grad_call(
            [gate(part) for part in pair_grad], pair_theirs, normed_second + second_theirs, core_ref
        )

    hidden_part = norm_back(hidden, inverse_three, scales[2], second_grad)
    hidden_grad = upstream + hidden_part
    branch_grad = norm_back(branch_out, inverse_two, scales[1], hidden_grad)

    branch_grad_low, query_raw_low, prior = [None] * 2, [None] * 2, [None] * 2

    def attend_back(c, rows):
        branch_grad_low[c] = rows
        grads = contract(rows, output_all, 1, 1).astype(LOW)
        query_raw_low[c], prior[c] = attend_back_call(
            queries[c],
            grads,
            attn_full[c],
            pair_all,
            inverse_sums[c],
            positions[c][None, :],
            key_positions[:, None],
            *tables[c],
            prior[0],
            group_size,
        )
        return query_raw_low[c], prior[c]

    def give_three(gate):
        sums = [
            jnp.sum(hidden_grad * gate(branch_out) * inverse_two, axis=0),
            jnp.sum(second_grad * gate(hidden) * inverse_three, axis=0),
            jnp.sum(upstream * gate(ffn_out) * inverse_four, axis=0),
        ]
        return jnp.stack(sums, axis=0), down_share.astype(WIDE)

    _, _, paired_grad, (scale_three, down_share) = line_gather(
        branch_grad.astype(LOW), attend_back, while_first=give_paired, while_last=give_three
    )
    paired_share = lax.psum_scatter(paired_grad, "plane", scatter_dimension=0, tiled=True)

    per_chunk = plane_count * span
    both_grads = jnp.concatenate(
        [prior[1][c * per_chunk : (c + 1) * per_chunk].reshape(plane_count, span, -1) for c in chunks],
        axis=1,
    ).reshape(2 * per_chunk, -1)
    own_terms = plane_scatter(both_grads)

    def shard_parts(left, right, parts):
        if plane_count == 4:
            return shard_grad_call(left, right, parts, place_ref, plane_count)
        grad = contract(
            jnp.concatenate(left, axis=0), jnp.concatenate(right, axis=0), 0, 0
        ).astype(LOW)
        blocks = [
            grad[first : first + rows * sharers].reshape(sharers, rows, model)
            for first, rows in parts
        ]
        blocks = jnp.concatenate(blocks, axis=1).reshape(plane_count, fsdp_count, -1, model)
        near = lax.dynamic_index_in_dim(blocks, core, 1, keepdims=False)
        return near, lax.dynamic_index_in_dim(blocks, 1 - core, 1, keepdims=False)

    output_near, output_away = shard_parts(
        [tie(part, prior[1]) for part in attn_low], branch_grad_low, [(0, edge_four - edge_three)]
    )
    own_terms = tie(own_terms, output_near)

    raw_low, first_part = [None] * 2, [None] * 2

    def project_back(c):
        terms = [term[c * span : (c + 1) * span] for term in own_terms]
        raw_low[c], first_part[c] = project_back_call(
            query_raw_low[c], *terms, projection, *tables[c]
        )
        return first_part[c]

    all_count = devices * fsdp_count

    def give_projection():
        early = project_back(0)
        parts = shard_parts(
            [tie(part, early) for part in raw_low],
            normed_first,
            [
                (0, query_local),
                (query_width, key_local),
                (query_width + key_width, key_local),
            ],
        )
        return early, parts

    def give_total(gate, parts):
        near, away = parts
        total = jnp.concatenate(
            [
                near.astype(WIDE) + sibling(gate(away)).astype(WIDE),
                output_near.astype(WIDE) + sibling(gate(output_away)).astype(WIDE),
            ],
            axis=1,
        ).reshape(-1, model)
        scale_one = 0.0
        for c in chunks:
            wide_line = gate(tokens_line[c]).astype(WIDE)
            scale_one += jnp.sum(first_part[c] * (wide_line * inverse_root(wide_line)), axis=0)
        return total, scale_one

    def give_far(gate, held):
        total, scale_one = held
        scale_grads = jnp.concatenate([scale_one[None], scale_three], axis=0)
        scale_cut = (
            scale_grads.reshape(4, all_count, -1).transpose(1, 0, 2).reshape(all_count, -1)
        )
        if plane_count == 4:
            return scale_cut, plane_scatter_far(total)
        return scale_cut, total

    first_grad, _, _, (scale_cut, attn_sends) = line_scatter(
        project_back(1), give_projection, while_second=give_total, while_last=give_far
    )
    if plane_count == 4:
        own, send_one, send_two = attn_sends
        one, two = swap(send_one, 1), swap(send_two, 2)
    else:
        own, one, two = plane_scatter(attn_sends)

    input_part = norm_back(inputs, inverse_root(inputs), scales[0], first_grad)
    input_grad = hidden_grad + input_part

    scale_cut = lax.all_to_all(scale_cut, EVERY, 0, 0, tiled=True)
    scale_share = jnp.sum(scale_cut, axis=0).reshape(4, -1)
    gate_share = paired_share[:ff_local].T.astype(WIDE)
    up_share = paired_share[ff_local:].T.astype(WIDE)
    one, two = tie((one, two), input_grad, gate_share, up_share, scale_share)
    attn_share = own + one.astype(WIDE) + two.astype(WIDE)

    return (
        result.astype(LOW)[None],
        input_grad.astype(LOW)[None],
        attn_share[:edge_one].T,
        attn_share[edge_one:edge_two].T,
        attn_share[edge_two:edge_three].T,
        attn_share[edge_three:],
        gate_share,
        up_share,
        down_share,
        scale_share,
    )


def solution(mesh):
    devices, fsdp_count = mesh.devices.shape
    inner = Mesh(
        mesh.devices.reshape(KV_HEADS, devices // KV_HEADS, fsdp_count), EVERY
    )
    rows = P("fsdp", ("line", "plane"), None)
    return jax.shard_map(
        shards,
        mesh=inner,
        in_specs=(
            rows,
            rows,
            P(),
            P(None, EVERY),
            P(None, EVERY),
            P(None, EVERY),
            P(EVERY, None),
            P(None, EVERY),
            P(None, EVERY),
            P(EVERY, None),
            P(),
        ),
        out_specs=(
            rows,
            rows,
            P(None, EVERY),
            P(None, EVERY),
            P(None, EVERY),
            P(EVERY, None),
            P(None, EVERY),
            P(None, EVERY),
            P(EVERY, None),
            P(None, EVERY),
        ),
        check_vma=False,
    )
```

```python
import functools

import jax
import jax.numpy as jnp
from jax import lax
from jax.experimental import pallas as pl
from jax.experimental.pallas import tpu as pltpu
from jax.sharding import Mesh, PartitionSpec as P

HEADS = 8
KV_HEADS = 4
HEAD = 256

EPSILON = 1e-06
SOFT_CAP = 50.0
QUERY_SCALE = 0.0625

LOW = jnp.bfloat16
WIDE = jnp.float32

EVERY = ("line", "plane", "fsdp")


def contract(left, right, left_dim, right_dim):
    return lax.dot_general(
        left, right, (((left_dim,), (right_dim,)), ((), ())), preferred_element_type=WIDE
    )


def inverse_root(matrix_in):
    return lax.rsqrt(jnp.mean(matrix_in * matrix_in, axis=-1, keepdims=True) + EPSILON)


def norm_back(matrix_in, inverse, scale_row, upstream):
    weighted = upstream * scale_row
    inner = jnp.mean(matrix_in * weighted, axis=-1, keepdims=True)
    return inverse * weighted - matrix_in * (inverse * inverse * inverse) * inner


def rope_tables(positions):
    half_size = HEAD // 2
    frequency = 10000.0 ** (-jnp.arange(half_size, dtype=WIDE) * 2.0 / HEAD)
    angles = positions.astype(WIDE)[:, None] * frequency[None, :]
    return (jnp.cos(angles), jnp.sin(angles))


VMEM_LIMIT = 56 * 1024 * 1024
COST = pl.CostEstimate(flops=0, bytes_accessed=64 * 1024 * 1024, transcendentals=0)


def params():
    return pltpu.CompilerParams(vmem_limit_bytes=VMEM_LIMIT)


def project_kernel(
    rows_ref, weight_ref, scale_ref, cos_ref, sin_ref, normed_ref, query_ref, pair_ref, *scratch
):
    key_width = pair_ref.shape[1] // 2
    query_width = query_ref.shape[0] // rows_ref.shape[0] * HEAD
    span = rows_ref.shape[0]
    packed = weight_ref
    if scratch:
        packed = scratch[0]
        sharers = weight_ref.shape[0]
        query_local, key_local = query_width // sharers, key_width // sharers
        for j in range(sharers):
            packed[j * query_local : (j + 1) * query_local] = weight_ref[j, :query_local]
            at = query_width + j * key_local
            from_row = query_local
            for _ in range(2):
                packed[at : at + key_local] = weight_ref[j, from_row : from_row + key_local]
                at += key_width
                from_row += key_local
    rows = rows_ref[...].astype(WIDE)
    inverse = lax.rsqrt(jnp.mean(rows * rows, axis=-1, keepdims=True) + EPSILON)
    normed = (rows * inverse * scale_ref[...]).astype(LOW)
    normed_ref[...] = normed
    cosine, sine_table = cos_ref[...], sin_ref[...]
    half = HEAD // 2

    def turn(raw):
        first, second = raw[:, :half], raw[:, half:]
        return first * cosine - second * sine_table, second * cosine + first * sine_table

    for head in range(query_width // HEAD):
        raw = contract(normed, packed[head * HEAD : (head + 1) * HEAD], 1, 1)
        first, second = turn(raw)
        query_ref[head * span : (head + 1) * span, :half] = (first * QUERY_SCALE).astype(LOW)
        query_ref[head * span : (head + 1) * span, half:] = (second * QUERY_SCALE).astype(LOW)
    raw = contract(normed, packed[query_width:], 1, 1)
    first, second = turn(raw[:, :key_width])
    pair_ref[:, :half] = first.astype(LOW)
    pair_ref[:, half:key_width] = second.astype(LOW)
    pair_ref[:, key_width:] = raw[:, key_width:].astype(LOW)


def project_call(rows, weights, scale_row, cosine, sine_table, query_width, key_width):
    span, model = rows.shape
    heads = query_width // HEAD
    return pl.pallas_call(
        project_kernel,
        out_shape=(
            jax.ShapeDtypeStruct((span, model), LOW),
            jax.ShapeDtypeStruct((heads * span, HEAD), LOW),
            jax.ShapeDtypeStruct((span, 2 * key_width), LOW),
        ),
        scratch_shapes=[pltpu.VMEM((query_width + 2 * key_width, model), LOW)]
        if weights.ndim == 3
        else [],
        compiler_params=params(),
        cost_estimate=COST,
    )(rows, weights, scale_row, cosine, sine_table)


KEY_BLOCK = 2048


def as_row(column):
    return jnp.broadcast_to(column, (column.shape[0], 128)).T[:1]


def attend_kernel(query_ref, pair_ref, place_ref, key_place_ref, out_ref, low_ref, inverse_ref):
    keys = pair_ref[:, :HEAD]
    values = pair_ref[:, HEAD:]
    bounded = jnp.tanh(contract(query_ref[...], keys, 1, 1) * (1.0 / SOFT_CAP))
    allowed = key_place_ref[...] <= place_ref[...]
    grown = jnp.where(allowed, jnp.exp(SOFT_CAP * bounded), 0.0)
    inverse = 1.0 / jnp.sum(grown, axis=-1, keepdims=True)
    weights = (grown * inverse).astype(LOW)
    out = contract(weights, values, 1, 0)
    out_ref[...] = out
    low_ref[...] = out.astype(LOW)
    inverse_ref[...] = as_row(inverse)


def attend_call(queries, pair, places_column, key_places_row, group_size):
    count = queries.shape[0]
    span = count // group_size
    keys = pair.shape[0]
    by_head = pl.BlockSpec((span, HEAD), lambda h: (0, h))
    return pl.pallas_call(
        attend_kernel,
        grid=(group_size,),
        in_specs=[
            pl.BlockSpec((span, HEAD), lambda h: (h, 0)),
            pl.BlockSpec((keys, 2 * HEAD), lambda h: (0, 0)),
            pl.BlockSpec((span, 1), lambda h: (0, 0)),
            pl.BlockSpec((1, keys), lambda h: (0, 0)),
        ],
        out_specs=[by_head, by_head, pl.BlockSpec((1, span), lambda h: (0, h))],
        out_shape=(
            jax.ShapeDtypeStruct((span, group_size * HEAD), WIDE),
            jax.ShapeDtypeStruct((span, group_size * HEAD), LOW),
            jax.ShapeDtypeStruct((1, count), WIDE),
        ),
        compiler_params=params(),
        cost_estimate=COST,
    )(queries, pair, places_column, key_places_row)


def attend_back_kernel(*refs):
    query_ref, grad_ref, out_ref, pair_ref, inverse_ref, place_ref, key_place_ref = refs[:7]
    cos_ref, sin_ref, *prior_refs, query_grad_ref, pair_grad_ref, total_ref, held_ref = refs[7:]
    part, head = pl.program_id(0), pl.program_id(1)
    keys = pair_ref[:, :HEAD]
    values = pair_ref[:, HEAD:]
    queries = query_ref[...]
    grads = grad_ref[...]
    inner = as_row(jnp.sum(grads.astype(WIDE) * out_ref[...], axis=-1, keepdims=True))
    bounded = jnp.tanh(contract(keys, queries, 1, 1) * (1.0 / SOFT_CAP))
    allowed = key_place_ref[...] <= place_ref[...]
    weights = jnp.where(allowed, jnp.exp(SOFT_CAP * bounded) * inverse_ref[...], 0.0)
    weight_grad = contract(values, grads, 1, 1)
    score_grad = (weights * (weight_grad - inner) * (1.0 - bounded * bounded)).astype(LOW)
    query_part = contract(score_grad, keys, 0, 0)

    @pl.when(part == 0)
    def _():
        held_ref[head] = query_part

    @pl.when(part > 0)
    def _():
        held_ref[head] += query_part

    query_grad = held_ref[head]
    half = HEAD // 2
    first, second = query_grad[:, :half], query_grad[:, half:]
    cosine, sine_table = cos_ref[...], sin_ref[...]
    query_grad_ref[:, :half] = ((first * cosine + second * sine_table) * QUERY_SCALE).astype(LOW)
    query_grad_ref[:, half:] = ((second * cosine - first * sine_table) * QUERY_SCALE).astype(LOW)
    key_grad = contract(score_grad, queries, 1, 0)
    value_grad = contract(weights.astype(LOW), grads, 1, 0)

    @pl.when(head == 0)
    def _():
        if prior_refs:
            total_ref[:, :HEAD] = prior_refs[0][:, :HEAD] + key_grad
            total_ref[:, HEAD:] = prior_refs[0][:, HEAD:] + value_grad
        else:
            total_ref[:, :HEAD] = key_grad
            total_ref[:, HEAD:] = value_grad

    @pl.when(head > 0)
    def _():
        total_ref[:, :HEAD] += key_grad
        total_ref[:, HEAD:] += value_grad

    @pl.when(head == pl.num_programs(1) - 1)
    def _():
        pair_grad_ref[...] = total_ref[...].astype(pair_grad_ref.dtype)


def attend_back_call(
    queries, grads, out, pair, inverse, places_row, key_places_column, cosine, sine_table, prior, group_size
):
    count = queries.shape[0]
    span = count // group_size
    keys = pair.shape[0]
    block = min(keys, KEY_BLOCK)
    by_head = pl.BlockSpec((span, HEAD), lambda k, h: (0, h))
    by_keys = pl.BlockSpec((block, 2 * HEAD), lambda k, h: (k, 0))
    table = pl.BlockSpec((span, HEAD // 2), lambda k, h: (0, 0))
    extra = [] if prior is None else [prior]
    return pl.pallas_call(
        attend_back_kernel,
        grid=(keys // block, group_size),
        in_specs=[
            pl.BlockSpec((span, HEAD), lambda k, h: (h, 0)),
            by_head,
            by_head,
            by_keys,
            pl.BlockSpec((1, span), lambda k, h: (0, h)),
            pl.BlockSpec((1, span), lambda k, h: (0, 0)),
            pl.BlockSpec((block, 1), lambda k, h: (k, 0)),
            table,
            table,
        ]
        + [by_keys] * len(extra),
        out_specs=[by_head, by_keys],
        out_shape=(
            jax.ShapeDtypeStruct((span, group_size * HEAD), LOW),
            jax.ShapeDtypeStruct((keys, 2 * HEAD), WIDE if prior is None else LOW),
        ),
        scratch_shapes=[
            pltpu.VMEM((block, 2 * HEAD), WIDE),
            pltpu.VMEM((group_size, span, HEAD), WIDE),
        ],
        compiler_params=params(),
        cost_estimate=COST,
    )(queries, grads, out, pair, inverse, places_row, key_places_column, cosine, sine_table, *extra)


def project_back_kernel(
    query_ref, own_ref, one_ref, two_ref, weight_ref, cos_ref, sin_ref, raw_ref, part_ref
):
    query_width = query_ref.shape[1]
    total = own_ref[...].astype(WIDE) + one_ref[...].astype(WIDE) + two_ref[...].astype(WIDE)
    half = HEAD // 2
    first, second = total[:, :half], total[:, half:HEAD]
    cosine, sine_table = cos_ref[...], sin_ref[...]
    raw_ref[:, :query_width] = query_ref[...]
    raw_ref[:, query_width : query_width + half] = (first * cosine + second * sine_table).astype(LOW)
    raw_ref[:, query_width + half : query_width + HEAD] = (
        second * cosine - first * sine_table
    ).astype(LOW)
    raw_ref[:, query_width + HEAD :] = total[:, HEAD:].astype(LOW)
    part_ref[...] = contract(raw_ref[...], weight_ref[...], 1, 0)


def project_back_call(query_grad, own, one, two, weights, cosine, sine_table):
    span = query_grad.shape[0]
    width, model = weights.shape
    return pl.pallas_call(
        project_back_kernel,
        out_shape=(
            jax.ShapeDtypeStruct((span, width), LOW),
            jax.ShapeDtypeStruct((span, model), WIDE),
        ),
        compiler_params=params(),
        cost_estimate=COST,
    )(query_grad, own, one, two, weights, cosine, sine_table)


GELU_ROOT = 0.7978845608028654
GELU_CUBE = 0.044715


STEPS = 4


def blocks_of(value, count, first):
    rows = value.shape[0] // (2 * count)
    return jnp.concatenate(
        [value[(2 * p + first) * rows : (2 * p + first + 1) * rows] for p in range(count)], axis=0
    )


def widen_kernel(
    parts, core_ref, rows_ref, weight_ref, mixed_ref, away_ref, bent_ref, slope_ref
):
    step = pl.program_id(0)
    both = contract(weight_ref[...], rows_ref[...], 1, 1)
    gate, up = blocks_of(both, parts, 0), blocks_of(both, parts, 1)
    square = gate * gate
    curve = jnp.tanh(GELU_ROOT * gate * (1.0 + GELU_CUBE * square))
    rise = 0.5 * (1.0 + curve)
    bent = gate * rise
    mixed = (bent * up).astype(LOW)
    mixed_ref[...] = mixed
    bent_ref[...] = bent
    steep = GELU_ROOT * (1.0 + 3.0 * GELU_CUBE * square)
    slope_ref[...] = up * (rise + 0.5 * gate * (1.0 - curve * curve) * steep)

    @pl.when(step // (STEPS // 2) != core_ref[0])
    def _():
        away_ref[...] = mixed


def away_block(step, core_ref):
    first = (1 - core_ref[0]) * (STEPS // 2)
    return (jnp.clip(step - first, 0, STEPS // 2 - 1), 0)


def widen_call(rows, weights, core, sharers):
    span, model = rows.shape
    amount = weights.shape[0] // 2
    block = amount // STEPS
    by_step = pl.BlockSpec((block, span), lambda j, core_ref: (j, 0))
    return pl.pallas_call(
        functools.partial(widen_kernel, sharers // STEPS),
        grid_spec=pltpu.PrefetchScalarGridSpec(
            num_scalar_prefetch=1,
            grid=(STEPS,),
            in_specs=[
                pl.BlockSpec((span, model), lambda j, core_ref: (0, 0)),
                pl.BlockSpec((2 * block, model), lambda j, core_ref: (j, 0)),
            ],
            out_specs=[by_step, pl.BlockSpec((block, span), away_block), by_step, by_step],
        ),
        out_shape=(
            jax.ShapeDtypeStruct((amount, span), LOW),
            jax.ShapeDtypeStruct((amount // 2, span), LOW),
            jax.ShapeDtypeStruct((amount, span), WIDE),
            jax.ShapeDtypeStruct((amount, span), WIDE),
        ),
        compiler_params=params(),
        cost_estimate=COST,
    )(core, rows, weights)


def narrow_back_kernel(
    parts, core_ref, rows_ref, weight_ref, bent_ref, slope_ref, grad_ref, away_ref
):
    step = pl.program_id(0)
    mixed_grad = contract(weight_ref[...], rows_ref[...], 1, 1)
    gate, up = mixed_grad * slope_ref[...], mixed_grad * bent_ref[...]
    rows = gate.shape[0] // parts
    grad = jnp.concatenate(
        [part[p * rows : (p + 1) * rows] for p in range(parts) for part in (gate, up)], axis=0
    ).astype(LOW)
    grad_ref[...] = grad

    @pl.when(step // (STEPS // 2) != core_ref[0])
    def _():
        away_ref[...] = grad


def narrow_back_call(rows, weights, bent, slope, core, sharers):
    span, model = rows.shape
    amount = weights.shape[0]
    block = amount // STEPS
    by_step = pl.BlockSpec((block, span), lambda j, core_ref: (j, 0))
    return pl.pallas_call(
        functools.partial(narrow_back_kernel, sharers // STEPS),
        grid_spec=pltpu.PrefetchScalarGridSpec(
            num_scalar_prefetch=1,
            grid=(STEPS,),
            in_specs=[
                pl.BlockSpec((span, model), lambda j, core_ref: (0, 0)),
                pl.BlockSpec((block, model), lambda j, core_ref: (j, 0)),
                by_step,
                by_step,
            ],
            out_specs=[
                pl.BlockSpec((2 * block, span), lambda j, core_ref: (j, 0)),
                pl.BlockSpec((2 * block, span), away_block),
            ],
        ),
        out_shape=(
            jax.ShapeDtypeStruct((2 * amount, span), LOW),
            jax.ShapeDtypeStruct((amount, span), LOW),
        ),
        compiler_params=params(),
        cost_estimate=COST,
    )(core, rows, weights, bent, slope)


def weight_grad_kernel(core_ref, *refs):
    *pairs, out_ref = refs
    half = len(pairs) // 2
    total = contract(pairs[0][...], pairs[half][...], 1, 0)
    for left, right in zip(pairs[1:half], pairs[half + 1 :]):
        total += contract(left[...], right[...], 1, 0)
    out_ref[...] = total.astype(LOW)


def weight_grad_call(own, away, rows, core):
    span, model = rows[0].shape
    amount = own[0].shape[0] // 2
    block = amount // STEPS
    mine = pl.BlockSpec((block, span), lambda j, core_ref: (core_ref[0] * STEPS + j, 0))
    theirs = pl.BlockSpec((block, span), lambda j, core_ref: (j, 0))
    whole = pl.BlockSpec((span, model), lambda j, core_ref: (0, 0))
    return pl.pallas_call(
        weight_grad_kernel,
        grid_spec=pltpu.PrefetchScalarGridSpec(
            num_scalar_prefetch=1,
            grid=(STEPS,),
            in_specs=[mine] * len(own) + [theirs] * len(away) + [whole] * len(rows),
            out_specs=pl.BlockSpec((block, model), lambda j, core_ref: (j, 0)),
        ),
        out_shape=jax.ShapeDtypeStruct((amount, model), LOW),
        compiler_params=params(),
        cost_estimate=COST,
    )(core, *own, *away, *rows)


def shard_grad_kernel(parts, place_ref, *refs):
    *pairs, near_ref, away_ref, total_ref = refs
    half = len(pairs) // 2
    total = contract(pairs[0][...], pairs[half][...], 0, 0)
    for left, right in zip(pairs[1:half], pairs[half + 1 :]):
        total += contract(left[...], right[...], 0, 0)
    total_ref[...] = total.astype(LOW)
    own, core = place_ref[0], place_ref[1]
    planes = near_ref.shape[0]
    for plane in range(planes):
        for side in range(2):
            to_row = 0
            for first, rows in parts:
                block = total_ref[pl.ds(first + (2 * plane + side) * rows, rows)]

                @pl.when(core == side)
                def _():
                    near_ref[plane ^ own, pl.ds(to_row, rows)] = block

                @pl.when(core != side)
                def _():
                    away_ref[plane ^ own, pl.ds(to_row, rows)] = block

                to_row += rows


def shard_grad_call(left, right, parts, place, planes):
    width, model = left[0].shape[1], right[0].shape[1]
    rows = sum(part[1] for part in parts)
    shape = jax.ShapeDtypeStruct((planes, rows, model), LOW)
    return pl.pallas_call(
        functools.partial(shard_grad_kernel, parts),
        in_specs=[pl.BlockSpec(memory_space=pltpu.SMEM)]
        + [pl.BlockSpec(memory_space=pltpu.VMEM)] * (len(left) + len(right)),
        out_specs=[pl.BlockSpec(memory_space=pltpu.VMEM)] * 2,
        out_shape=(shape, shape),
        scratch_shapes=[pltpu.VMEM((width, model), LOW)],
        compiler_params=params(),
        cost_estimate=COST,
    )(place, *left, *right)


def tie(value, *others):
    return lax.optimization_barrier((value, others))[0]


def choose(flag, one, two):
    return jnp.where(flag, one, two)


def nothing(*others):
    return ()


def shift(value, step):
    count = lax.axis_size("line")
    return lax.ppermute(value, "line", [(at, (at + step) % count) for at in range(count)])


def line_gather(block, work, while_first=nothing):
    half = block.shape[0] // 2
    up, down = shift(block, 1), shift(block, -1)
    done = while_first(lambda value: tie(value, block))
    up, down, done_first = lax.optimization_barrier((up, down, done))
    far_low, far_high = shift(down[:half], -1), shift(up[half:], 1)
    first = work(0, jnp.concatenate([block, up], axis=0))
    far_low, far_high = tie((far_low, far_high), first)
    second = work(1, jnp.concatenate([down, far_low, far_high], axis=0))
    return first, second, done_first


def line_order():
    turns = jnp.array([0, 3, 1, 2], jnp.int32)
    return lax.rem(lax.axis_index("line").astype(jnp.int32) + turns, 4)


def line_scatter(late, work, while_last=nothing):
    rows = late.shape[0] // 2
    half = rows // 2
    following, far = late[:rows], late[rows:]
    low_far = far.astype(LOW)
    for_following, for_former = shift(low_far[:half], 1), shift(low_far[half:], -1)
    for_following, for_former, (early, done_first) = lax.optimization_barrier(
        (for_following, for_former, work())
    )
    own, former = early[:rows], early[rows:]
    sends = lax.optimization_barrier(
        (
            jnp.concatenate(
                [following[:half] + for_following.astype(WIDE), following[half:]], axis=0
            ).astype(LOW),
            jnp.concatenate(
                [former[:half], former[half:] + for_former.astype(WIDE)], axis=0
            ).astype(LOW),
        )
    )
    terms = shift(sends[0], 1), shift(sends[1], -1)
    done = while_last(lambda value: tie(value, *sends), done_first)
    terms, done_last = lax.optimization_barrier((terms, done))
    return own + sum(term.astype(WIDE) for term in terms), done_first, done_last


def swap(value, bits):
    count = lax.axis_size("plane")
    return lax.ppermute(value, "plane", [(b, b ^ bits) for b in range(count)])


def plane_order():
    count = lax.axis_size("plane")
    if count == 4:
        own = lax.axis_index("plane")
        return [own, own ^ 1, own ^ 2, own ^ 3]
    return list(range(count))


def plane_gather(block):
    if lax.axis_size("plane") != 4:
        return lax.all_gather(block, "plane", axis=0, tiled=True)
    half = block.shape[0] // 2
    one, two = swap(block, 1), swap(block, 2)
    first, second = swap(two[:half], 1), swap(one[half:], 2)
    return jnp.concatenate([block, one, two, first, second], axis=0)


def plane_scatter_far(total):
    count = lax.axis_size("plane")
    rows = total.shape[0] // count
    half = rows // 2
    own, one, two, far = [total[i * rows : (i + 1) * rows] for i in range(count)]
    one, two = one.astype(WIDE), two.astype(WIDE)
    low_far = far.astype(LOW)
    for_two = swap(low_far[:half], 1).astype(WIDE)
    for_one = swap(low_far[half:], 2).astype(WIDE)
    send_one = jnp.concatenate([one[:half], one[half:] + for_one], axis=0).astype(LOW)
    send_two = jnp.concatenate([two[:half] + for_two, two[half:]], axis=0).astype(LOW)
    return own, send_one, send_two


def plane_scatter(total):
    if lax.axis_size("plane") != 4:
        summed = lax.psum_scatter(total, "plane", scatter_dimension=0, tiled=True)
        empty = jnp.zeros(summed.shape, LOW)
        return summed, empty, empty
    own, send_one, send_two = plane_scatter_far(total)
    return own, swap(send_one, 1), swap(send_two, 2)


def sibling(value):
    return lax.ppermute(value, "fsdp", [(0, 1), (1, 0)])


def shards(
    tokens,
    cotangent,
    pair_table,
    query_weight,
    key_weight,
    value_weight,
    output_weight,
    gate_weight,
    up_weight,
    down_weight,
    norm_scales,
):
    line_count = lax.axis_size("line")
    plane_count = lax.axis_size("plane")
    fsdp_count = lax.axis_size("fsdp")
    sharers = plane_count * fsdp_count
    line_place = lax.axis_index("line")
    plane_place = lax.axis_index("plane")
    core = lax.axis_index("fsdp")
    devices = line_count * plane_count
    model = tokens.shape[2]
    row_count = tokens.shape[1]
    half_rows = row_count // 2
    span = 2 * row_count
    group_size = HEADS // KV_HEADS
    query_local = query_weight.shape[1]
    key_local = key_weight.shape[1]
    ff_local = gate_weight.shape[1]
    query_width = query_local * sharers
    key_width = key_local * sharers
    chunks = range(2)

    attn_local = jnp.concatenate(
        [jnp.concatenate([query_weight, key_weight, value_weight], axis=1).T, output_weight], axis=0
    )
    attn_flat = lax.all_gather(attn_local, ("plane", "fsdp"), axis=0, tiled=False)
    core_ref = core.astype(jnp.int32)[None]
    place_ref = jnp.stack([plane_place, core]).astype(jnp.int32)
    paired_local = jnp.concatenate([gate_weight.T, up_weight.T], axis=0)
    paired_all = lax.all_gather(paired_local, ("fsdp", "plane"), axis=0, tiled=True)
    down_all = lax.all_gather(down_weight, ("fsdp", "plane"), axis=0, tiled=True)

    edge_one = query_local
    edge_two = edge_one + key_local
    edge_three = edge_two + key_local
    edge_four = edge_three + output_weight.shape[0]
    pair_ids = jnp.arange(devices, dtype=jnp.int32)
    order = line_order()

    def places(members, chunk):
        lines = order[2 * chunk : 2 * chunk + 2]
        index = (lines[None, :] * plane_count + members[:, None]).reshape(-1)
        pair = jnp.sum(
            jnp.where(index[:, None] == pair_ids[None, :], pair_table[None, :], 0), axis=1
        )
        offsets = jnp.arange(row_count, dtype=jnp.int32)
        return jnp.where(
            offsets[None, :] < half_rows,
            pair[:, None] * half_rows + offsets[None, :],
            (2 * devices - 1 - pair[:, None]) * half_rows + offsets[None, :] - half_rows,
        ).reshape(-1)

    members = jnp.stack([jnp.asarray(member, jnp.int32) for member in plane_order()])
    positions = [places(plane_place[None], c) for c in chunks]
    key_positions = jnp.concatenate([places(members, c) for c in chunks])
    tables = [rope_tables(positions[c]) for c in chunks]
    key_column = key_positions[:, None]
    tables, key_column = lax.optimization_barrier((tables, key_column))
    scales = norm_scales.astype(WIDE)

    tokens_own = tokens[0]
    tokens_line, normed_first, queries = [None] * 2, [None] * 2, [None] * 2

    def packed(held):
        return jnp.concatenate(
            [
                held[:, :edge_one].reshape(-1, model),
                held[:, edge_one:edge_two].reshape(-1, model),
                held[:, edge_two:edge_three].reshape(-1, model),
            ],
            axis=0,
        )

    def project(c, rows):
        tokens_line[c] = rows
        weights = attn_flat if plane_count == 4 else packed(attn_flat)
        normed_first[c], queries[c], both = project_call(
            rows, weights, scales[0:1], *tables[c], query_width, key_width
        )
        return plane_gather(both)

    pair_all = jnp.concatenate(line_gather(tokens_own, project)[:2], axis=0)
    attn_held = tie(attn_flat, queries[1])
    output_all = attn_held[:, edge_three:].reshape(-1, model)

    attn_full, attn_low, inverse_sums = [None] * 2, [None] * 2, [None] * 2

    def attend(c):
        attn_full[c], attn_low[c], inverse_sums[c] = attend_call(
            queries[c], pair_all, positions[c][:, None], key_positions[None, :], group_size
        )
        return contract(attn_low[c], output_all, 1, 0)

    def reorder(gate, _):
        return packed(gate(attn_flat))

    branch_out, _, projection = line_scatter(
        attend(1), lambda: (attend(0), ()), while_last=reorder
    )

    inputs = tokens_own.astype(WIDE)
    inverse_two = inverse_root(branch_out)
    hidden = inputs + branch_out * inverse_two * scales[1]
    inverse_three = inverse_root(hidden)

    normed_second, mixed, mixed_away = [None] * 2, [None] * 2, [None] * 2
    bent, slope = [None] * 2, [None] * 2

    def widen(c, rows):
        normed_second[c] = rows
        mixed[c], mixed_away[c], bent[c], slope[c] = widen_call(rows, paired_all, core_ref, sharers)
        return mixed[c]

    line_gather((hidden * inverse_three * scales[2]).astype(LOW), widen)

    def keep(gate, _):
        return (
            [sibling(gate(part)) for part in mixed_away],
            [sibling(gate(part)) for part in normed_second],
        )

    ffn_out, _, (mixed_theirs, second_theirs) = line_scatter(
        contract(mixed[1], down_all, 0, 0),
        lambda: (contract(mixed[0], down_all, 0, 0), ()),
        while_last=keep,
    )

    inverse_four = inverse_root(ffn_out)
    result = hidden + ffn_out * inverse_four * scales[3]
    upstream = cotangent[0].astype(WIDE)
    ffn_grad = norm_back(ffn_out, inverse_four, scales[3], upstream)

    ffn_grad_low, pair_grad, pair_away = [None] * 2, [None] * 2, [None] * 2

    def narrow_back(c, rows):
        ffn_grad_low[c] = rows
        pair_grad[c], pair_away[c] = narrow_back_call(
            rows, down_all, bent[c], slope[c], core_ref, sharers
        )
        return pair_grad[c]

    line_gather(ffn_grad.astype(LOW), narrow_back)

    pair_theirs = [sibling(part) for part in pair_away]
    grad_theirs = [sibling(part) for part in ffn_grad_low]
    second_part = contract(jnp.concatenate(pair_grad, axis=1), paired_all, 0, 0)

    def give_down():
        return second_part[:span], weight_grad_call(
            [tie(part, second_part) for part in mixed],
            mixed_theirs,
            ffn_grad_low + grad_theirs,
            core_ref,
        )

    def give_paired(gate, _):
        return weight_grad_call(
            [gate(part) for part in pair_grad], pair_theirs, normed_second + second_theirs, core_ref
        )

    second_grad, down_grad, paired_grad = line_scatter(
        second_part[span:], give_down, while_last=give_paired
    )
    down_share = lax.psum_scatter(down_grad, "plane", scatter_dimension=0, tiled=True)
    paired_share = lax.psum_scatter(paired_grad, "plane", scatter_dimension=0, tiled=True)

    hidden_part = norm_back(hidden, inverse_three, scales[2], second_grad)
    hidden_grad = upstream + hidden_part
    branch_grad = norm_back(branch_out, inverse_two, scales[1], hidden_grad)

    branch_grad_low, query_raw_low, prior = [None] * 2, [None] * 2, [None] * 2

    def attend_back(c, rows):
        branch_grad_low[c] = rows
        grads = contract(rows, output_all, 1, 1).astype(LOW)
        query_raw_low[c], prior[c] = attend_back_call(
            queries[c],
            grads,
            attn_full[c],
            pair_all,
            inverse_sums[c],
            positions[c][None, :],
            key_column,
            *tables[c],
            prior[0],
            group_size,
        )
        return query_raw_low[c], prior[c]

    def give_three(gate):
        sums = [
            jnp.sum(hidden_grad * gate(branch_out) * inverse_two, axis=0),
            jnp.sum(second_grad * gate(hidden) * inverse_three, axis=0),
            jnp.sum(upstream * gate(ffn_out) * inverse_four, axis=0),
        ]
        return jnp.stack(sums, axis=0)

    _, _, scale_three = line_gather(branch_grad.astype(LOW), attend_back, while_first=give_three)

    per_chunk = plane_count * span
    both_grads = jnp.concatenate(
        [prior[1][c * per_chunk : (c + 1) * per_chunk].reshape(plane_count, span, -1) for c in chunks],
        axis=1,
    ).reshape(2 * per_chunk, -1)
    own_terms = plane_scatter(both_grads)

    def shard_parts(left, right, parts):
        if plane_count == 4:
            return shard_grad_call(left, right, parts, place_ref, plane_count)
        grad = contract(
            jnp.concatenate(left, axis=0), jnp.concatenate(right, axis=0), 0, 0
        ).astype(LOW)
        blocks = [
            grad[first : first + rows * sharers].reshape(sharers, rows, model)
            for first, rows in parts
        ]
        blocks = jnp.concatenate(blocks, axis=1).reshape(plane_count, fsdp_count, -1, model)
        near = lax.dynamic_index_in_dim(blocks, core, 1, keepdims=False)
        return near, lax.dynamic_index_in_dim(blocks, 1 - core, 1, keepdims=False)

    output_near, output_away = shard_parts(
        [tie(part, prior[1]) for part in attn_low], branch_grad_low, [(0, edge_four - edge_three)]
    )
    own_terms = tie(own_terms, output_near)

    raw_low, first_part = [None] * 2, [None] * 2

    def project_back(c):
        terms = [term[c * span : (c + 1) * span] for term in own_terms]
        raw_low[c], first_part[c] = project_back_call(
            query_raw_low[c], *terms, projection, *tables[c]
        )
        return first_part[c]

    all_count = devices * fsdp_count

    def give_projection():
        early = project_back(0)
        parts = shard_parts(
            [tie(part, early) for part in raw_low],
            normed_first,
            [
                (0, query_local),
                (query_width, key_local),
                (query_width + key_width, key_local),
            ],
        )
        return early, parts

    def give_far(gate, parts):
        near, away = parts
        total = jnp.concatenate(
            [
                near.astype(WIDE) + sibling(gate(away)).astype(WIDE),
                output_near.astype(WIDE) + sibling(gate(output_away)).astype(WIDE),
            ],
            axis=1,
        ).reshape(-1, model)
        scale_one = 0.0
        for c in chunks:
            wide_line = gate(tokens_line[c]).astype(WIDE)
            scale_one += jnp.sum(first_part[c] * (wide_line * inverse_root(wide_line)), axis=0)
        scale_grads = jnp.concatenate([scale_one[None], scale_three], axis=0)
        scale_cut = (
            scale_grads.reshape(4, all_count, -1).transpose(1, 0, 2).reshape(all_count, -1)
        )
        if plane_count == 4:
            return scale_cut, plane_scatter_far(total)
        return scale_cut, total

    first_grad, _, (scale_cut, attn_sends) = line_scatter(
        project_back(1), give_projection, while_last=give_far
    )
    if plane_count == 4:
        own, send_one, send_two = attn_sends
        one, two = swap(send_one, 1), swap(send_two, 2)
    else:
        own, one, two = plane_scatter(attn_sends)

    input_part = norm_back(inputs, inverse_root(inputs), scales[0], first_grad)
    input_grad = hidden_grad + input_part

    scale_cut = lax.all_to_all(scale_cut, EVERY, 0, 0, tiled=True)
    gate_share = paired_share[:ff_local].T.astype(WIDE)
    up_share = paired_share[ff_local:].T.astype(WIDE)
    down_share = down_share.astype(WIDE)
    scale_cut = tie(scale_cut, gate_share, up_share, down_share)
    scale_share = jnp.sum(scale_cut, axis=0).reshape(4, -1)
    one, two = tie((one, two), input_grad, gate_share, up_share, scale_share)
    attn_share = own + one.astype(WIDE) + two.astype(WIDE)

    return (
        result.astype(LOW)[None],
        input_grad.astype(LOW)[None],
        attn_share[:edge_one].T,
        attn_share[edge_one:edge_two].T,
        attn_share[edge_two:edge_three].T,
        attn_share[edge_three:],
        gate_share,
        up_share,
        down_share,
        scale_share,
    )


def solution(mesh):
    devices, fsdp_count = mesh.devices.shape
    inner = Mesh(
        mesh.devices.reshape(KV_HEADS, devices // KV_HEADS, fsdp_count), EVERY
    )
    rows = P("fsdp", ("line", "plane"), None)
    return jax.shard_map(
        shards,
        mesh=inner,
        in_specs=(
            rows,
            rows,
            P(),
            P(None, EVERY),
            P(None, EVERY),
            P(None, EVERY),
            P(EVERY, None),
            P(None, EVERY),
            P(None, EVERY),
            P(EVERY, None),
            P(),
        ),
        out_specs=(
            rows,
            rows,
            P(None, EVERY),
            P(None, EVERY),
            P(None, EVERY),
            P(EVERY, None),
            P(None, EVERY),
            P(None, EVERY),
            P(EVERY, None),
            P(None, EVERY),
        ),
        check_vma=False,
    )
```

```python
import functools

import jax
import jax.numpy as jnp
from jax import lax
from jax.experimental import pallas as pl
from jax.experimental.pallas import tpu as pltpu
from jax.sharding import Mesh, PartitionSpec as P

HEADS = 8
KV_HEADS = 4
HEAD = 256

EPSILON = 1e-06
SOFT_CAP = 50.0
QUERY_SCALE = 0.0625

LOW = jnp.bfloat16
WIDE = jnp.float32

EVERY = ("line", "plane", "fsdp")


def contract(left, right, left_dim, right_dim):
    return lax.dot_general(
        left, right, (((left_dim,), (right_dim,)), ((), ())), preferred_element_type=WIDE
    )


def inverse_root(matrix_in):
    return lax.rsqrt(jnp.mean(matrix_in * matrix_in, axis=-1, keepdims=True) + EPSILON)


def norm_back(matrix_in, inverse, scale_row, upstream):
    weighted = upstream * scale_row
    inner = jnp.mean(matrix_in * weighted, axis=-1, keepdims=True)
    return inverse * weighted - matrix_in * (inverse * inverse * inverse) * inner


def rope_tables(positions):
    half_size = HEAD // 2
    frequency = 10000.0 ** (-jnp.arange(half_size, dtype=WIDE) * 2.0 / HEAD)
    angles = positions.astype(WIDE)[:, None] * frequency[None, :]
    return (jnp.cos(angles), jnp.sin(angles))


VMEM_LIMIT = 56 * 1024 * 1024
COST = pl.CostEstimate(flops=0, bytes_accessed=64 * 1024 * 1024, transcendentals=0)


def params():
    return pltpu.CompilerParams(vmem_limit_bytes=VMEM_LIMIT)


def project_kernel(
    rows_ref, weight_ref, scale_ref, cos_ref, sin_ref, normed_ref, query_ref, pair_ref, *scratch
):
    key_width = pair_ref.shape[1] // 2
    query_width = query_ref.shape[0] // rows_ref.shape[0] * HEAD
    span = rows_ref.shape[0]
    packed = weight_ref
    if scratch:
        packed = scratch[0]
        sharers = weight_ref.shape[0]
        query_local, key_local = query_width // sharers, key_width // sharers
        for j in range(sharers):
            packed[j * query_local : (j + 1) * query_local] = weight_ref[j, :query_local]
            at = query_width + j * key_local
            from_row = query_local
            for _ in range(2):
                packed[at : at + key_local] = weight_ref[j, from_row : from_row + key_local]
                at += key_width
                from_row += key_local
    rows = rows_ref[...].astype(WIDE)
    inverse = lax.rsqrt(jnp.mean(rows * rows, axis=-1, keepdims=True) + EPSILON)
    normed = (rows * inverse * scale_ref[...]).astype(LOW)
    normed_ref[...] = normed
    cosine, sine_table = cos_ref[...], sin_ref[...]
    half = HEAD // 2

    def turn(raw):
        first, second = raw[:, :half], raw[:, half:]
        return first * cosine - second * sine_table, second * cosine + first * sine_table

    for head in range(query_width // HEAD):
        raw = contract(normed, packed[head * HEAD : (head + 1) * HEAD], 1, 1)
        first, second = turn(raw)
        query_ref[head * span : (head + 1) * span, :half] = (first * QUERY_SCALE).astype(LOW)
        query_ref[head * span : (head + 1) * span, half:] = (second * QUERY_SCALE).astype(LOW)
    raw = contract(normed, packed[query_width:], 1, 1)
    first, second = turn(raw[:, :key_width])
    pair_ref[:, :half] = first.astype(LOW)
    pair_ref[:, half:key_width] = second.astype(LOW)
    pair_ref[:, key_width:] = raw[:, key_width:].astype(LOW)


def project_call(rows, weights, scale_row, cosine, sine_table, query_width, key_width):
    span, model = rows.shape
    heads = query_width // HEAD
    return pl.pallas_call(
        project_kernel,
        out_shape=(
            jax.ShapeDtypeStruct((span, model), LOW),
            jax.ShapeDtypeStruct((heads * span, HEAD), LOW),
            jax.ShapeDtypeStruct((span, 2 * key_width), LOW),
        ),
        scratch_shapes=[pltpu.VMEM((query_width + 2 * key_width, model), LOW)]
        if weights.ndim == 3
        else [],
        compiler_params=params(),
        cost_estimate=COST,
    )(rows, weights, scale_row, cosine, sine_table)


KEY_BLOCK = 2048


def as_row(column):
    return jnp.broadcast_to(column, (column.shape[0], 128)).T[:1]


def attend_kernel(query_ref, pair_ref, place_ref, key_place_ref, out_ref, low_ref, inverse_ref):
    keys = pair_ref[:, :HEAD]
    values = pair_ref[:, HEAD:]
    bounded = jnp.tanh(contract(query_ref[...], keys, 1, 1) * (1.0 / SOFT_CAP))
    allowed = key_place_ref[...] <= place_ref[...]
    grown = jnp.where(allowed, jnp.exp(SOFT_CAP * bounded), 0.0)
    inverse = 1.0 / jnp.sum(grown, axis=-1, keepdims=True)
    weights = (grown * inverse).astype(LOW)
    out = contract(weights, values, 1, 0)
    out_ref[...] = out
    low_ref[...] = out.astype(LOW)
    inverse_ref[...] = as_row(inverse)


def attend_call(queries, pair, places_column, key_places_row, group_size):
    count = queries.shape[0]
    span = count // group_size
    keys = pair.shape[0]
    by_head = pl.BlockSpec((span, HEAD), lambda h: (0, h))
    return pl.pallas_call(
        attend_kernel,
        grid=(group_size,),
        in_specs=[
            pl.BlockSpec((span, HEAD), lambda h: (h, 0)),
            pl.BlockSpec((keys, 2 * HEAD), lambda h: (0, 0)),
            pl.BlockSpec((span, 1), lambda h: (0, 0)),
            pl.BlockSpec((1, keys), lambda h: (0, 0)),
        ],
        out_specs=[by_head, by_head, pl.BlockSpec((1, span), lambda h: (0, h))],
        out_shape=(
            jax.ShapeDtypeStruct((span, group_size * HEAD), WIDE),
            jax.ShapeDtypeStruct((span, group_size * HEAD), LOW),
            jax.ShapeDtypeStruct((1, count), WIDE),
        ),
        compiler_params=params(),
        cost_estimate=COST,
    )(queries, pair, places_column, key_places_row)


def attend_back_kernel(*refs):
    query_ref, grad_ref, out_ref, pair_ref, inverse_ref, place_ref, base_ref = refs[:7]
    cos_ref, sin_ref, *prior_refs, query_grad_ref, pair_grad_ref, total_ref, held_ref = refs[7:]
    part, head = pl.program_id(0), pl.program_id(1)
    keys = pair_ref[:, :HEAD]
    values = pair_ref[:, HEAD:]
    queries = query_ref[...]
    grads = grad_ref[...]
    inner = as_row(jnp.sum(grads.astype(WIDE) * out_ref[...], axis=-1, keepdims=True))
    bounded = jnp.tanh(contract(keys, queries, 1, 1) * (1.0 / SOFT_CAP))
    blocks = base_ref.shape[0] // pl.num_programs(0)
    rows = keys.shape[0] // blocks
    offsets = lax.broadcasted_iota(jnp.int32, (rows, 1), 0)
    key_places = jnp.concatenate(
        [base_ref[part * blocks + block] + offsets for block in range(blocks)], axis=0
    )
    allowed = key_places <= place_ref[...]
    weights = jnp.where(allowed, jnp.exp(SOFT_CAP * bounded) * inverse_ref[...], 0.0)
    weight_grad = contract(values, grads, 1, 1)
    score_grad = (weights * (weight_grad - inner) * (1.0 - bounded * bounded)).astype(LOW)
    query_part = contract(score_grad, keys, 0, 0)

    @pl.when(part == 0)
    def _():
        held_ref[head] = query_part

    @pl.when(part > 0)
    def _():
        held_ref[head] += query_part

    query_grad = held_ref[head]
    half = HEAD // 2
    first, second = query_grad[:, :half], query_grad[:, half:]
    cosine, sine_table = cos_ref[...], sin_ref[...]
    query_grad_ref[:, :half] = ((first * cosine + second * sine_table) * QUERY_SCALE).astype(LOW)
    query_grad_ref[:, half:] = ((second * cosine - first * sine_table) * QUERY_SCALE).astype(LOW)
    key_grad = contract(score_grad, queries, 1, 0)
    value_grad = contract(weights.astype(LOW), grads, 1, 0)

    @pl.when(head == 0)
    def _():
        if prior_refs:
            total_ref[:, :HEAD] = prior_refs[0][:, :HEAD] + key_grad
            total_ref[:, HEAD:] = prior_refs[0][:, HEAD:] + value_grad
        else:
            total_ref[:, :HEAD] = key_grad
            total_ref[:, HEAD:] = value_grad

    @pl.when(head > 0)
    def _():
        total_ref[:, :HEAD] += key_grad
        total_ref[:, HEAD:] += value_grad

    @pl.when(head == pl.num_programs(1) - 1)
    def _():
        pair_grad_ref[...] = total_ref[...].astype(pair_grad_ref.dtype)


def attend_back_call(
    queries, grads, out, pair, inverse, places_row, key_bases, cosine, sine_table, prior, group_size
):
    count = queries.shape[0]
    span = count // group_size
    keys = pair.shape[0]
    block = min(keys, KEY_BLOCK)
    by_head = pl.BlockSpec((span, HEAD), lambda k, h: (0, h))
    by_keys = pl.BlockSpec((block, 2 * HEAD), lambda k, h: (k, 0))
    table = pl.BlockSpec((span, HEAD // 2), lambda k, h: (0, 0))
    extra = [] if prior is None else [prior]
    return pl.pallas_call(
        attend_back_kernel,
        grid=(keys // block, group_size),
        in_specs=[
            pl.BlockSpec((span, HEAD), lambda k, h: (h, 0)),
            by_head,
            by_head,
            by_keys,
            pl.BlockSpec((1, span), lambda k, h: (0, h)),
            pl.BlockSpec((1, span), lambda k, h: (0, 0)),
            pl.BlockSpec(memory_space=pltpu.SMEM),
            table,
            table,
        ]
        + [by_keys] * len(extra),
        out_specs=[by_head, by_keys],
        out_shape=(
            jax.ShapeDtypeStruct((span, group_size * HEAD), LOW),
            jax.ShapeDtypeStruct((keys, 2 * HEAD), WIDE if prior is None else LOW),
        ),
        scratch_shapes=[
            pltpu.VMEM((block, 2 * HEAD), WIDE),
            pltpu.VMEM((group_size, span, HEAD), WIDE),
        ],
        compiler_params=params(),
        cost_estimate=COST,
    )(queries, grads, out, pair, inverse, places_row, key_bases, cosine, sine_table, *extra)


def project_back_kernel(
    query_ref, own_ref, one_ref, two_ref, weight_ref, cos_ref, sin_ref, raw_ref, part_ref, low_ref
):
    query_width = query_ref.shape[1]
    total = own_ref[...].astype(WIDE) + one_ref[...].astype(WIDE) + two_ref[...].astype(WIDE)
    half = HEAD // 2
    first, second = total[:, :half], total[:, half:HEAD]
    cosine, sine_table = cos_ref[...], sin_ref[...]
    raw_ref[:, :query_width] = query_ref[...]
    raw_ref[:, query_width : query_width + half] = (first * cosine + second * sine_table).astype(LOW)
    raw_ref[:, query_width + half : query_width + HEAD] = (
        second * cosine - first * sine_table
    ).astype(LOW)
    raw_ref[:, query_width + HEAD :] = total[:, HEAD:].astype(LOW)
    part = contract(raw_ref[...], weight_ref[...], 1, 0)
    part_ref[...] = part
    low_ref[...] = part[part.shape[0] // 2 :].astype(LOW)


def project_back_call(query_grad, own, one, two, weights, cosine, sine_table):
    span = query_grad.shape[0]
    width, model = weights.shape
    return pl.pallas_call(
        project_back_kernel,
        out_shape=(
            jax.ShapeDtypeStruct((span, width), LOW),
            jax.ShapeDtypeStruct((span, model), WIDE),
            jax.ShapeDtypeStruct((span // 2, model), LOW),
        ),
        compiler_params=params(),
        cost_estimate=COST,
    )(query_grad, own, one, two, weights, cosine, sine_table)


GELU_ROOT = 0.7978845608028654
GELU_CUBE = 0.044715


STEPS = 4


def blocks_of(value, count, first):
    rows = value.shape[0] // (2 * count)
    return jnp.concatenate(
        [value[(2 * p + first) * rows : (2 * p + first + 1) * rows] for p in range(count)], axis=0
    )


def widen_kernel(
    parts, core_ref, rows_ref, weight_ref, mixed_ref, away_ref, bent_ref, slope_ref
):
    step = pl.program_id(0)
    both = contract(weight_ref[...], rows_ref[...], 1, 1)
    gate, up = blocks_of(both, parts, 0), blocks_of(both, parts, 1)
    square = gate * gate
    curve = jnp.tanh(GELU_ROOT * gate * (1.0 + GELU_CUBE * square))
    rise = 0.5 * (1.0 + curve)
    bent = gate * rise
    mixed = (bent * up).astype(LOW)
    mixed_ref[...] = mixed
    bent_ref[...] = bent
    steep = GELU_ROOT * (1.0 + 3.0 * GELU_CUBE * square)
    slope_ref[...] = up * (rise + 0.5 * gate * (1.0 - curve * curve) * steep)

    @pl.when(step // (STEPS // 2) != core_ref[0])
    def _():
        away_ref[...] = mixed


def away_block(step, core_ref):
    first = (1 - core_ref[0]) * (STEPS // 2)
    return (jnp.clip(step - first, 0, STEPS // 2 - 1), 0)


def widen_call(rows, weights, core, sharers):
    span, model = rows.shape
    amount = weights.shape[0] // 2
    block = amount // STEPS
    by_step = pl.BlockSpec((block, span), lambda j, core_ref: (j, 0))
    return pl.pallas_call(
        functools.partial(widen_kernel, sharers // STEPS),
        grid_spec=pltpu.PrefetchScalarGridSpec(
            num_scalar_prefetch=1,
            grid=(STEPS,),
            in_specs=[
                pl.BlockSpec((span, model), lambda j, core_ref: (0, 0)),
                pl.BlockSpec((2 * block, model), lambda j, core_ref: (j, 0)),
            ],
            out_specs=[by_step, pl.BlockSpec((block, span), away_block), by_step, by_step],
        ),
        out_shape=(
            jax.ShapeDtypeStruct((amount, span), LOW),
            jax.ShapeDtypeStruct((amount // 2, span), LOW),
            jax.ShapeDtypeStruct((amount, span), WIDE),
            jax.ShapeDtypeStruct((amount, span), WIDE),
        ),
        compiler_params=params(),
        cost_estimate=COST,
    )(core, rows, weights)


def narrow_back_kernel(
    parts, core_ref, rows_ref, weight_ref, bent_ref, slope_ref, grad_ref, away_ref
):
    step = pl.program_id(0)
    mixed_grad = contract(weight_ref[...], rows_ref[...], 1, 1)
    gate, up = mixed_grad * slope_ref[...], mixed_grad * bent_ref[...]
    rows = gate.shape[0] // parts
    grad = jnp.concatenate(
        [part[p * rows : (p + 1) * rows] for p in range(parts) for part in (gate, up)], axis=0
    ).astype(LOW)
    grad_ref[...] = grad

    @pl.when(step // (STEPS // 2) != core_ref[0])
    def _():
        away_ref[...] = grad


def narrow_back_call(rows, weights, bent, slope, core, sharers):
    span, model = rows.shape
    amount = weights.shape[0]
    block = amount // STEPS
    by_step = pl.BlockSpec((block, span), lambda j, core_ref: (j, 0))
    return pl.pallas_call(
        functools.partial(narrow_back_kernel, sharers // STEPS),
        grid_spec=pltpu.PrefetchScalarGridSpec(
            num_scalar_prefetch=1,
            grid=(STEPS,),
            in_specs=[
                pl.BlockSpec((span, model), lambda j, core_ref: (0, 0)),
                pl.BlockSpec((block, model), lambda j, core_ref: (j, 0)),
                by_step,
                by_step,
            ],
            out_specs=[
                pl.BlockSpec((2 * block, span), lambda j, core_ref: (j, 0)),
                pl.BlockSpec((2 * block, span), away_block),
            ],
        ),
        out_shape=(
            jax.ShapeDtypeStruct((2 * amount, span), LOW),
            jax.ShapeDtypeStruct((amount, span), LOW),
        ),
        compiler_params=params(),
        cost_estimate=COST,
    )(core, rows, weights, bent, slope)


def weight_grad_kernel(core_ref, *refs):
    *pairs, out_ref, left_ref, right_ref = refs
    half = len(pairs) // 2

    @pl.when(pl.program_id(0) == 0)
    def _():
        first = 0
        for part in pairs[half:]:
            right_ref[first : first + part.shape[0]] = part[...]
            first += part.shape[0]

    first = 0
    for part in pairs[:half]:
        left_ref[:, first : first + part.shape[1]] = part[...]
        first += part.shape[1]
    out_ref[...] = contract(left_ref[...], right_ref[...], 1, 0).astype(LOW)


def weight_grad_call(own, away, rows, core):
    span, model = rows[0].shape
    amount = own[0].shape[0] // 2
    block = amount // STEPS
    mine = pl.BlockSpec((block, span), lambda j, core_ref: (core_ref[0] * STEPS + j, 0))
    theirs = pl.BlockSpec((block, span), lambda j, core_ref: (j, 0))
    whole = pl.BlockSpec((span, model), lambda j, core_ref: (0, 0))
    return pl.pallas_call(
        weight_grad_kernel,
        grid_spec=pltpu.PrefetchScalarGridSpec(
            num_scalar_prefetch=1,
            grid=(STEPS,),
            in_specs=[mine] * len(own) + [theirs] * len(away) + [whole] * len(rows),
            out_specs=pl.BlockSpec((block, model), lambda j, core_ref: (j, 0)),
            scratch_shapes=[
                pltpu.VMEM((block, len(rows) * span), LOW),
                pltpu.VMEM((len(rows) * span, model), LOW),
            ],
        ),
        out_shape=jax.ShapeDtypeStruct((amount, model), LOW),
        compiler_params=params(),
        cost_estimate=COST,
    )(core, *own, *away, *rows)


def shard_grad_kernel(parts, place_ref, *refs):
    *pairs, near_ref, away_ref, total_ref = refs
    half = len(pairs) // 2
    total = contract(pairs[0][...], pairs[half][...], 0, 0)
    for left, right in zip(pairs[1:half], pairs[half + 1 :]):
        total += contract(left[...], right[...], 0, 0)
    total_ref[...] = total.astype(LOW)
    own, core = place_ref[0], place_ref[1]
    planes = near_ref.shape[0]
    for plane in range(planes):
        for side in range(2):
            to_row = 0
            for first, rows in parts:
                block = total_ref[pl.ds(first + (2 * plane + side) * rows, rows)]

                @pl.when(core == side)
                def _():
                    near_ref[plane ^ own, pl.ds(to_row, rows)] = block

                @pl.when(core != side)
                def _():
                    away_ref[plane ^ own, pl.ds(to_row, rows)] = block

                to_row += rows


def shard_grad_call(left, right, parts, place, planes):
    width, model = left[0].shape[1], right[0].shape[1]
    rows = sum(part[1] for part in parts)
    shape = jax.ShapeDtypeStruct((planes, rows, model), LOW)
    return pl.pallas_call(
        functools.partial(shard_grad_kernel, parts),
        in_specs=[pl.BlockSpec(memory_space=pltpu.SMEM)]
        + [pl.BlockSpec(memory_space=pltpu.VMEM)] * (len(left) + len(right)),
        out_specs=[pl.BlockSpec(memory_space=pltpu.VMEM)] * 2,
        out_shape=(shape, shape),
        scratch_shapes=[pltpu.VMEM((width, model), LOW)],
        compiler_params=params(),
        cost_estimate=COST,
    )(place, *left, *right)


def tie(value, *others):
    return lax.optimization_barrier((value, others))[0]


def choose(flag, one, two):
    return jnp.where(flag, one, two)


def nothing(*others):
    return ()


def shift(value, step):
    count = lax.axis_size("line")
    return lax.ppermute(value, "line", [(at, (at + step) % count) for at in range(count)])


def line_gather(block, work, while_first=nothing):
    half = block.shape[0] // 2
    up, down = shift(block, 1), shift(block, -1)
    done = while_first(lambda value: tie(value, block))
    up, down, done_first = lax.optimization_barrier((up, down, done))
    far_low, far_high = shift(down[:half], -1), shift(up[half:], 1)
    first = work(0, jnp.concatenate([block, up], axis=0))
    far_low, far_high = tie((far_low, far_high), first)
    second = work(1, jnp.concatenate([down, far_low, far_high], axis=0))
    return first, second, done_first


def line_order():
    turns = jnp.array([0, 3, 1, 2], jnp.int32)
    return lax.rem(lax.axis_index("line").astype(jnp.int32) + turns, 4)


def line_scatter(late, work, while_last=nothing, low_far=None):
    rows = late.shape[0] // 2
    half = rows // 2
    following, far = late[:rows], late[rows:]
    low_far = far.astype(LOW) if low_far is None else low_far
    for_following, for_former = shift(low_far[:half], 1), shift(low_far[half:], -1)
    for_following, for_former, (early, done_first) = lax.optimization_barrier(
        (for_following, for_former, work())
    )
    own, former = early[:rows], early[rows:]
    sends = lax.optimization_barrier(
        (
            jnp.concatenate(
                [following[:half] + for_following.astype(WIDE), following[half:]], axis=0
            ).astype(LOW),
            jnp.concatenate(
                [former[:half], former[half:] + for_former.astype(WIDE)], axis=0
            ).astype(LOW),
        )
    )
    terms = shift(sends[0], 1), shift(sends[1], -1)
    done = while_last(lambda value: tie(value, *sends), done_first)
    terms, done_last = lax.optimization_barrier((terms, done))
    return own + sum(term.astype(WIDE) for term in terms), done_first, done_last


def swap(value, bits):
    count = lax.axis_size("plane")
    return lax.ppermute(value, "plane", [(b, b ^ bits) for b in range(count)])


def plane_order():
    count = lax.axis_size("plane")
    if count == 4:
        own = lax.axis_index("plane")
        return [own, own ^ 1, own ^ 2, own ^ 3]
    return list(range(count))


def plane_gather(block):
    if lax.axis_size("plane") != 4:
        return lax.all_gather(block, "plane", axis=0, tiled=True)
    half = block.shape[0] // 2
    one, two = swap(block, 1), swap(block, 2)
    first, second = swap(two[:half], 1), swap(one[half:], 2)
    return jnp.concatenate([block, one, two, first, second], axis=0)


def plane_scatter_far(total):
    count = lax.axis_size("plane")
    rows = total.shape[0] // count
    half = rows // 2
    own, one, two, far = [total[i * rows : (i + 1) * rows] for i in range(count)]
    one, two = one.astype(WIDE), two.astype(WIDE)
    low_far = far.astype(LOW)
    for_two = swap(low_far[:half], 1).astype(WIDE)
    for_one = swap(low_far[half:], 2).astype(WIDE)
    send_one = jnp.concatenate([one[:half], one[half:] + for_one], axis=0).astype(LOW)
    send_two = jnp.concatenate([two[:half] + for_two, two[half:]], axis=0).astype(LOW)
    return own, send_one, send_two


def plane_scatter(total):
    if lax.axis_size("plane") != 4:
        summed = lax.psum_scatter(total, "plane", scatter_dimension=0, tiled=True)
        empty = jnp.zeros(summed.shape, LOW)
        return summed, empty, empty
    own, send_one, send_two = plane_scatter_far(total)
    return own, swap(send_one, 1), swap(send_two, 2)


def sibling(value):
    return lax.ppermute(value, "fsdp", [(0, 1), (1, 0)])


def shards(
    tokens,
    cotangent,
    pair_table,
    query_weight,
    key_weight,
    value_weight,
    output_weight,
    gate_weight,
    up_weight,
    down_weight,
    norm_scales,
):
    line_count = lax.axis_size("line")
    plane_count = lax.axis_size("plane")
    fsdp_count = lax.axis_size("fsdp")
    sharers = plane_count * fsdp_count
    line_place = lax.axis_index("line")
    plane_place = lax.axis_index("plane")
    core = lax.axis_index("fsdp")
    devices = line_count * plane_count
    model = tokens.shape[2]
    row_count = tokens.shape[1]
    half_rows = row_count // 2
    span = 2 * row_count
    group_size = HEADS // KV_HEADS
    query_local = query_weight.shape[1]
    key_local = key_weight.shape[1]
    ff_local = gate_weight.shape[1]
    query_width = query_local * sharers
    key_width = key_local * sharers
    chunks = range(2)

    attn_local = jnp.concatenate(
        [jnp.concatenate([query_weight, key_weight, value_weight], axis=1).T, output_weight], axis=0
    )
    attn_flat = lax.all_gather(attn_local, ("plane", "fsdp"), axis=0, tiled=False)
    core_ref = core.astype(jnp.int32)[None]
    place_ref = jnp.stack([plane_place, core]).astype(jnp.int32)
    paired_local = jnp.concatenate([gate_weight.T, up_weight.T], axis=0)
    paired_all = lax.all_gather(paired_local, ("fsdp", "plane"), axis=0, tiled=True)
    down_all = lax.all_gather(down_weight, ("fsdp", "plane"), axis=0, tiled=True)

    edge_one = query_local
    edge_two = edge_one + key_local
    edge_three = edge_two + key_local
    edge_four = edge_three + output_weight.shape[0]
    pair_ids = jnp.arange(devices, dtype=jnp.int32)
    order = line_order()

    def places(members, chunk):
        lines = order[2 * chunk : 2 * chunk + 2]
        index = (lines[None, :] * plane_count + members[:, None]).reshape(-1)
        pair = jnp.sum(
            jnp.where(index[:, None] == pair_ids[None, :], pair_table[None, :], 0), axis=1
        )
        offsets = jnp.arange(row_count, dtype=jnp.int32)
        return jnp.where(
            offsets[None, :] < half_rows,
            pair[:, None] * half_rows + offsets[None, :],
            (2 * devices - 1 - pair[:, None]) * half_rows + offsets[None, :] - half_rows,
        ).reshape(-1)

    members = jnp.stack([jnp.asarray(member, jnp.int32) for member in plane_order()])
    positions = [places(plane_place[None], c) for c in chunks]
    key_positions = jnp.concatenate([places(members, c) for c in chunks])
    tables = [rope_tables(positions[c]) for c in chunks]
    key_bases = key_positions.reshape(-1, half_rows)[:, 0]
    tables, key_bases = lax.optimization_barrier((tables, key_bases))
    scales = norm_scales.astype(WIDE)

    tokens_own = tokens[0]
    tokens_line, normed_first, queries = [None] * 2, [None] * 2, [None] * 2

    def packed(held):
        return jnp.concatenate(
            [
                held[:, :edge_one].reshape(-1, model),
                held[:, edge_one:edge_two].reshape(-1, model),
                held[:, edge_two:edge_three].reshape(-1, model),
            ],
            axis=0,
        )

    def project(c, rows):
        tokens_line[c] = rows
        weights = attn_flat if plane_count == 4 else packed(attn_flat)
        normed_first[c], queries[c], both = project_call(
            rows, weights, scales[0:1], *tables[c], query_width, key_width
        )
        return plane_gather(both)

    pair_all = jnp.concatenate(line_gather(tokens_own, project)[:2], axis=0)
    attn_held = tie(attn_flat, queries[1])
    output_all = attn_held[:, edge_three:].reshape(-1, model)

    attn_full, attn_low, inverse_sums = [None] * 2, [None] * 2, [None] * 2

    def attend(c):
        attn_full[c], attn_low[c], inverse_sums[c] = attend_call(
            queries[c], pair_all, positions[c][:, None], key_positions[None, :], group_size
        )
        return contract(attn_low[c], output_all, 1, 0)

    def reorder(gate, _):
        return packed(gate(attn_flat))

    branch_out, _, projection = line_scatter(
        attend(1), lambda: (attend(0), ()), while_last=reorder
    )

    inputs = tokens_own.astype(WIDE)
    inverse_two = inverse_root(branch_out)
    hidden = inputs + branch_out * inverse_two * scales[1]
    inverse_three = inverse_root(hidden)

    normed_second, mixed, mixed_away = [None] * 2, [None] * 2, [None] * 2
    bent, slope = [None] * 2, [None] * 2

    def widen(c, rows):
        normed_second[c] = rows
        mixed[c], mixed_away[c], bent[c], slope[c] = widen_call(rows, paired_all, core_ref, sharers)
        return mixed[c]

    line_gather((hidden * inverse_three * scales[2]).astype(LOW), widen)

    def keep(gate, _):
        return (
            [sibling(gate(part)) for part in mixed_away],
            [sibling(gate(part)) for part in normed_second],
        )

    ffn_out, _, (mixed_theirs, second_theirs) = line_scatter(
        contract(mixed[1], down_all, 0, 0),
        lambda: (contract(mixed[0], down_all, 0, 0), ()),
        while_last=keep,
    )

    inverse_four = inverse_root(ffn_out)
    result = hidden + ffn_out * inverse_four * scales[3]
    upstream = cotangent[0].astype(WIDE)
    ffn_grad = norm_back(ffn_out, inverse_four, scales[3], upstream)

    ffn_grad_low, pair_grad, pair_away = [None] * 2, [None] * 2, [None] * 2

    def narrow_back(c, rows):
        ffn_grad_low[c] = rows
        pair_grad[c], pair_away[c] = narrow_back_call(
            rows, down_all, bent[c], slope[c], core_ref, sharers
        )
        return pair_grad[c]

    line_gather(ffn_grad.astype(LOW), narrow_back)

    pair_theirs = [sibling(part) for part in pair_away]
    grad_theirs = [sibling(part) for part in ffn_grad_low]
    second_part = contract(jnp.concatenate(pair_grad, axis=1), paired_all, 0, 0)

    def give_down():
        return second_part[:span], weight_grad_call(
            [tie(part, second_part) for part in mixed],
            mixed_theirs,
            ffn_grad_low + grad_theirs,
            core_ref,
        )

    def give_paired(gate, _):
        return weight_grad_call(
            [gate(part) for part in pair_grad], pair_theirs, normed_second + second_theirs, core_ref
        )

    second_grad, down_grad, paired_grad = line_scatter(
        second_part[span:], give_down, while_last=give_paired
    )
    down_share = lax.psum_scatter(down_grad, "plane", scatter_dimension=0, tiled=True)
    paired_share = lax.psum_scatter(paired_grad, "plane", scatter_dimension=0, tiled=True)

    hidden_part = norm_back(hidden, inverse_three, scales[2], second_grad)
    hidden_grad = upstream + hidden_part
    branch_grad = norm_back(branch_out, inverse_two, scales[1], hidden_grad)

    branch_grad_low, query_raw_low, prior = [None] * 2, [None] * 2, [None] * 2

    def attend_back(c, rows):
        branch_grad_low[c] = rows
        grads = contract(rows, output_all, 1, 1).astype(LOW)
        query_raw_low[c], prior[c] = attend_back_call(
            queries[c],
            grads,
            attn_full[c],
            pair_all,
            inverse_sums[c],
            positions[c][None, :],
            key_bases,
            *tables[c],
            prior[0],
            group_size,
        )
        return query_raw_low[c], prior[c]

    def give_three(gate):
        sums = [
            jnp.sum(hidden_grad * gate(branch_out) * inverse_two, axis=0),
            jnp.sum(second_grad * gate(hidden) * inverse_three, axis=0),
            jnp.sum(upstream * gate(ffn_out) * inverse_four, axis=0),
        ]
        return jnp.stack(sums, axis=0)

    _, _, scale_three = line_gather(branch_grad.astype(LOW), attend_back, while_first=give_three)

    per_chunk = plane_count * span
    both_grads = jnp.concatenate(
        [prior[1][c * per_chunk : (c + 1) * per_chunk].reshape(plane_count, span, -1) for c in chunks],
        axis=1,
    ).reshape(2 * per_chunk, -1)
    own_terms = plane_scatter(both_grads)

    def shard_parts(left, right, parts):
        if plane_count == 4:
            return shard_grad_call(left, right, parts, place_ref, plane_count)
        grad = contract(
            jnp.concatenate(left, axis=0), jnp.concatenate(right, axis=0), 0, 0
        ).astype(LOW)
        blocks = [
            grad[first : first + rows * sharers].reshape(sharers, rows, model)
            for first, rows in parts
        ]
        blocks = jnp.concatenate(blocks, axis=1).reshape(plane_count, fsdp_count, -1, model)
        near = lax.dynamic_index_in_dim(blocks, core, 1, keepdims=False)
        return near, lax.dynamic_index_in_dim(blocks, 1 - core, 1, keepdims=False)

    output_near, output_away = shard_parts(
        [tie(part, prior[1]) for part in attn_low], branch_grad_low, [(0, edge_four - edge_three)]
    )
    own_terms = tie(own_terms, output_near)

    raw_low, first_part, low_part = [None] * 2, [None] * 2, [None] * 2

    def project_back(c):
        terms = [term[c * span : (c + 1) * span] for term in own_terms]
        raw_low[c], first_part[c], low_part[c] = project_back_call(
            query_raw_low[c], *terms, projection, *tables[c]
        )
        return first_part[c]

    all_count = devices * fsdp_count

    def give_projection():
        early = project_back(0)
        parts = shard_parts(
            [tie(part, early) for part in raw_low],
            normed_first,
            [
                (0, query_local),
                (query_width, key_local),
                (query_width + key_width, key_local),
            ],
        )
        return early, parts

    def give_far(gate, parts):
        near, away = parts
        total = jnp.concatenate(
            [
                near.astype(WIDE) + sibling(gate(away)).astype(WIDE),
                output_near.astype(WIDE) + sibling(gate(output_away)).astype(WIDE),
            ],
            axis=1,
        ).reshape(-1, model)
        scale_one = 0.0
        for c in chunks:
            wide_line = gate(tokens_line[c]).astype(WIDE)
            scale_one += jnp.sum(first_part[c] * (wide_line * inverse_root(wide_line)), axis=0)
        scale_grads = jnp.concatenate([scale_one[None], scale_three], axis=0)
        scale_cut = (
            scale_grads.reshape(4, all_count, -1).transpose(1, 0, 2).reshape(all_count, -1)
        )
        if plane_count == 4:
            return scale_cut, plane_scatter_far(total)
        return scale_cut, total

    first_grad, _, (scale_cut, attn_sends) = line_scatter(
        project_back(1), give_projection, while_last=give_far, low_far=low_part[1]
    )
    if plane_count == 4:
        own, send_one, send_two = attn_sends
        one, two = swap(send_one, 1), swap(send_two, 2)
    else:
        own, one, two = plane_scatter(attn_sends)

    input_part = norm_back(inputs, inverse_root(inputs), scales[0], first_grad)
    input_grad = hidden_grad + input_part

    gate_share = paired_share[:ff_local].T.astype(WIDE)
    up_share = paired_share[ff_local:].T.astype(WIDE)
    down_share = down_share.astype(WIDE)
    scale_cut = tie(scale_cut, gate_share, up_share, down_share)
    scale_cut = lax.all_to_all(scale_cut, EVERY, 0, 0, tiled=True)
    scale_share = jnp.sum(scale_cut, axis=0).reshape(4, -1)
    one, two = tie((one, two), input_grad, gate_share, up_share, down_share)
    attn_share = own + one.astype(WIDE) + two.astype(WIDE)

    return (
        result.astype(LOW)[None],
        input_grad.astype(LOW)[None],
        attn_share[:edge_one].T,
        attn_share[edge_one:edge_two].T,
        attn_share[edge_two:edge_three].T,
        attn_share[edge_three:],
        gate_share,
        up_share,
        down_share,
        scale_share,
    )


def solution(mesh):
    devices, fsdp_count = mesh.devices.shape
    inner = Mesh(
        mesh.devices.reshape(KV_HEADS, devices // KV_HEADS, fsdp_count), EVERY
    )
    rows = P("fsdp", ("line", "plane"), None)
    return jax.shard_map(
        shards,
        mesh=inner,
        in_specs=(
            rows,
            rows,
            P(),
            P(None, EVERY),
            P(None, EVERY),
            P(None, EVERY),
            P(EVERY, None),
            P(None, EVERY),
            P(None, EVERY),
            P(EVERY, None),
            P(),
        ),
        out_specs=(
            rows,
            rows,
            P(None, EVERY),
            P(None, EVERY),
            P(None, EVERY),
            P(EVERY, None),
            P(None, EVERY),
            P(None, EVERY),
            P(EVERY, None),
            P(None, EVERY),
        ),
        check_vma=False,
    )
```

```python
import functools

import jax
import jax.numpy as jnp
from jax import lax
from jax.experimental import pallas as pl
from jax.experimental.pallas import tpu as pltpu
from jax.sharding import Mesh, PartitionSpec as P

HEADS = 8
KV_HEADS = 4
HEAD = 256

EPSILON = 1e-06
SOFT_CAP = 50.0
QUERY_SCALE = 0.0625

LOW = jnp.bfloat16
WIDE = jnp.float32

EVERY = ("line", "plane", "fsdp")


def contract(left, right, left_dim, right_dim):
    return lax.dot_general(
        left, right, (((left_dim,), (right_dim,)), ((), ())), preferred_element_type=WIDE
    )


def inverse_root(matrix_in):
    return lax.rsqrt(jnp.mean(matrix_in * matrix_in, axis=-1, keepdims=True) + EPSILON)


def norm_back(matrix_in, inverse, scale_row, upstream):
    weighted = upstream * scale_row
    inner = jnp.mean(matrix_in * weighted, axis=-1, keepdims=True)
    return inverse * weighted - matrix_in * (inverse * inverse * inverse) * inner


def rope_tables(positions):
    half_size = HEAD // 2
    frequency = 10000.0 ** (-jnp.arange(half_size, dtype=WIDE) * 2.0 / HEAD)
    angles = positions.astype(WIDE)[:, None] * frequency[None, :]
    return (jnp.cos(angles), jnp.sin(angles))


VMEM_LIMIT = 56 * 1024 * 1024
COST = pl.CostEstimate(flops=0, bytes_accessed=64 * 1024 * 1024, transcendentals=0)


def params():
    return pltpu.CompilerParams(vmem_limit_bytes=VMEM_LIMIT)


def project_kernel(
    rows_ref, weight_ref, scale_ref, cos_ref, sin_ref, normed_ref, query_ref, pair_ref, *scratch
):
    key_width = pair_ref.shape[1] // 2
    query_width = query_ref.shape[0] // rows_ref.shape[0] * HEAD
    span = rows_ref.shape[0]
    packed = weight_ref
    if scratch:
        packed = scratch[0]
        sharers = weight_ref.shape[0]
        query_local, key_local = query_width // sharers, key_width // sharers
        for j in range(sharers):
            packed[j * query_local : (j + 1) * query_local] = weight_ref[j, :query_local]
            at = query_width + j * key_local
            from_row = query_local
            for _ in range(2):
                packed[at : at + key_local] = weight_ref[j, from_row : from_row + key_local]
                at += key_width
                from_row += key_local
    rows = rows_ref[...].astype(WIDE)
    inverse = lax.rsqrt(jnp.mean(rows * rows, axis=-1, keepdims=True) + EPSILON)
    normed = (rows * inverse * scale_ref[...]).astype(LOW)
    normed_ref[...] = normed
    cosine, sine_table = cos_ref[...], sin_ref[...]
    half = HEAD // 2

    def turn(raw):
        first, second = raw[:, :half], raw[:, half:]
        return first * cosine - second * sine_table, second * cosine + first * sine_table

    for head in range(query_width // HEAD):
        raw = contract(normed, packed[head * HEAD : (head + 1) * HEAD], 1, 1)
        first, second = turn(raw)
        query_ref[head * span : (head + 1) * span, :half] = (first * QUERY_SCALE).astype(LOW)
        query_ref[head * span : (head + 1) * span, half:] = (second * QUERY_SCALE).astype(LOW)
    raw = contract(normed, packed[query_width:], 1, 1)
    first, second = turn(raw[:, :key_width])
    pair_ref[:, :half] = first.astype(LOW)
    pair_ref[:, half:key_width] = second.astype(LOW)
    pair_ref[:, key_width:] = raw[:, key_width:].astype(LOW)


def project_call(rows, weights, scale_row, cosine, sine_table, query_width, key_width):
    span, model = rows.shape
    heads = query_width // HEAD
    return pl.pallas_call(
        project_kernel,
        out_shape=(
            jax.ShapeDtypeStruct((span, model), LOW),
            jax.ShapeDtypeStruct((heads * span, HEAD), LOW),
            jax.ShapeDtypeStruct((span, 2 * key_width), LOW),
        ),
        scratch_shapes=[pltpu.VMEM((query_width + 2 * key_width, model), LOW)]
        if weights.ndim == 3
        else [],
        compiler_params=params(),
        cost_estimate=COST,
    )(rows, weights, scale_row, cosine, sine_table)


KEY_BLOCK = 2048


def as_row(column):
    return jnp.broadcast_to(column, (column.shape[0], 128)).T[:1]


def attend_kernel(query_ref, pair_ref, place_ref, key_place_ref, out_ref, low_ref, inverse_ref):
    keys = pair_ref[:, :HEAD]
    values = pair_ref[:, HEAD:]
    bounded = jnp.tanh(contract(query_ref[...], keys, 1, 1) * (1.0 / SOFT_CAP))
    allowed = key_place_ref[...] <= place_ref[...]
    grown = jnp.where(allowed, jnp.exp(SOFT_CAP * bounded), 0.0)
    inverse = 1.0 / jnp.sum(grown, axis=-1, keepdims=True)
    weights = (grown * inverse).astype(LOW)
    out = contract(weights, values, 1, 0)
    out_ref[...] = out
    low_ref[...] = out.astype(LOW)
    inverse_ref[...] = as_row(inverse)


def attend_call(queries, pair, places_column, key_places_row, group_size):
    count = queries.shape[0]
    span = count // group_size
    keys = pair.shape[0]
    by_head = pl.BlockSpec((span, HEAD), lambda h: (0, h))
    return pl.pallas_call(
        attend_kernel,
        grid=(group_size,),
        in_specs=[
            pl.BlockSpec((span, HEAD), lambda h: (h, 0)),
            pl.BlockSpec((keys, 2 * HEAD), lambda h: (0, 0)),
            pl.BlockSpec((span, 1), lambda h: (0, 0)),
            pl.BlockSpec((1, keys), lambda h: (0, 0)),
        ],
        out_specs=[by_head, by_head, pl.BlockSpec((1, span), lambda h: (0, h))],
        out_shape=(
            jax.ShapeDtypeStruct((span, group_size * HEAD), WIDE),
            jax.ShapeDtypeStruct((span, group_size * HEAD), LOW),
            jax.ShapeDtypeStruct((1, count), WIDE),
        ),
        compiler_params=params(),
        cost_estimate=COST,
    )(queries, pair, places_column, key_places_row)


def attend_back_kernel(*refs):
    query_ref, grad_ref, out_ref, pair_ref, inverse_ref, place_ref, base_ref = refs[:7]
    cos_ref, sin_ref, *prior_refs, query_grad_ref, pair_grad_ref, total_ref, held_ref = refs[7:]
    part, head = pl.program_id(0), pl.program_id(1)
    keys = pair_ref[:, :HEAD]
    values = pair_ref[:, HEAD:]
    queries = query_ref[...]
    grads = grad_ref[...]
    inner = as_row(jnp.sum(grads.astype(WIDE) * out_ref[...], axis=-1, keepdims=True))
    bounded = jnp.tanh(contract(keys, queries, 1, 1) * (1.0 / SOFT_CAP))
    blocks = base_ref.shape[0] // pl.num_programs(0)
    rows = keys.shape[0] // blocks
    offsets = lax.broadcasted_iota(jnp.int32, (rows, 1), 0)
    key_places = jnp.concatenate(
        [base_ref[part * blocks + block] + offsets for block in range(blocks)], axis=0
    )
    allowed = key_places <= place_ref[...]
    weights = jnp.where(allowed, jnp.exp(SOFT_CAP * bounded) * inverse_ref[...], 0.0)
    weight_grad = contract(values, grads, 1, 1)
    score_grad = (weights * (weight_grad - inner) * (1.0 - bounded * bounded)).astype(LOW)
    query_part = contract(score_grad, keys, 0, 0)

    @pl.when(part == 0)
    def _():
        held_ref[head] = query_part

    @pl.when(part > 0)
    def _():
        held_ref[head] += query_part

    query_grad = held_ref[head]
    half = HEAD // 2
    first, second = query_grad[:, :half], query_grad[:, half:]
    cosine, sine_table = cos_ref[...], sin_ref[...]
    query_grad_ref[:, :half] = ((first * cosine + second * sine_table) * QUERY_SCALE).astype(LOW)
    query_grad_ref[:, half:] = ((second * cosine - first * sine_table) * QUERY_SCALE).astype(LOW)
    key_grad = contract(score_grad, queries, 1, 0)
    value_grad = contract(weights.astype(LOW), grads, 1, 0)

    @pl.when(head == 0)
    def _():
        if prior_refs:
            total_ref[:, :HEAD] = prior_refs[0][:, :HEAD] + key_grad
            total_ref[:, HEAD:] = prior_refs[0][:, HEAD:] + value_grad
        else:
            total_ref[:, :HEAD] = key_grad
            total_ref[:, HEAD:] = value_grad

    @pl.when(head > 0)
    def _():
        total_ref[:, :HEAD] += key_grad
        total_ref[:, HEAD:] += value_grad

    @pl.when(head == pl.num_programs(1) - 1)
    def _():
        pair_grad_ref[...] = total_ref[...].astype(pair_grad_ref.dtype)


def attend_back_call(
    queries, grads, out, pair, inverse, places_row, key_bases, cosine, sine_table, prior, group_size
):
    count = queries.shape[0]
    span = count // group_size
    keys = pair.shape[0]
    block = min(keys, KEY_BLOCK)
    by_head = pl.BlockSpec((span, HEAD), lambda k, h: (0, h))
    by_keys = pl.BlockSpec((block, 2 * HEAD), lambda k, h: (k, 0))
    table = pl.BlockSpec((span, HEAD // 2), lambda k, h: (0, 0))
    extra = [] if prior is None else [prior]
    return pl.pallas_call(
        attend_back_kernel,
        grid=(keys // block, group_size),
        in_specs=[
            pl.BlockSpec((span, HEAD), lambda k, h: (h, 0)),
            by_head,
            by_head,
            by_keys,
            pl.BlockSpec((1, span), lambda k, h: (0, h)),
            pl.BlockSpec((1, span), lambda k, h: (0, 0)),
            pl.BlockSpec(memory_space=pltpu.SMEM),
            table,
            table,
        ]
        + [by_keys] * len(extra),
        out_specs=[by_head, by_keys],
        out_shape=(
            jax.ShapeDtypeStruct((span, group_size * HEAD), LOW),
            jax.ShapeDtypeStruct((keys, 2 * HEAD), WIDE if prior is None else LOW),
        ),
        scratch_shapes=[
            pltpu.VMEM((block, 2 * HEAD), WIDE),
            pltpu.VMEM((group_size, span, HEAD), WIDE),
        ],
        compiler_params=params(),
        cost_estimate=COST,
    )(queries, grads, out, pair, inverse, places_row, key_bases, cosine, sine_table, *extra)


def project_back_kernel(
    query_ref, own_ref, one_ref, two_ref, weight_ref, cos_ref, sin_ref, raw_ref, part_ref, low_ref
):
    query_width = query_ref.shape[1]
    total = own_ref[...].astype(WIDE) + one_ref[...].astype(WIDE) + two_ref[...].astype(WIDE)
    half = HEAD // 2
    first, second = total[:, :half], total[:, half:HEAD]
    cosine, sine_table = cos_ref[...], sin_ref[...]
    raw_ref[:, :query_width] = query_ref[...]
    raw_ref[:, query_width : query_width + half] = (first * cosine + second * sine_table).astype(LOW)
    raw_ref[:, query_width + half : query_width + HEAD] = (
        second * cosine - first * sine_table
    ).astype(LOW)
    raw_ref[:, query_width + HEAD :] = total[:, HEAD:].astype(LOW)
    part = contract(raw_ref[...], weight_ref[...], 1, 0)
    part_ref[...] = part
    low_ref[...] = part[part.shape[0] // 2 :].astype(LOW)


def project_back_call(query_grad, own, one, two, weights, cosine, sine_table):
    span = query_grad.shape[0]
    width, model = weights.shape
    return pl.pallas_call(
        project_back_kernel,
        out_shape=(
            jax.ShapeDtypeStruct((span, width), LOW),
            jax.ShapeDtypeStruct((span, model), WIDE),
            jax.ShapeDtypeStruct((span // 2, model), LOW),
        ),
        compiler_params=params(),
        cost_estimate=COST,
    )(query_grad, own, one, two, weights, cosine, sine_table)


GELU_ROOT = 0.7978845608028654
GELU_CUBE = 0.044715


STEPS = 4


def blocks_of(value, count, first):
    rows = value.shape[0] // (2 * count)
    return jnp.concatenate(
        [value[(2 * p + first) * rows : (2 * p + first + 1) * rows] for p in range(count)], axis=0
    )


def widen_kernel(
    parts, core_ref, rows_ref, weight_ref, mixed_ref, away_ref, bent_ref, slope_ref
):
    step = pl.program_id(0)
    both = contract(weight_ref[...], rows_ref[...], 1, 1)
    gate, up = blocks_of(both, parts, 0), blocks_of(both, parts, 1)
    square = gate * gate
    curve = jnp.tanh(GELU_ROOT * gate * (1.0 + GELU_CUBE * square))
    rise = 0.5 * (1.0 + curve)
    bent = gate * rise
    mixed = (bent * up).astype(LOW)
    mixed_ref[...] = mixed
    bent_ref[...] = bent
    steep = GELU_ROOT * (1.0 + 3.0 * GELU_CUBE * square)
    slope_ref[...] = up * (rise + 0.5 * gate * (1.0 - curve * curve) * steep)

    @pl.when(step // (STEPS // 2) != core_ref[0])
    def _():
        away_ref[...] = mixed


def away_block(step, core_ref):
    first = (1 - core_ref[0]) * (STEPS // 2)
    return (jnp.clip(step - first, 0, STEPS // 2 - 1), 0)


def widen_call(rows, weights, core, sharers):
    span, model = rows.shape
    amount = weights.shape[0] // 2
    block = amount // STEPS
    by_step = pl.BlockSpec((block, span), lambda j, core_ref: (j, 0))
    return pl.pallas_call(
        functools.partial(widen_kernel, sharers // STEPS),
        grid_spec=pltpu.PrefetchScalarGridSpec(
            num_scalar_prefetch=1,
            grid=(STEPS,),
            in_specs=[
                pl.BlockSpec((span, model), lambda j, core_ref: (0, 0)),
                pl.BlockSpec((2 * block, model), lambda j, core_ref: (j, 0)),
            ],
            out_specs=[by_step, pl.BlockSpec((block, span), away_block), by_step, by_step],
        ),
        out_shape=(
            jax.ShapeDtypeStruct((amount, span), LOW),
            jax.ShapeDtypeStruct((amount // 2, span), LOW),
            jax.ShapeDtypeStruct((amount, span), WIDE),
            jax.ShapeDtypeStruct((amount, span), WIDE),
        ),
        compiler_params=params(),
        cost_estimate=COST,
    )(core, rows, weights)


def narrow_back_kernel(
    parts, core_ref, rows_ref, weight_ref, bent_ref, slope_ref, grad_ref, away_ref
):
    step = pl.program_id(0)
    mixed_grad = contract(weight_ref[...], rows_ref[...], 1, 1)
    gate, up = mixed_grad * slope_ref[...], mixed_grad * bent_ref[...]
    rows = gate.shape[0] // parts
    grad = jnp.concatenate(
        [part[p * rows : (p + 1) * rows] for p in range(parts) for part in (gate, up)], axis=0
    ).astype(LOW)
    grad_ref[...] = grad

    @pl.when(step // (STEPS // 2) != core_ref[0])
    def _():
        away_ref[...] = grad


def narrow_back_call(rows, weights, bent, slope, core, sharers):
    span, model = rows.shape
    amount = weights.shape[0]
    block = amount // STEPS
    by_step = pl.BlockSpec((block, span), lambda j, core_ref: (j, 0))
    return pl.pallas_call(
        functools.partial(narrow_back_kernel, sharers // STEPS),
        grid_spec=pltpu.PrefetchScalarGridSpec(
            num_scalar_prefetch=1,
            grid=(STEPS,),
            in_specs=[
                pl.BlockSpec((span, model), lambda j, core_ref: (0, 0)),
                pl.BlockSpec((block, model), lambda j, core_ref: (j, 0)),
                by_step,
                by_step,
            ],
            out_specs=[
                pl.BlockSpec((2 * block, span), lambda j, core_ref: (j, 0)),
                pl.BlockSpec((2 * block, span), away_block),
            ],
        ),
        out_shape=(
            jax.ShapeDtypeStruct((2 * amount, span), LOW),
            jax.ShapeDtypeStruct((amount, span), LOW),
        ),
        compiler_params=params(),
        cost_estimate=COST,
    )(core, rows, weights, bent, slope)


def weight_grad_kernel(core_ref, *refs):
    *pairs, out_ref, left_ref, right_ref = refs
    half = len(pairs) // 2

    @pl.when(pl.program_id(0) == 0)
    def _():
        first = 0
        for part in pairs[half:]:
            right_ref[first : first + part.shape[0]] = part[...]
            first += part.shape[0]

    first = 0
    for part in pairs[:half]:
        left_ref[:, first : first + part.shape[1]] = part[...]
        first += part.shape[1]
    out_ref[...] = contract(left_ref[...], right_ref[...], 1, 0).astype(LOW)


def weight_grad_call(own, away, rows, core):
    span, model = rows[0].shape
    amount = own[0].shape[0] // 2
    block = amount // STEPS
    mine = pl.BlockSpec((block, span), lambda j, core_ref: (core_ref[0] * STEPS + j, 0))
    theirs = pl.BlockSpec((block, span), lambda j, core_ref: (j, 0))
    whole = pl.BlockSpec((span, model), lambda j, core_ref: (0, 0))
    return pl.pallas_call(
        weight_grad_kernel,
        grid_spec=pltpu.PrefetchScalarGridSpec(
            num_scalar_prefetch=1,
            grid=(STEPS,),
            in_specs=[mine] * len(own) + [theirs] * len(away) + [whole] * len(rows),
            out_specs=pl.BlockSpec((block, model), lambda j, core_ref: (j, 0)),
            scratch_shapes=[
                pltpu.VMEM((block, len(rows) * span), LOW),
                pltpu.VMEM((len(rows) * span, model), LOW),
            ],
        ),
        out_shape=jax.ShapeDtypeStruct((amount, model), LOW),
        compiler_params=params(),
        cost_estimate=COST,
    )(core, *own, *away, *rows)


def shard_grad_kernel(parts, place_ref, *refs):
    *pairs, near_ref, away_ref, total_ref = refs
    half = len(pairs) // 2
    total = contract(pairs[0][...], pairs[half][...], 0, 0)
    for left, right in zip(pairs[1:half], pairs[half + 1 :]):
        total += contract(left[...], right[...], 0, 0)
    total_ref[...] = total.astype(LOW)
    own, core = place_ref[0], place_ref[1]
    planes = near_ref.shape[0]
    for plane in range(planes):
        for side in range(2):
            to_row = 0
            for first, rows in parts:
                block = total_ref[pl.ds(first + (2 * plane + side) * rows, rows)]

                @pl.when(core == side)
                def _():
                    near_ref[plane ^ own, pl.ds(to_row, rows)] = block

                @pl.when(core != side)
                def _():
                    away_ref[plane ^ own, pl.ds(to_row, rows)] = block

                to_row += rows


def shard_grad_call(left, right, parts, place, planes):
    width, model = left[0].shape[1], right[0].shape[1]
    rows = sum(part[1] for part in parts)
    shape = jax.ShapeDtypeStruct((planes, rows, model), LOW)
    return pl.pallas_call(
        functools.partial(shard_grad_kernel, parts),
        in_specs=[pl.BlockSpec(memory_space=pltpu.SMEM)]
        + [pl.BlockSpec(memory_space=pltpu.VMEM)] * (len(left) + len(right)),
        out_specs=[pl.BlockSpec(memory_space=pltpu.VMEM)] * 2,
        out_shape=(shape, shape),
        scratch_shapes=[pltpu.VMEM((width, model), LOW)],
        compiler_params=params(),
        cost_estimate=COST,
    )(place, *left, *right)


def tie(value, *others):
    return lax.optimization_barrier((value, others))[0]


def choose(flag, one, two):
    return jnp.where(flag, one, two)


def nothing(*others):
    return ()


def shift(value, step):
    count = lax.axis_size("line")
    return lax.ppermute(value, "line", [(at, (at + step) % count) for at in range(count)])


def line_gather(block, work, while_first=nothing):
    half = block.shape[0] // 2
    up, down = shift(block, 1), shift(block, -1)
    done = while_first(lambda value: tie(value, block))
    up, down, done_first = lax.optimization_barrier((up, down, done))
    far_low, far_high = shift(down[:half], -1), shift(up[half:], 1)
    first = work(0, jnp.concatenate([block, up], axis=0))
    far_low, far_high = tie((far_low, far_high), first)
    second = work(1, jnp.concatenate([down, far_low, far_high], axis=0))
    return first, second, done_first


def line_order():
    turns = jnp.array([0, 3, 1, 2], jnp.int32)
    return lax.rem(lax.axis_index("line").astype(jnp.int32) + turns, 4)


def line_scatter(late, work, while_last=nothing, low_far=None):
    rows = late.shape[0] // 2
    half = rows // 2
    following, far = late[:rows], late[rows:]
    low_far = far.astype(LOW) if low_far is None else low_far
    for_following, for_former = shift(low_far[:half], 1), shift(low_far[half:], -1)
    for_following, for_former, (early, done_first) = lax.optimization_barrier(
        (for_following, for_former, work())
    )
    own, former = early[:rows], early[rows:]
    sends = lax.optimization_barrier(
        (
            (following + jnp.pad(for_following, ((0, half), (0, 0))).astype(WIDE)).astype(LOW),
            (former + jnp.pad(for_former, ((half, 0), (0, 0))).astype(WIDE)).astype(LOW),
        )
    )
    terms = shift(sends[0], 1), shift(sends[1], -1)
    done = while_last(lambda value: tie(value, *sends), done_first)
    terms, done_last = lax.optimization_barrier((terms, done))
    return own + sum(term.astype(WIDE) for term in terms), done_first, done_last


def swap(value, bits):
    count = lax.axis_size("plane")
    return lax.ppermute(value, "plane", [(b, b ^ bits) for b in range(count)])


def plane_order():
    count = lax.axis_size("plane")
    if count == 4:
        own = lax.axis_index("plane")
        return [own, own ^ 1, own ^ 2, own ^ 3]
    return list(range(count))


def plane_gather(block):
    if lax.axis_size("plane") != 4:
        return lax.all_gather(block, "plane", axis=0, tiled=True)
    half = block.shape[0] // 2
    one, two = swap(block, 1), swap(block, 2)
    first, second = swap(two[:half], 1), swap(one[half:], 2)
    return jnp.concatenate([block, one, two, first, second], axis=0)


def plane_scatter_far(total):
    count = lax.axis_size("plane")
    rows = total.shape[0] // count
    half = rows // 2
    own, one, two, far = [total[i * rows : (i + 1) * rows] for i in range(count)]
    one, two = one.astype(WIDE), two.astype(WIDE)
    low_far = far.astype(LOW)
    for_two = swap(low_far[:half], 1).astype(WIDE)
    for_one = swap(low_far[half:], 2).astype(WIDE)
    send_one = (one + jnp.pad(for_one, ((half, 0), (0, 0)))).astype(LOW)
    send_two = (two + jnp.pad(for_two, ((0, half), (0, 0)))).astype(LOW)
    return own, send_one, send_two


def plane_scatter(total):
    if lax.axis_size("plane") != 4:
        summed = lax.psum_scatter(total, "plane", scatter_dimension=0, tiled=True)
        empty = jnp.zeros(summed.shape, LOW)
        return summed, empty, empty
    own, send_one, send_two = plane_scatter_far(total)
    return own, swap(send_one, 1), swap(send_two, 2)


def sibling(value):
    return lax.ppermute(value, "fsdp", [(0, 1), (1, 0)])


def shards(
    tokens,
    cotangent,
    pair_table,
    query_weight,
    key_weight,
    value_weight,
    output_weight,
    gate_weight,
    up_weight,
    down_weight,
    norm_scales,
):
    line_count = lax.axis_size("line")
    plane_count = lax.axis_size("plane")
    fsdp_count = lax.axis_size("fsdp")
    sharers = plane_count * fsdp_count
    line_place = lax.axis_index("line")
    plane_place = lax.axis_index("plane")
    core = lax.axis_index("fsdp")
    devices = line_count * plane_count
    model = tokens.shape[2]
    row_count = tokens.shape[1]
    half_rows = row_count // 2
    span = 2 * row_count
    group_size = HEADS // KV_HEADS
    query_local = query_weight.shape[1]
    key_local = key_weight.shape[1]
    ff_local = gate_weight.shape[1]
    query_width = query_local * sharers
    key_width = key_local * sharers
    chunks = range(2)

    attn_local = jnp.concatenate(
        [jnp.concatenate([query_weight, key_weight, value_weight], axis=1).T, output_weight], axis=0
    )
    attn_flat = lax.all_gather(attn_local, ("plane", "fsdp"), axis=0, tiled=False)
    core_ref = core.astype(jnp.int32)[None]
    place_ref = jnp.stack([plane_place, core]).astype(jnp.int32)
    paired_local = jnp.concatenate([gate_weight.T, up_weight.T], axis=0)
    paired_all = lax.all_gather(paired_local, ("fsdp", "plane"), axis=0, tiled=True)
    down_all = lax.all_gather(down_weight, ("fsdp", "plane"), axis=0, tiled=True)

    edge_one = query_local
    edge_two = edge_one + key_local
    edge_three = edge_two + key_local
    edge_four = edge_three + output_weight.shape[0]
    pair_ids = jnp.arange(devices, dtype=jnp.int32)
    order = line_order()

    def places(members, chunk):
        lines = order[2 * chunk : 2 * chunk + 2]
        index = (lines[None, :] * plane_count + members[:, None]).reshape(-1)
        pair = jnp.sum(
            jnp.where(index[:, None] == pair_ids[None, :], pair_table[None, :], 0), axis=1
        )
        offsets = jnp.arange(row_count, dtype=jnp.int32)
        return jnp.where(
            offsets[None, :] < half_rows,
            pair[:, None] * half_rows + offsets[None, :],
            (2 * devices - 1 - pair[:, None]) * half_rows + offsets[None, :] - half_rows,
        ).reshape(-1)

    members = jnp.stack([jnp.asarray(member, jnp.int32) for member in plane_order()])
    positions = [places(plane_place[None], c) for c in chunks]
    key_positions = jnp.concatenate([places(members, c) for c in chunks])
    tables = [rope_tables(positions[c]) for c in chunks]
    key_bases = key_positions.reshape(-1, half_rows)[:, 0]
    tables, key_bases = lax.optimization_barrier((tables, key_bases))
    scales = norm_scales.astype(WIDE)

    tokens_own = tokens[0]
    tokens_line, normed_first, queries = [None] * 2, [None] * 2, [None] * 2

    def packed(held):
        return jnp.concatenate(
            [
                held[:, :edge_one].reshape(-1, model),
                held[:, edge_one:edge_two].reshape(-1, model),
                held[:, edge_two:edge_three].reshape(-1, model),
            ],
            axis=0,
        )

    def project(c, rows):
        tokens_line[c] = rows
        weights = attn_flat if plane_count == 4 else packed(attn_flat)
        normed_first[c], queries[c], both = project_call(
            rows, weights, scales[0:1], *tables[c], query_width, key_width
        )
        return plane_gather(both)

    pair_all = jnp.concatenate(line_gather(tokens_own, project)[:2], axis=0)
    attn_held = tie(attn_flat, queries[1])
    output_all = attn_held[:, edge_three:].reshape(-1, model)

    attn_full, attn_low, inverse_sums = [None] * 2, [None] * 2, [None] * 2

    def attend(c):
        attn_full[c], attn_low[c], inverse_sums[c] = attend_call(
            queries[c], pair_all, positions[c][:, None], key_positions[None, :], group_size
        )
        return contract(attn_low[c], output_all, 1, 0)

    def reorder(gate, _):
        return packed(gate(attn_flat))

    branch_out, _, projection = line_scatter(
        attend(1), lambda: (attend(0), ()), while_last=reorder
    )

    inputs = tokens_own.astype(WIDE)
    inverse_two = inverse_root(branch_out)
    hidden = inputs + branch_out * inverse_two * scales[1]
    inverse_three = inverse_root(hidden)

    normed_second, mixed, mixed_away = [None] * 2, [None] * 2, [None] * 2
    bent, slope = [None] * 2, [None] * 2

    def widen(c, rows):
        normed_second[c] = rows
        mixed[c], mixed_away[c], bent[c], slope[c] = widen_call(rows, paired_all, core_ref, sharers)
        return mixed[c]

    line_gather((hidden * inverse_three * scales[2]).astype(LOW), widen)

    def keep(gate, _):
        return (
            [sibling(gate(part)) for part in mixed_away],
            [sibling(gate(part)) for part in normed_second],
        )

    ffn_out, _, (mixed_theirs, second_theirs) = line_scatter(
        contract(mixed[1], down_all, 0, 0),
        lambda: (contract(mixed[0], down_all, 0, 0), ()),
        while_last=keep,
    )

    inverse_four = inverse_root(ffn_out)
    result = hidden + ffn_out * inverse_four * scales[3]
    upstream = cotangent[0].astype(WIDE)
    ffn_grad = norm_back(ffn_out, inverse_four, scales[3], upstream)

    ffn_grad_low, pair_grad, pair_away = [None] * 2, [None] * 2, [None] * 2

    def narrow_back(c, rows):
        ffn_grad_low[c] = rows
        pair_grad[c], pair_away[c] = narrow_back_call(
            rows, down_all, bent[c], slope[c], core_ref, sharers
        )
        return pair_grad[c]

    line_gather(ffn_grad.astype(LOW), narrow_back)

    pair_theirs = [sibling(part) for part in pair_away]
    grad_theirs = [sibling(part) for part in ffn_grad_low]
    second_part = contract(jnp.concatenate(pair_grad, axis=1), paired_all, 0, 0)

    def give_down():
        return second_part[:span], weight_grad_call(
            [tie(part, second_part) for part in mixed],
            mixed_theirs,
            ffn_grad_low + grad_theirs,
            core_ref,
        )

    def give_paired(gate, _):
        return weight_grad_call(
            [gate(part) for part in pair_grad], pair_theirs, normed_second + second_theirs, core_ref
        )

    second_grad, down_grad, paired_grad = line_scatter(
        second_part[span:], give_down, while_last=give_paired
    )
    down_share = lax.psum_scatter(down_grad, "plane", scatter_dimension=0, tiled=True)
    paired_share = lax.psum_scatter(paired_grad, "plane", scatter_dimension=0, tiled=True)

    hidden_part = norm_back(hidden, inverse_three, scales[2], second_grad)
    hidden_grad = upstream + hidden_part
    branch_grad = norm_back(branch_out, inverse_two, scales[1], hidden_grad)

    branch_grad_low, query_raw_low, prior = [None] * 2, [None] * 2, [None] * 2

    def attend_back(c, rows):
        branch_grad_low[c] = rows
        grads = contract(rows, output_all, 1, 1).astype(LOW)
        query_raw_low[c], prior[c] = attend_back_call(
            queries[c],
            grads,
            attn_full[c],
            pair_all,
            inverse_sums[c],
            positions[c][None, :],
            key_bases,
            *tables[c],
            prior[0],
            group_size,
        )
        return query_raw_low[c], prior[c]

    def give_three(gate):
        sums = [
            jnp.sum(hidden_grad * gate(branch_out) * inverse_two, axis=0),
            jnp.sum(second_grad * gate(hidden) * inverse_three, axis=0),
            jnp.sum(upstream * gate(ffn_out) * inverse_four, axis=0),
        ]
        return jnp.stack(sums, axis=0)

    _, _, scale_three = line_gather(branch_grad.astype(LOW), attend_back, while_first=give_three)

    per_chunk = plane_count * span
    both_grads = jnp.concatenate(
        [prior[1][c * per_chunk : (c + 1) * per_chunk].reshape(plane_count, span, -1) for c in chunks],
        axis=1,
    ).reshape(2 * per_chunk, -1)
    own_terms = plane_scatter(both_grads)

    def shard_parts(left, right, parts):
        if plane_count == 4:
            return shard_grad_call(left, right, parts, place_ref, plane_count)
        grad = contract(
            jnp.concatenate(left, axis=0), jnp.concatenate(right, axis=0), 0, 0
        ).astype(LOW)
        blocks = [
            grad[first : first + rows * sharers].reshape(sharers, rows, model)
            for first, rows in parts
        ]
        blocks = jnp.concatenate(blocks, axis=1).reshape(plane_count, fsdp_count, -1, model)
        near = lax.dynamic_index_in_dim(blocks, core, 1, keepdims=False)
        return near, lax.dynamic_index_in_dim(blocks, 1 - core, 1, keepdims=False)

    output_near, output_away = shard_parts(
        [tie(part, prior[1]) for part in attn_low], branch_grad_low, [(0, edge_four - edge_three)]
    )
    own_terms = tie(own_terms, output_near)

    raw_low, first_part, low_part = [None] * 2, [None] * 2, [None] * 2

    def project_back(c):
        terms = [term[c * span : (c + 1) * span] for term in own_terms]
        raw_low[c], first_part[c], low_part[c] = project_back_call(
            query_raw_low[c], *terms, projection, *tables[c]
        )
        return first_part[c]

    all_count = devices * fsdp_count

    def give_projection():
        early = project_back(0)
        parts = shard_parts(
            [tie(part, early) for part in raw_low],
            normed_first,
            [
                (0, query_local),
                (query_width, key_local),
                (query_width + key_width, key_local),
            ],
        )
        return early, parts

    def give_far(gate, parts):
        near, away = parts
        total = jnp.concatenate(
            [
                near.astype(WIDE) + sibling(gate(away)).astype(WIDE),
                output_near.astype(WIDE) + sibling(gate(output_away)).astype(WIDE),
            ],
            axis=1,
        ).reshape(-1, model)
        scale_one = 0.0
        for c in chunks:
            wide_line = gate(tokens_line[c]).astype(WIDE)
            scale_one += jnp.sum(first_part[c] * (wide_line * inverse_root(wide_line)), axis=0)
        scale_grads = jnp.concatenate([scale_one[None], scale_three], axis=0)
        scale_cut = (
            scale_grads.reshape(4, all_count, -1).transpose(1, 0, 2).reshape(all_count, -1)
        )
        if plane_count == 4:
            return scale_cut, plane_scatter_far(total)
        return scale_cut, total

    first_grad, _, (scale_cut, attn_sends) = line_scatter(
        project_back(1), give_projection, while_last=give_far, low_far=low_part[1]
    )
    if plane_count == 4:
        own, send_one, send_two = attn_sends
        one, two = swap(send_one, 1), swap(send_two, 2)
    else:
        own, one, two = plane_scatter(attn_sends)

    input_part = norm_back(inputs, inverse_root(inputs), scales[0], first_grad)
    input_grad = hidden_grad + input_part

    gate_share = paired_share[:ff_local].T.astype(WIDE)
    up_share = paired_share[ff_local:].T.astype(WIDE)
    down_share = down_share.astype(WIDE)
    scale_cut = tie(scale_cut, gate_share, up_share, down_share)
    scale_cut = lax.all_to_all(scale_cut, EVERY, 0, 0, tiled=True)
    scale_share = jnp.sum(scale_cut, axis=0).reshape(4, -1)
    one, two = tie((one, two), input_grad, gate_share, up_share, down_share)
    attn_share = own + one.astype(WIDE) + two.astype(WIDE)

    return (
        result.astype(LOW)[None],
        input_grad.astype(LOW)[None],
        attn_share[:edge_one].T,
        attn_share[edge_one:edge_two].T,
        attn_share[edge_two:edge_three].T,
        attn_share[edge_three:],
        gate_share,
        up_share,
        down_share,
        scale_share,
    )


def solution(mesh):
    devices, fsdp_count = mesh.devices.shape
    inner = Mesh(
        mesh.devices.reshape(KV_HEADS, devices // KV_HEADS, fsdp_count), EVERY
    )
    rows = P("fsdp", ("line", "plane"), None)
    return jax.shard_map(
        shards,
        mesh=inner,
        in_specs=(
            rows,
            rows,
            P(),
            P(None, EVERY),
            P(None, EVERY),
            P(None, EVERY),
            P(EVERY, None),
            P(None, EVERY),
            P(None, EVERY),
            P(EVERY, None),
            P(),
        ),
        out_specs=(
            rows,
            rows,
            P(None, EVERY),
            P(None, EVERY),
            P(None, EVERY),
            P(EVERY, None),
            P(None, EVERY),
            P(None, EVERY),
            P(EVERY, None),
            P(None, EVERY),
        ),
        check_vma=False,
    )
```

```python
import functools

import jax
import jax.numpy as jnp
from jax import lax
from jax.experimental import pallas as pl
from jax.experimental.pallas import tpu as pltpu
from jax.sharding import Mesh, PartitionSpec as P

HEADS = 8
KV_HEADS = 4
HEAD = 256

EPSILON = 1e-06
SOFT_CAP = 50.0
QUERY_SCALE = 0.0625

LOW = jnp.bfloat16
WIDE = jnp.float32

EVERY = ("line", "plane", "fsdp")


def contract(left, right, left_dim, right_dim):
    return lax.dot_general(
        left, right, (((left_dim,), (right_dim,)), ((), ())), preferred_element_type=WIDE
    )


def inverse_root(matrix_in):
    return lax.rsqrt(jnp.mean(matrix_in * matrix_in, axis=-1, keepdims=True) + EPSILON)


def norm_back(matrix_in, inverse, scale_row, upstream):
    weighted = upstream * scale_row
    inner = jnp.mean(matrix_in * weighted, axis=-1, keepdims=True)
    return inverse * weighted - matrix_in * (inverse * inverse * inverse) * inner


def rope_tables(positions):
    half_size = HEAD // 2
    frequency = 10000.0 ** (-jnp.arange(half_size, dtype=WIDE) * 2.0 / HEAD)
    angles = positions.astype(WIDE)[:, None] * frequency[None, :]
    return (jnp.cos(angles), jnp.sin(angles))


VMEM_LIMIT = 56 * 1024 * 1024
COST = pl.CostEstimate(flops=0, bytes_accessed=64 * 1024 * 1024, transcendentals=0)


def params():
    return pltpu.CompilerParams(vmem_limit_bytes=VMEM_LIMIT)


def project_kernel(
    rows_ref, weight_ref, scale_ref, cos_ref, sin_ref, normed_ref, query_ref, pair_ref, *scratch
):
    key_width = pair_ref.shape[1] // 2
    query_width = query_ref.shape[0] // rows_ref.shape[0] * HEAD
    span = rows_ref.shape[0]
    packed = weight_ref
    if scratch:
        packed = scratch[0]
        sharers = weight_ref.shape[0]
        query_local, key_local = query_width // sharers, key_width // sharers
        for j in range(sharers):
            packed[j * query_local : (j + 1) * query_local] = weight_ref[j, :query_local]
            at = query_width + j * key_local
            from_row = query_local
            for _ in range(2):
                packed[at : at + key_local] = weight_ref[j, from_row : from_row + key_local]
                at += key_width
                from_row += key_local
    rows = rows_ref[...].astype(WIDE)
    inverse = lax.rsqrt(jnp.mean(rows * rows, axis=-1, keepdims=True) + EPSILON)
    normed = (rows * inverse * scale_ref[...]).astype(LOW)
    normed_ref[...] = normed
    cosine, sine_table = cos_ref[...], sin_ref[...]
    half = HEAD // 2

    def turn(raw):
        first, second = raw[:, :half], raw[:, half:]
        return first * cosine - second * sine_table, second * cosine + first * sine_table

    for head in range(query_width // HEAD):
        raw = contract(normed, packed[head * HEAD : (head + 1) * HEAD], 1, 1)
        first, second = turn(raw)
        query_ref[head * span : (head + 1) * span, :half] = (first * QUERY_SCALE).astype(LOW)
        query_ref[head * span : (head + 1) * span, half:] = (second * QUERY_SCALE).astype(LOW)
    raw = contract(normed, packed[query_width:], 1, 1)
    first, second = turn(raw[:, :key_width])
    pair_ref[:, :half] = first.astype(LOW)
    pair_ref[:, half:key_width] = second.astype(LOW)
    pair_ref[:, key_width:] = raw[:, key_width:].astype(LOW)


def project_call(rows, weights, scale_row, cosine, sine_table, query_width, key_width):
    span, model = rows.shape
    heads = query_width // HEAD
    return pl.pallas_call(
        project_kernel,
        out_shape=(
            jax.ShapeDtypeStruct((span, model), LOW),
            jax.ShapeDtypeStruct((heads * span, HEAD), LOW),
            jax.ShapeDtypeStruct((span, 2 * key_width), LOW),
        ),
        scratch_shapes=[pltpu.VMEM((query_width + 2 * key_width, model), LOW)]
        if weights.ndim == 3
        else [],
        compiler_params=params(),
        cost_estimate=COST,
    )(rows, weights, scale_row, cosine, sine_table)


KEY_BLOCK = 2048


def as_row(column):
    return jnp.broadcast_to(column, (column.shape[0], 128)).T[:1]


def attend_kernel(query_ref, pair_ref, place_ref, key_place_ref, out_ref, low_ref, inverse_ref):
    keys = pair_ref[:, :HEAD]
    values = pair_ref[:, HEAD:]
    bounded = jnp.tanh(contract(query_ref[...], keys, 1, 1) * (1.0 / SOFT_CAP))
    allowed = key_place_ref[...] <= place_ref[...]
    grown = jnp.where(allowed, jnp.exp(SOFT_CAP * bounded), 0.0)
    inverse = 1.0 / jnp.sum(grown, axis=-1, keepdims=True)
    weights = (grown * inverse).astype(LOW)
    out = contract(weights, values, 1, 0)
    out_ref[...] = out
    low_ref[...] = out.astype(LOW)
    inverse_ref[...] = as_row(inverse)


def attend_call(queries, pair, places_column, key_places_row, group_size):
    count = queries.shape[0]
    span = count // group_size
    keys = pair.shape[0]
    by_head = pl.BlockSpec((span, HEAD), lambda h: (0, h))
    return pl.pallas_call(
        attend_kernel,
        grid=(group_size,),
        in_specs=[
            pl.BlockSpec((span, HEAD), lambda h: (h, 0)),
            pl.BlockSpec((keys, 2 * HEAD), lambda h: (0, 0)),
            pl.BlockSpec((span, 1), lambda h: (0, 0)),
            pl.BlockSpec((1, keys), lambda h: (0, 0)),
        ],
        out_specs=[by_head, by_head, pl.BlockSpec((1, span), lambda h: (0, h))],
        out_shape=(
            jax.ShapeDtypeStruct((span, group_size * HEAD), WIDE),
            jax.ShapeDtypeStruct((span, group_size * HEAD), LOW),
            jax.ShapeDtypeStruct((1, count), WIDE),
        ),
        compiler_params=params(),
        cost_estimate=COST,
    )(queries, pair, places_column, key_places_row)


def attend_back_kernel(*refs):
    query_ref, grad_ref, out_ref, pair_ref, inverse_ref, place_ref, base_ref = refs[:7]
    cos_ref, sin_ref, *prior_refs, query_grad_ref, pair_grad_ref, total_ref, held_ref = refs[7:]
    part, head = pl.program_id(0), pl.program_id(1)
    keys = pair_ref[:, :HEAD]
    values = pair_ref[:, HEAD:]
    queries = query_ref[...]
    grads = grad_ref[...]
    inner = as_row(jnp.sum(grads.astype(WIDE) * out_ref[...], axis=-1, keepdims=True))
    bounded = jnp.tanh(contract(keys, queries, 1, 1) * (1.0 / SOFT_CAP))
    blocks = base_ref.shape[0] // pl.num_programs(0)
    rows = keys.shape[0] // blocks
    offsets = lax.broadcasted_iota(jnp.int32, (rows, 1), 0)
    key_places = jnp.concatenate(
        [base_ref[part * blocks + block] + offsets for block in range(blocks)], axis=0
    )
    allowed = key_places <= place_ref[...]
    weights = jnp.where(allowed, jnp.exp(SOFT_CAP * bounded) * inverse_ref[...], 0.0)
    weight_grad = contract(values, grads, 1, 1)
    score_grad = (weights * (weight_grad - inner) * (1.0 - bounded * bounded)).astype(LOW)
    query_part = contract(score_grad, keys, 0, 0)

    @pl.when(part == 0)
    def _():
        held_ref[head] = query_part

    @pl.when(part > 0)
    def _():
        held_ref[head] += query_part

    query_grad = held_ref[head]
    half = HEAD // 2
    first, second = query_grad[:, :half], query_grad[:, half:]
    cosine, sine_table = cos_ref[...], sin_ref[...]
    query_grad_ref[:, :half] = ((first * cosine + second * sine_table) * QUERY_SCALE).astype(LOW)
    query_grad_ref[:, half:] = ((second * cosine - first * sine_table) * QUERY_SCALE).astype(LOW)
    key_grad = contract(score_grad, queries, 1, 0)
    value_grad = contract(weights.astype(LOW), grads, 1, 0)

    @pl.when(head == 0)
    def _():
        if prior_refs:
            total_ref[:, :HEAD] = prior_refs[0][:, :HEAD] + key_grad
            total_ref[:, HEAD:] = prior_refs[0][:, HEAD:] + value_grad
        else:
            total_ref[:, :HEAD] = key_grad
            total_ref[:, HEAD:] = value_grad

    @pl.when(head > 0)
    def _():
        total_ref[:, :HEAD] += key_grad
        total_ref[:, HEAD:] += value_grad

    @pl.when(head == pl.num_programs(1) - 1)
    def _():
        pair_grad_ref[...] = total_ref[...].astype(pair_grad_ref.dtype)


def attend_back_call(
    queries, grads, out, pair, inverse, places_row, key_bases, cosine, sine_table, prior, group_size
):
    count = queries.shape[0]
    span = count // group_size
    keys = pair.shape[0]
    block = min(keys, KEY_BLOCK)
    by_head = pl.BlockSpec((span, HEAD), lambda k, h: (0, h))
    by_keys = pl.BlockSpec((block, 2 * HEAD), lambda k, h: (k, 0))
    table = pl.BlockSpec((span, HEAD // 2), lambda k, h: (0, 0))
    extra = [] if prior is None else [prior]
    return pl.pallas_call(
        attend_back_kernel,
        grid=(keys // block, group_size),
        in_specs=[
            pl.BlockSpec((span, HEAD), lambda k, h: (h, 0)),
            by_head,
            by_head,
            by_keys,
            pl.BlockSpec((1, span), lambda k, h: (0, h)),
            pl.BlockSpec((1, span), lambda k, h: (0, 0)),
            pl.BlockSpec(memory_space=pltpu.SMEM),
            table,
            table,
        ]
        + [by_keys] * len(extra),
        out_specs=[by_head, by_keys],
        out_shape=(
            jax.ShapeDtypeStruct((span, group_size * HEAD), LOW),
            jax.ShapeDtypeStruct((keys, 2 * HEAD), WIDE if prior is None else LOW),
        ),
        scratch_shapes=[
            pltpu.VMEM((block, 2 * HEAD), WIDE),
            pltpu.VMEM((group_size, span, HEAD), WIDE),
        ],
        compiler_params=params(),
        cost_estimate=COST,
    )(queries, grads, out, pair, inverse, places_row, key_bases, cosine, sine_table, *extra)


def project_back_kernel(
    query_ref, own_ref, one_ref, two_ref, weight_ref, cos_ref, sin_ref, raw_ref, part_ref, low_ref
):
    query_width = query_ref.shape[1]
    total = own_ref[...].astype(WIDE) + one_ref[...].astype(WIDE) + two_ref[...].astype(WIDE)
    half = HEAD // 2
    first, second = total[:, :half], total[:, half:HEAD]
    cosine, sine_table = cos_ref[...], sin_ref[...]
    raw_ref[:, :query_width] = query_ref[...]
    raw_ref[:, query_width : query_width + half] = (first * cosine + second * sine_table).astype(LOW)
    raw_ref[:, query_width + half : query_width + HEAD] = (
        second * cosine - first * sine_table
    ).astype(LOW)
    raw_ref[:, query_width + HEAD :] = total[:, HEAD:].astype(LOW)
    part = contract(raw_ref[...], weight_ref[...], 1, 0)
    part_ref[...] = part
    low_ref[...] = part[part.shape[0] // 2 :].astype(LOW)


def project_back_call(query_grad, own, one, two, weights, cosine, sine_table):
    span = query_grad.shape[0]
    width, model = weights.shape
    return pl.pallas_call(
        project_back_kernel,
        out_shape=(
            jax.ShapeDtypeStruct((span, width), LOW),
            jax.ShapeDtypeStruct((span, model), WIDE),
            jax.ShapeDtypeStruct((span // 2, model), LOW),
        ),
        compiler_params=params(),
        cost_estimate=COST,
    )(query_grad, own, one, two, weights, cosine, sine_table)


GELU_ROOT = 0.7978845608028654
GELU_CUBE = 0.044715


STEPS = 4


def blocks_of(value, count, first):
    rows = value.shape[0] // (2 * count)
    return jnp.concatenate(
        [value[(2 * p + first) * rows : (2 * p + first + 1) * rows] for p in range(count)], axis=0
    )


def widen_kernel(
    parts, core_ref, rows_ref, weight_ref, mixed_ref, away_ref, bent_ref, slope_ref
):
    step = pl.program_id(0)
    both = contract(weight_ref[...], rows_ref[...], 1, 1)
    gate, up = blocks_of(both, parts, 0), blocks_of(both, parts, 1)
    square = gate * gate
    curve = jnp.tanh(GELU_ROOT * gate * (1.0 + GELU_CUBE * square))
    rise = 0.5 * (1.0 + curve)
    bent = gate * rise
    mixed = (bent * up).astype(LOW)
    mixed_ref[...] = mixed
    bent_ref[...] = bent
    steep = GELU_ROOT * (1.0 + 3.0 * GELU_CUBE * square)
    slope_ref[...] = up * (rise + 0.5 * gate * (1.0 - curve * curve) * steep)

    @pl.when(step // (STEPS // 2) != core_ref[0])
    def _():
        away_ref[...] = mixed


def away_block(step, core_ref):
    first = (1 - core_ref[0]) * (STEPS // 2)
    return (jnp.clip(step - first, 0, STEPS // 2 - 1), 0)


def widen_call(rows, weights, core, sharers):
    span, model = rows.shape
    amount = weights.shape[0] // 2
    block = amount // STEPS
    by_step = pl.BlockSpec((block, span), lambda j, core_ref: (j, 0))
    return pl.pallas_call(
        functools.partial(widen_kernel, sharers // STEPS),
        grid_spec=pltpu.PrefetchScalarGridSpec(
            num_scalar_prefetch=1,
            grid=(STEPS,),
            in_specs=[
                pl.BlockSpec((span, model), lambda j, core_ref: (0, 0)),
                pl.BlockSpec((2 * block, model), lambda j, core_ref: (j, 0)),
            ],
            out_specs=[by_step, pl.BlockSpec((block, span), away_block), by_step, by_step],
        ),
        out_shape=(
            jax.ShapeDtypeStruct((amount, span), LOW),
            jax.ShapeDtypeStruct((amount // 2, span), LOW),
            jax.ShapeDtypeStruct((amount, span), WIDE),
            jax.ShapeDtypeStruct((amount, span), WIDE),
        ),
        compiler_params=params(),
        cost_estimate=COST,
    )(core, rows, weights)


def narrow_back_kernel(
    parts, core_ref, rows_ref, weight_ref, bent_ref, slope_ref, grad_ref, away_ref
):
    step = pl.program_id(0)
    mixed_grad = contract(weight_ref[...], rows_ref[...], 1, 1)
    gate, up = mixed_grad * slope_ref[...], mixed_grad * bent_ref[...]
    rows = gate.shape[0] // parts
    grad = jnp.concatenate(
        [part[p * rows : (p + 1) * rows] for p in range(parts) for part in (gate, up)], axis=0
    ).astype(LOW)
    grad_ref[...] = grad

    @pl.when(step // (STEPS // 2) != core_ref[0])
    def _():
        away_ref[...] = grad


def narrow_back_call(rows, weights, bent, slope, core, sharers):
    span, model = rows.shape
    amount = weights.shape[0]
    block = amount // STEPS
    by_step = pl.BlockSpec((block, span), lambda j, core_ref: (j, 0))
    return pl.pallas_call(
        functools.partial(narrow_back_kernel, sharers // STEPS),
        grid_spec=pltpu.PrefetchScalarGridSpec(
            num_scalar_prefetch=1,
            grid=(STEPS,),
            in_specs=[
                pl.BlockSpec((span, model), lambda j, core_ref: (0, 0)),
                pl.BlockSpec((block, model), lambda j, core_ref: (j, 0)),
                by_step,
                by_step,
            ],
            out_specs=[
                pl.BlockSpec((2 * block, span), lambda j, core_ref: (j, 0)),
                pl.BlockSpec((2 * block, span), away_block),
            ],
        ),
        out_shape=(
            jax.ShapeDtypeStruct((2 * amount, span), LOW),
            jax.ShapeDtypeStruct((amount, span), LOW),
        ),
        compiler_params=params(),
        cost_estimate=COST,
    )(core, rows, weights, bent, slope)


def weight_grad_kernel(core_ref, *refs):
    *pairs, out_ref, left_ref, right_ref = refs
    half = len(pairs) // 2

    @pl.when(pl.program_id(0) == 0)
    def _():
        first = 0
        for part in pairs[half:]:
            right_ref[first : first + part.shape[0]] = part[...]
            first += part.shape[0]

    first = 0
    for part in pairs[:half]:
        left_ref[:, first : first + part.shape[1]] = part[...]
        first += part.shape[1]
    out_ref[...] = contract(left_ref[...], right_ref[...], 1, 0).astype(LOW)


def weight_grad_call(own, away, rows, core):
    span, model = rows[0].shape
    amount = own[0].shape[0] // 2
    block = amount // STEPS
    mine = pl.BlockSpec((block, span), lambda j, core_ref: (core_ref[0] * STEPS + j, 0))
    theirs = pl.BlockSpec((block, span), lambda j, core_ref: (j, 0))
    whole = pl.BlockSpec((span, model), lambda j, core_ref: (0, 0))
    return pl.pallas_call(
        weight_grad_kernel,
        grid_spec=pltpu.PrefetchScalarGridSpec(
            num_scalar_prefetch=1,
            grid=(STEPS,),
            in_specs=[mine] * len(own) + [theirs] * len(away) + [whole] * len(rows),
            out_specs=pl.BlockSpec((block, model), lambda j, core_ref: (j, 0)),
            scratch_shapes=[
                pltpu.VMEM((block, len(rows) * span), LOW),
                pltpu.VMEM((len(rows) * span, model), LOW),
            ],
        ),
        out_shape=jax.ShapeDtypeStruct((amount, model), LOW),
        compiler_params=params(),
        cost_estimate=COST,
    )(core, *own, *away, *rows)


def shard_grad_kernel(parts, place_ref, *refs):
    *pairs, near_ref, away_ref, total_ref = refs
    half = len(pairs) // 2
    total = contract(pairs[0][...], pairs[half][...], 0, 0)
    for left, right in zip(pairs[1:half], pairs[half + 1 :]):
        total += contract(left[...], right[...], 0, 0)
    total_ref[...] = total.astype(LOW)
    own, core = place_ref[0], place_ref[1]
    planes = near_ref.shape[0]
    for plane in range(planes):
        for side in range(2):
            to_row = 0
            for first, rows in parts:
                block = total_ref[pl.ds(first + (2 * plane + side) * rows, rows)]

                @pl.when(core == side)
                def _():
                    near_ref[plane ^ own, pl.ds(to_row, rows)] = block

                @pl.when(core != side)
                def _():
                    away_ref[plane ^ own, pl.ds(to_row, rows)] = block

                to_row += rows


def shard_grad_call(left, right, parts, place, planes):
    width, model = left[0].shape[1], right[0].shape[1]
    rows = sum(part[1] for part in parts)
    shape = jax.ShapeDtypeStruct((planes, rows, model), LOW)
    return pl.pallas_call(
        functools.partial(shard_grad_kernel, parts),
        in_specs=[pl.BlockSpec(memory_space=pltpu.SMEM)]
        + [pl.BlockSpec(memory_space=pltpu.VMEM)] * (len(left) + len(right)),
        out_specs=[pl.BlockSpec(memory_space=pltpu.VMEM)] * 2,
        out_shape=(shape, shape),
        scratch_shapes=[pltpu.VMEM((width, model), LOW)],
        compiler_params=params(),
        cost_estimate=COST,
    )(place, *left, *right)


def tie(value, *others):
    return lax.optimization_barrier((value, others))[0]


def choose(flag, one, two):
    return jnp.where(flag, one, two)


def nothing(*others):
    return ()


def shift(value, step):
    count = lax.axis_size("line")
    return lax.ppermute(value, "line", [(at, (at + step) % count) for at in range(count)])


def line_gather(block, work, while_first=nothing):
    half = block.shape[0] // 2
    up, down = shift(block, 1), shift(block, -1)
    done = while_first(lambda value: tie(value, block))
    up, down, done_first = lax.optimization_barrier((up, down, done))
    far_low, far_high = shift(down[:half], -1), shift(up[half:], 1)
    first = work(0, jnp.concatenate([block, up], axis=0))
    far_low, far_high = tie((far_low, far_high), first)
    second = work(1, jnp.concatenate([down, far_low, far_high], axis=0))
    return first, second, done_first


def line_order():
    turns = jnp.array([0, 3, 1, 2], jnp.int32)
    return lax.rem(lax.axis_index("line").astype(jnp.int32) + turns, 4)


def line_scatter(late, work, while_last=nothing, low_far=None):
    rows = late.shape[0] // 2
    half = rows // 2
    following, far = late[:rows], late[rows:]
    low_far = far.astype(LOW) if low_far is None else low_far
    for_following, for_former = shift(low_far[:half], 1), shift(low_far[half:], -1)
    for_following, for_former, (early, done_first) = lax.optimization_barrier(
        (for_following, for_former, work())
    )
    own, former = early[:rows], early[rows:]
    sends = lax.optimization_barrier(
        (
            (following + jnp.pad(for_following, ((0, half), (0, 0))).astype(WIDE)).astype(LOW),
            (former + jnp.pad(for_former, ((half, 0), (0, 0))).astype(WIDE)).astype(LOW),
        )
    )
    terms = shift(sends[0], 1), shift(sends[1], -1)
    done = while_last(lambda value: tie(value, *sends), done_first)
    terms, done_last = lax.optimization_barrier((terms, done))
    return own + sum(term.astype(WIDE) for term in terms), done_first, done_last


def swap(value, bits):
    count = lax.axis_size("plane")
    return lax.ppermute(value, "plane", [(b, b ^ bits) for b in range(count)])


def plane_order():
    count = lax.axis_size("plane")
    if count == 4:
        own = lax.axis_index("plane")
        return [own, own ^ 1, own ^ 2, own ^ 3]
    return list(range(count))


def plane_gather(block):
    if lax.axis_size("plane") != 4:
        return lax.all_gather(block, "plane", axis=0, tiled=True)
    half = block.shape[0] // 2
    one, two = swap(block, 1), swap(block, 2)
    first, second = swap(two[:half], 1), swap(one[half:], 2)
    return jnp.concatenate([block, one, two, first, second], axis=0)


def plane_scatter_far(total):
    count = lax.axis_size("plane")
    rows = total.shape[0] // count
    half = rows // 2
    own, one, two, far = [total[i * rows : (i + 1) * rows] for i in range(count)]
    one, two = one.astype(WIDE), two.astype(WIDE)
    low_far = far.astype(LOW)
    for_two = swap(low_far[:half], 1).astype(WIDE)
    for_one = swap(low_far[half:], 2).astype(WIDE)
    send_one = (one + jnp.pad(for_one, ((half, 0), (0, 0)))).astype(LOW)
    send_two = (two + jnp.pad(for_two, ((0, half), (0, 0)))).astype(LOW)
    return own, send_one, send_two


def plane_scatter(total):
    if lax.axis_size("plane") != 4:
        summed = lax.psum_scatter(total, "plane", scatter_dimension=0, tiled=True)
        empty = jnp.zeros(summed.shape, LOW)
        return summed, empty, empty
    own, send_one, send_two = plane_scatter_far(total)
    return own, swap(send_one, 1), swap(send_two, 2)


def sibling(value):
    return lax.ppermute(value, "fsdp", [(0, 1), (1, 0)])


def shards(
    tokens,
    cotangent,
    pair_table,
    query_weight,
    key_weight,
    value_weight,
    output_weight,
    gate_weight,
    up_weight,
    down_weight,
    norm_scales,
):
    line_count = lax.axis_size("line")
    plane_count = lax.axis_size("plane")
    fsdp_count = lax.axis_size("fsdp")
    sharers = plane_count * fsdp_count
    line_place = lax.axis_index("line")
    plane_place = lax.axis_index("plane")
    core = lax.axis_index("fsdp")
    devices = line_count * plane_count
    model = tokens.shape[2]
    row_count = tokens.shape[1]
    half_rows = row_count // 2
    span = 2 * row_count
    group_size = HEADS // KV_HEADS
    query_local = query_weight.shape[1]
    key_local = key_weight.shape[1]
    ff_local = gate_weight.shape[1]
    query_width = query_local * sharers
    key_width = key_local * sharers
    chunks = range(2)

    attn_local = jnp.concatenate(
        [jnp.concatenate([query_weight, key_weight, value_weight], axis=1).T, output_weight], axis=0
    )
    attn_flat = lax.all_gather(attn_local, ("plane", "fsdp"), axis=0, tiled=False)
    core_ref = core.astype(jnp.int32)[None]
    place_ref = jnp.stack([plane_place, core]).astype(jnp.int32)
    paired_local = jnp.concatenate([gate_weight.T, up_weight.T], axis=0)
    paired_all = lax.all_gather(paired_local, ("fsdp", "plane"), axis=0, tiled=True)
    down_all = lax.all_gather(down_weight, ("fsdp", "plane"), axis=0, tiled=True)

    edge_one = query_local
    edge_two = edge_one + key_local
    edge_three = edge_two + key_local
    edge_four = edge_three + output_weight.shape[0]
    pair_ids = jnp.arange(devices, dtype=jnp.int32)
    order = line_order()

    def places(members, chunk):
        lines = order[2 * chunk : 2 * chunk + 2]
        index = (lines[None, :] * plane_count + members[:, None]).reshape(-1)
        pair = jnp.sum(
            jnp.where(index[:, None] == pair_ids[None, :], pair_table[None, :], 0), axis=1
        )
        offsets = jnp.arange(row_count, dtype=jnp.int32)
        return jnp.where(
            offsets[None, :] < half_rows,
            pair[:, None] * half_rows + offsets[None, :],
            (2 * devices - 1 - pair[:, None]) * half_rows + offsets[None, :] - half_rows,
        ).reshape(-1)

    members = jnp.stack([jnp.asarray(member, jnp.int32) for member in plane_order()])
    positions = [places(plane_place[None], c) for c in chunks]
    key_positions = jnp.concatenate([places(members, c) for c in chunks])
    tables = [rope_tables(positions[c]) for c in chunks]
    key_bases = key_positions.reshape(-1, half_rows)[:, 0]
    tables, key_bases = lax.optimization_barrier((tables, key_bases))
    scales = norm_scales.astype(WIDE)

    tokens_own = tokens[0]
    tokens_line, normed_first, queries = [None] * 2, [None] * 2, [None] * 2

    def packed(held):
        return jnp.concatenate(
            [
                held[:, :edge_one].reshape(-1, model),
                held[:, edge_one:edge_two].reshape(-1, model),
                held[:, edge_two:edge_three].reshape(-1, model),
            ],
            axis=0,
        )

    def project(c, rows):
        tokens_line[c] = rows
        weights = attn_flat if plane_count == 4 else packed(attn_flat)
        normed_first[c], queries[c], both = project_call(
            rows, weights, scales[0:1], *tables[c], query_width, key_width
        )
        return plane_gather(both)

    pair_all = jnp.concatenate(line_gather(tokens_own, project)[:2], axis=0)
    attn_held = tie(attn_flat, queries[1])
    output_all = attn_held[:, edge_three:].reshape(-1, model)

    attn_full, attn_low, inverse_sums = [None] * 2, [None] * 2, [None] * 2

    def attend(c):
        attn_full[c], attn_low[c], inverse_sums[c] = attend_call(
            queries[c], pair_all, positions[c][:, None], key_positions[None, :], group_size
        )
        return contract(attn_low[c], output_all, 1, 0)

    def reorder(gate, _):
        return packed(gate(attn_flat))

    branch_out, _, projection = line_scatter(
        attend(1), lambda: (attend(0), ()), while_last=reorder
    )

    inputs = tokens_own.astype(WIDE)
    inverse_two = inverse_root(branch_out)
    hidden = inputs + branch_out * inverse_two * scales[1]
    inverse_three = inverse_root(hidden)

    normed_second, mixed, mixed_away = [None] * 2, [None] * 2, [None] * 2
    bent, slope = [None] * 2, [None] * 2

    def widen(c, rows):
        normed_second[c] = rows
        mixed[c], mixed_away[c], bent[c], slope[c] = widen_call(rows, paired_all, core_ref, sharers)
        return mixed[c]

    line_gather((hidden * inverse_three * scales[2]).astype(LOW), widen)

    mixed_theirs = [sibling(part) for part in mixed_away]
    second_theirs = [sibling(part) for part in normed_second]
    mixed[1] = tie(mixed[1], mixed_theirs, second_theirs)
    ffn_out, _, _ = line_scatter(
        contract(mixed[1], down_all, 0, 0), lambda: (contract(mixed[0], down_all, 0, 0), ())
    )

    inverse_four = inverse_root(ffn_out)
    result = hidden + ffn_out * inverse_four * scales[3]
    upstream = cotangent[0].astype(WIDE)
    ffn_grad = norm_back(ffn_out, inverse_four, scales[3], upstream)

    ffn_grad_low, pair_grad, pair_away = [None] * 2, [None] * 2, [None] * 2

    def narrow_back(c, rows):
        ffn_grad_low[c] = rows
        pair_grad[c], pair_away[c] = narrow_back_call(
            rows, down_all, bent[c], slope[c], core_ref, sharers
        )
        return pair_grad[c]

    line_gather(ffn_grad.astype(LOW), narrow_back)

    pair_theirs = [sibling(part) for part in pair_away]
    grad_theirs = [sibling(part) for part in ffn_grad_low]
    second_part = contract(jnp.concatenate(pair_grad, axis=1), paired_all, 0, 0)

    def give_down():
        return second_part[:span], weight_grad_call(
            [tie(part, second_part) for part in mixed],
            mixed_theirs,
            ffn_grad_low + grad_theirs,
            core_ref,
        )

    def give_paired(gate, _):
        return weight_grad_call(
            [gate(part) for part in pair_grad], pair_theirs, normed_second + second_theirs, core_ref
        )

    second_grad, down_grad, paired_grad = line_scatter(
        second_part[span:], give_down, while_last=give_paired
    )
    down_share = lax.psum_scatter(down_grad, "plane", scatter_dimension=0, tiled=True)
    paired_share = lax.psum_scatter(paired_grad, "plane", scatter_dimension=0, tiled=True)

    hidden_part = norm_back(hidden, inverse_three, scales[2], second_grad)
    hidden_grad = upstream + hidden_part
    branch_grad = norm_back(branch_out, inverse_two, scales[1], hidden_grad)

    branch_grad_low, query_raw_low, prior = [None] * 2, [None] * 2, [None] * 2

    def attend_back(c, rows):
        branch_grad_low[c] = rows
        grads = contract(rows, output_all, 1, 1).astype(LOW)
        query_raw_low[c], prior[c] = attend_back_call(
            queries[c],
            grads,
            attn_full[c],
            pair_all,
            inverse_sums[c],
            positions[c][None, :],
            key_bases,
            *tables[c],
            prior[0],
            group_size,
        )
        return query_raw_low[c], prior[c]

    def give_three(gate):
        sums = [
            jnp.sum(hidden_grad * gate(branch_out) * inverse_two, axis=0),
            jnp.sum(second_grad * gate(hidden) * inverse_three, axis=0),
            jnp.sum(upstream * gate(ffn_out) * inverse_four, axis=0),
        ]
        return jnp.stack(sums, axis=0)

    _, _, scale_three = line_gather(branch_grad.astype(LOW), attend_back, while_first=give_three)

    per_chunk = plane_count * span
    both_grads = jnp.concatenate(
        [prior[1][c * per_chunk : (c + 1) * per_chunk].reshape(plane_count, span, -1) for c in chunks],
        axis=1,
    ).reshape(2 * per_chunk, -1)
    own_terms = plane_scatter(both_grads)

    def shard_parts(left, right, parts):
        if plane_count == 4:
            return shard_grad_call(left, right, parts, place_ref, plane_count)
        grad = contract(
            jnp.concatenate(left, axis=0), jnp.concatenate(right, axis=0), 0, 0
        ).astype(LOW)
        blocks = [
            grad[first : first + rows * sharers].reshape(sharers, rows, model)
            for first, rows in parts
        ]
        blocks = jnp.concatenate(blocks, axis=1).reshape(plane_count, fsdp_count, -1, model)
        near = lax.dynamic_index_in_dim(blocks, core, 1, keepdims=False)
        return near, lax.dynamic_index_in_dim(blocks, 1 - core, 1, keepdims=False)

    output_near, output_away = shard_parts(
        [tie(part, prior[1]) for part in attn_low], branch_grad_low, [(0, edge_four - edge_three)]
    )
    own_terms = tie(own_terms, output_near)

    raw_low, first_part, low_part = [None] * 2, [None] * 2, [None] * 2

    def project_back(c):
        terms = [term[c * span : (c + 1) * span] for term in own_terms]
        raw_low[c], first_part[c], low_part[c] = project_back_call(
            query_raw_low[c], *terms, projection, *tables[c]
        )
        return first_part[c]

    all_count = devices * fsdp_count

    def give_projection():
        early = project_back(0)
        parts = shard_parts(
            [tie(part, early) for part in raw_low],
            normed_first,
            [
                (0, query_local),
                (query_width, key_local),
                (query_width + key_width, key_local),
            ],
        )
        return early, parts

    def give_far(gate, parts):
        near, away = parts
        total = jnp.concatenate(
            [
                near.astype(WIDE) + sibling(gate(away)).astype(WIDE),
                output_near.astype(WIDE) + sibling(gate(output_away)).astype(WIDE),
            ],
            axis=1,
        ).reshape(-1, model)
        scale_one = 0.0
        for c in chunks:
            wide_line = gate(tokens_line[c]).astype(WIDE)
            scale_one += jnp.sum(first_part[c] * (wide_line * inverse_root(wide_line)), axis=0)
        scale_grads = jnp.concatenate([scale_one[None], scale_three], axis=0)
        scale_cut = (
            scale_grads.reshape(4, all_count, -1).transpose(1, 0, 2).reshape(all_count, -1)
        )
        if plane_count == 4:
            return scale_cut, plane_scatter_far(total)
        return scale_cut, total

    first_grad, _, (scale_cut, attn_sends) = line_scatter(
        project_back(1), give_projection, while_last=give_far, low_far=low_part[1]
    )
    if plane_count == 4:
        own, send_one, send_two = attn_sends
        one, two = swap(send_one, 1), swap(send_two, 2)
    else:
        own, one, two = plane_scatter(attn_sends)

    input_part = norm_back(inputs, inverse_root(inputs), scales[0], first_grad)
    input_grad = hidden_grad + input_part

    gate_share = paired_share[:ff_local].T.astype(WIDE)
    up_share = paired_share[ff_local:].T.astype(WIDE)
    down_share = down_share.astype(WIDE)
    scale_cut = tie(scale_cut, gate_share, up_share, down_share)
    scale_cut = lax.all_to_all(scale_cut, EVERY, 0, 0, tiled=True)
    scale_share = jnp.sum(scale_cut, axis=0).reshape(4, -1)
    one, two = tie((one, two), input_grad, gate_share, up_share, down_share)
    attn_share = own + one.astype(WIDE) + two.astype(WIDE)

    return (
        result.astype(LOW)[None],
        input_grad.astype(LOW)[None],
        attn_share[:edge_one].T,
        attn_share[edge_one:edge_two].T,
        attn_share[edge_two:edge_three].T,
        attn_share[edge_three:],
        gate_share,
        up_share,
        down_share,
        scale_share,
    )


def solution(mesh):
    devices, fsdp_count = mesh.devices.shape
    inner = Mesh(
        mesh.devices.reshape(KV_HEADS, devices // KV_HEADS, fsdp_count), EVERY
    )
    rows = P("fsdp", ("line", "plane"), None)
    return jax.shard_map(
        shards,
        mesh=inner,
        in_specs=(
            rows,
            rows,
            P(),
            P(None, EVERY),
            P(None, EVERY),
            P(None, EVERY),
            P(EVERY, None),
            P(None, EVERY),
            P(None, EVERY),
            P(EVERY, None),
            P(),
        ),
        out_specs=(
            rows,
            rows,
            P(None, EVERY),
            P(None, EVERY),
            P(None, EVERY),
            P(EVERY, None),
            P(None, EVERY),
            P(None, EVERY),
            P(EVERY, None),
            P(None, EVERY),
        ),
        check_vma=False,
    )
```

```python
import functools

import jax
import jax.numpy as jnp
from jax import lax
from jax.experimental import pallas as pl
from jax.experimental.pallas import tpu as pltpu
from jax.sharding import Mesh, PartitionSpec as P

HEADS = 8
KV_HEADS = 4
HEAD = 256

EPSILON = 1e-06
SOFT_CAP = 50.0
QUERY_SCALE = 0.0625

LOW = jnp.bfloat16
WIDE = jnp.float32

EVERY = ("line", "plane", "fsdp")


def contract(left, right, left_dim, right_dim):
    return lax.dot_general(
        left, right, (((left_dim,), (right_dim,)), ((), ())), preferred_element_type=WIDE
    )


def inverse_root(matrix_in):
    return lax.rsqrt(jnp.mean(matrix_in * matrix_in, axis=-1, keepdims=True) + EPSILON)


def norm_back(matrix_in, inverse, scale_row, upstream):
    weighted = upstream * scale_row
    inner = jnp.mean(matrix_in * weighted, axis=-1, keepdims=True)
    return inverse * weighted - matrix_in * (inverse * inverse * inverse) * inner


def rope_tables(positions):
    half_size = HEAD // 2
    frequency = 10000.0 ** (-jnp.arange(half_size, dtype=WIDE) * 2.0 / HEAD)
    angles = positions.astype(WIDE)[:, None] * frequency[None, :]
    return (jnp.cos(angles), jnp.sin(angles))


VMEM_LIMIT = 56 * 1024 * 1024
COST = pl.CostEstimate(flops=0, bytes_accessed=64 * 1024 * 1024, transcendentals=0)


def params():
    return pltpu.CompilerParams(vmem_limit_bytes=VMEM_LIMIT)


def project_kernel(
    rows_ref, weight_ref, scale_ref, cos_ref, sin_ref, normed_ref, query_ref, pair_ref, *scratch
):
    key_width = pair_ref.shape[1] // 2
    query_width = query_ref.shape[0] // rows_ref.shape[0] * HEAD
    span = rows_ref.shape[0]
    packed = weight_ref
    if scratch:
        packed = scratch[0]
        sharers = weight_ref.shape[0]
        query_local, key_local = query_width // sharers, key_width // sharers
        for j in range(sharers):
            packed[j * query_local : (j + 1) * query_local] = weight_ref[j, :query_local]
            at = query_width + j * key_local
            from_row = query_local
            for _ in range(2):
                packed[at : at + key_local] = weight_ref[j, from_row : from_row + key_local]
                at += key_width
                from_row += key_local
    rows = rows_ref[...].astype(WIDE)
    inverse = lax.rsqrt(jnp.mean(rows * rows, axis=-1, keepdims=True) + EPSILON)
    normed = (rows * inverse * scale_ref[...]).astype(LOW)
    normed_ref[...] = normed
    cosine, sine_table = cos_ref[...], sin_ref[...]
    half = HEAD // 2

    def turn(raw):
        first, second = raw[:, :half], raw[:, half:]
        return first * cosine - second * sine_table, second * cosine + first * sine_table

    for head in range(query_width // HEAD):
        raw = contract(normed, packed[head * HEAD : (head + 1) * HEAD], 1, 1)
        first, second = turn(raw)
        query_ref[head * span : (head + 1) * span, :half] = (first * QUERY_SCALE).astype(LOW)
        query_ref[head * span : (head + 1) * span, half:] = (second * QUERY_SCALE).astype(LOW)
    raw = contract(normed, packed[query_width:], 1, 1)
    first, second = turn(raw[:, :key_width])
    pair_ref[:, :half] = first.astype(LOW)
    pair_ref[:, half:key_width] = second.astype(LOW)
    pair_ref[:, key_width:] = raw[:, key_width:].astype(LOW)


def project_call(rows, weights, scale_row, cosine, sine_table, query_width, key_width):
    span, model = rows.shape
    heads = query_width // HEAD
    return pl.pallas_call(
        project_kernel,
        out_shape=(
            jax.ShapeDtypeStruct((span, model), LOW),
            jax.ShapeDtypeStruct((heads * span, HEAD), LOW),
            jax.ShapeDtypeStruct((span, 2 * key_width), LOW),
        ),
        scratch_shapes=[pltpu.VMEM((query_width + 2 * key_width, model), LOW)]
        if weights.ndim == 3
        else [],
        compiler_params=params(),
        cost_estimate=COST,
    )(rows, weights, scale_row, cosine, sine_table)


KEY_BLOCK = 2048


def as_row(column):
    return jnp.broadcast_to(column, (column.shape[0], 128)).T[:1]


def attend_kernel(query_ref, pair_ref, place_ref, key_place_ref, out_ref, low_ref, inverse_ref):
    keys = pair_ref[:, :HEAD]
    values = pair_ref[:, HEAD:]
    bounded = jnp.tanh(contract(query_ref[...], keys, 1, 1) * (1.0 / SOFT_CAP))
    allowed = key_place_ref[...] <= place_ref[...]
    grown = jnp.where(allowed, jnp.exp(SOFT_CAP * bounded), 0.0)
    inverse = 1.0 / jnp.sum(grown, axis=-1, keepdims=True)
    weights = (grown * inverse).astype(LOW)
    out = contract(weights, values, 1, 0)
    out_ref[...] = out
    low_ref[...] = out.astype(LOW)
    inverse_ref[...] = as_row(inverse)


def attend_call(queries, pair, places_column, key_places_row, group_size):
    count = queries.shape[0]
    span = count // group_size
    keys = pair.shape[0]
    by_head = pl.BlockSpec((span, HEAD), lambda h: (0, h))
    return pl.pallas_call(
        attend_kernel,
        grid=(group_size,),
        in_specs=[
            pl.BlockSpec((span, HEAD), lambda h: (h, 0)),
            pl.BlockSpec((keys, 2 * HEAD), lambda h: (0, 0)),
            pl.BlockSpec((span, 1), lambda h: (0, 0)),
            pl.BlockSpec((1, keys), lambda h: (0, 0)),
        ],
        out_specs=[by_head, by_head, pl.BlockSpec((1, span), lambda h: (0, h))],
        out_shape=(
            jax.ShapeDtypeStruct((span, group_size * HEAD), WIDE),
            jax.ShapeDtypeStruct((span, group_size * HEAD), LOW),
            jax.ShapeDtypeStruct((1, count), WIDE),
        ),
        compiler_params=params(),
        cost_estimate=COST,
    )(queries, pair, places_column, key_places_row)


def attend_back_kernel(*refs):
    query_ref, grad_ref, out_ref, pair_ref, inverse_ref, place_ref, base_ref = refs[:7]
    cos_ref, sin_ref, *prior_refs, query_grad_ref, pair_grad_ref, total_ref, held_ref = refs[7:]
    part, head = pl.program_id(0), pl.program_id(1)
    keys = pair_ref[:, :HEAD]
    values = pair_ref[:, HEAD:]
    queries = query_ref[...]
    grads = grad_ref[...]
    inner = as_row(jnp.sum(grads.astype(WIDE) * out_ref[...], axis=-1, keepdims=True))
    bounded = jnp.tanh(contract(keys, queries, 1, 1) * (1.0 / SOFT_CAP))
    blocks = base_ref.shape[0] // pl.num_programs(0)
    rows = keys.shape[0] // blocks
    offsets = lax.broadcasted_iota(jnp.int32, (rows, 1), 0)
    key_places = jnp.concatenate(
        [base_ref[part * blocks + block] + offsets for block in range(blocks)], axis=0
    )
    allowed = key_places <= place_ref[...]
    weights = jnp.where(allowed, jnp.exp(SOFT_CAP * bounded) * inverse_ref[...], 0.0)
    weight_grad = contract(values, grads, 1, 1)
    score_grad = (weights * (weight_grad - inner) * (1.0 - bounded * bounded)).astype(LOW)
    query_part = contract(score_grad, keys, 0, 0)

    @pl.when(part == 0)
    def _():
        held_ref[head] = query_part

    @pl.when(part > 0)
    def _():
        held_ref[head] += query_part

    query_grad = held_ref[head]
    half = HEAD // 2
    first, second = query_grad[:, :half], query_grad[:, half:]
    cosine, sine_table = cos_ref[...], sin_ref[...]
    query_grad_ref[:, :half] = ((first * cosine + second * sine_table) * QUERY_SCALE).astype(LOW)
    query_grad_ref[:, half:] = ((second * cosine - first * sine_table) * QUERY_SCALE).astype(LOW)
    key_grad = contract(score_grad, queries, 1, 0)
    value_grad = contract(weights.astype(LOW), grads, 1, 0)

    @pl.when(head == 0)
    def _():
        if prior_refs:
            total_ref[:, :HEAD] = prior_refs[0][:, :HEAD] + key_grad
            total_ref[:, HEAD:] = prior_refs[0][:, HEAD:] + value_grad
        else:
            total_ref[:, :HEAD] = key_grad
            total_ref[:, HEAD:] = value_grad

    @pl.when(head > 0)
    def _():
        total_ref[:, :HEAD] += key_grad
        total_ref[:, HEAD:] += value_grad

    @pl.when(head == pl.num_programs(1) - 1)
    def _():
        pair_grad_ref[...] = total_ref[...].astype(pair_grad_ref.dtype)


def attend_back_call(
    queries, grads, out, pair, inverse, places_row, key_bases, cosine, sine_table, prior, group_size
):
    count = queries.shape[0]
    span = count // group_size
    keys = pair.shape[0]
    block = min(keys, KEY_BLOCK)
    by_head = pl.BlockSpec((span, HEAD), lambda k, h: (0, h))
    by_keys = pl.BlockSpec((block, 2 * HEAD), lambda k, h: (k, 0))
    table = pl.BlockSpec((span, HEAD // 2), lambda k, h: (0, 0))
    extra = [] if prior is None else [prior]
    return pl.pallas_call(
        attend_back_kernel,
        grid=(keys // block, group_size),
        in_specs=[
            pl.BlockSpec((span, HEAD), lambda k, h: (h, 0)),
            by_head,
            by_head,
            by_keys,
            pl.BlockSpec((1, span), lambda k, h: (0, h)),
            pl.BlockSpec((1, span), lambda k, h: (0, 0)),
            pl.BlockSpec(memory_space=pltpu.SMEM),
            table,
            table,
        ]
        + [by_keys] * len(extra),
        out_specs=[by_head, by_keys],
        out_shape=(
            jax.ShapeDtypeStruct((span, group_size * HEAD), LOW),
            jax.ShapeDtypeStruct((keys, 2 * HEAD), WIDE if prior is None else LOW),
        ),
        scratch_shapes=[
            pltpu.VMEM((block, 2 * HEAD), WIDE),
            pltpu.VMEM((group_size, span, HEAD), WIDE),
        ],
        compiler_params=params(),
        cost_estimate=COST,
    )(queries, grads, out, pair, inverse, places_row, key_bases, cosine, sine_table, *extra)


def project_back_kernel(
    query_ref, own_ref, one_ref, two_ref, weight_ref, cos_ref, sin_ref, raw_ref, part_ref, low_ref
):
    query_width = query_ref.shape[1]
    total = own_ref[...].astype(WIDE) + one_ref[...].astype(WIDE) + two_ref[...].astype(WIDE)
    half = HEAD // 2
    first, second = total[:, :half], total[:, half:HEAD]
    cosine, sine_table = cos_ref[...], sin_ref[...]
    raw_ref[:, :query_width] = query_ref[...]
    raw_ref[:, query_width : query_width + half] = (first * cosine + second * sine_table).astype(LOW)
    raw_ref[:, query_width + half : query_width + HEAD] = (
        second * cosine - first * sine_table
    ).astype(LOW)
    raw_ref[:, query_width + HEAD :] = total[:, HEAD:].astype(LOW)
    part = contract(raw_ref[...], weight_ref[...], 1, 0)
    part_ref[...] = part
    low_ref[...] = part[part.shape[0] // 2 :].astype(LOW)


def project_back_call(query_grad, own, one, two, weights, cosine, sine_table):
    span = query_grad.shape[0]
    width, model = weights.shape
    return pl.pallas_call(
        project_back_kernel,
        out_shape=(
            jax.ShapeDtypeStruct((span, width), LOW),
            jax.ShapeDtypeStruct((span, model), WIDE),
            jax.ShapeDtypeStruct((span // 2, model), LOW),
        ),
        compiler_params=params(),
        cost_estimate=COST,
    )(query_grad, own, one, two, weights, cosine, sine_table)


GELU_ROOT = 0.7978845608028654
GELU_CUBE = 0.044715


STEPS = 4


def blocks_of(value, count, first):
    rows = value.shape[0] // (2 * count)
    return jnp.concatenate(
        [value[(2 * p + first) * rows : (2 * p + first + 1) * rows] for p in range(count)], axis=0
    )


def widen_kernel(
    parts, core_ref, rows_ref, weight_ref, mixed_ref, away_ref, bent_ref, slope_ref
):
    step = pl.program_id(0)
    both = contract(weight_ref[...], rows_ref[...], 1, 1)
    gate, up = blocks_of(both, parts, 0), blocks_of(both, parts, 1)
    square = gate * gate
    curve = jnp.tanh(GELU_ROOT * gate * (1.0 + GELU_CUBE * square))
    rise = 0.5 * (1.0 + curve)
    bent = gate * rise
    mixed = (bent * up).astype(LOW)
    mixed_ref[...] = mixed
    bent_ref[...] = bent.astype(LOW)
    steep = GELU_ROOT * (1.0 + 3.0 * GELU_CUBE * square)
    slope = up * (rise + 0.5 * gate * (1.0 - curve * curve) * steep)
    slope_ref[...] = slope.astype(LOW)

    @pl.when(step // (STEPS // 2) != core_ref[0])
    def _():
        away_ref[...] = mixed


def away_block(step, core_ref):
    first = (1 - core_ref[0]) * (STEPS // 2)
    return (jnp.clip(step - first, 0, STEPS // 2 - 1), 0)


def widen_call(rows, weights, core, sharers):
    span, model = rows.shape
    amount = weights.shape[0] // 2
    block = amount // STEPS
    by_step = pl.BlockSpec((block, span), lambda j, core_ref: (j, 0))
    return pl.pallas_call(
        functools.partial(widen_kernel, sharers // STEPS),
        grid_spec=pltpu.PrefetchScalarGridSpec(
            num_scalar_prefetch=1,
            grid=(STEPS,),
            in_specs=[
                pl.BlockSpec((span, model), lambda j, core_ref: (0, 0)),
                pl.BlockSpec((2 * block, model), lambda j, core_ref: (j, 0)),
            ],
            out_specs=[by_step, pl.BlockSpec((block, span), away_block), by_step, by_step],
        ),
        out_shape=(
            jax.ShapeDtypeStruct((amount, span), LOW),
            jax.ShapeDtypeStruct((amount // 2, span), LOW),
            jax.ShapeDtypeStruct((amount, span), LOW),
            jax.ShapeDtypeStruct((amount, span), LOW),
        ),
        compiler_params=params(),
        cost_estimate=COST,
    )(core, rows, weights)


def narrow_back_kernel(
    parts, core_ref, rows_ref, weight_ref, bent_ref, slope_ref, grad_ref, away_ref
):
    step = pl.program_id(0)
    mixed_grad = contract(weight_ref[...], rows_ref[...], 1, 1)
    gate = mixed_grad * slope_ref[...].astype(WIDE)
    up = mixed_grad * bent_ref[...].astype(WIDE)
    rows = gate.shape[0] // parts
    grad = jnp.concatenate(
        [part[p * rows : (p + 1) * rows] for p in range(parts) for part in (gate, up)], axis=0
    ).astype(LOW)
    grad_ref[...] = grad

    @pl.when(step // (STEPS // 2) != core_ref[0])
    def _():
        away_ref[...] = grad


def narrow_back_call(rows, weights, bent, slope, core, sharers):
    span, model = rows.shape
    amount = weights.shape[0]
    block = amount // STEPS
    by_step = pl.BlockSpec((block, span), lambda j, core_ref: (j, 0))
    return pl.pallas_call(
        functools.partial(narrow_back_kernel, sharers // STEPS),
        grid_spec=pltpu.PrefetchScalarGridSpec(
            num_scalar_prefetch=1,
            grid=(STEPS,),
            in_specs=[
                pl.BlockSpec((span, model), lambda j, core_ref: (0, 0)),
                pl.BlockSpec((block, model), lambda j, core_ref: (j, 0)),
                by_step,
                by_step,
            ],
            out_specs=[
                pl.BlockSpec((2 * block, span), lambda j, core_ref: (j, 0)),
                pl.BlockSpec((2 * block, span), away_block),
            ],
        ),
        out_shape=(
            jax.ShapeDtypeStruct((2 * amount, span), LOW),
            jax.ShapeDtypeStruct((amount, span), LOW),
        ),
        compiler_params=params(),
        cost_estimate=COST,
    )(core, rows, weights, bent, slope)


def weight_grad_kernel(core_ref, *refs):
    *pairs, out_ref, left_ref, right_ref = refs
    half = len(pairs) // 2

    @pl.when(pl.program_id(0) == 0)
    def _():
        first = 0
        for part in pairs[half:]:
            right_ref[first : first + part.shape[0]] = part[...]
            first += part.shape[0]

    first = 0
    for part in pairs[:half]:
        left_ref[:, first : first + part.shape[1]] = part[...]
        first += part.shape[1]
    out_ref[...] = contract(left_ref[...], right_ref[...], 1, 0).astype(LOW)


def weight_grad_call(own, away, rows, core):
    span, model = rows[0].shape
    amount = own[0].shape[0] // 2
    block = amount // STEPS
    mine = pl.BlockSpec((block, span), lambda j, core_ref: (core_ref[0] * STEPS + j, 0))
    theirs = pl.BlockSpec((block, span), lambda j, core_ref: (j, 0))
    whole = pl.BlockSpec((span, model), lambda j, core_ref: (0, 0))
    return pl.pallas_call(
        weight_grad_kernel,
        grid_spec=pltpu.PrefetchScalarGridSpec(
            num_scalar_prefetch=1,
            grid=(STEPS,),
            in_specs=[mine] * len(own) + [theirs] * len(away) + [whole] * len(rows),
            out_specs=pl.BlockSpec((block, model), lambda j, core_ref: (j, 0)),
            scratch_shapes=[
                pltpu.VMEM((block, len(rows) * span), LOW),
                pltpu.VMEM((len(rows) * span, model), LOW),
            ],
        ),
        out_shape=jax.ShapeDtypeStruct((amount, model), LOW),
        compiler_params=params(),
        cost_estimate=COST,
    )(core, *own, *away, *rows)


def shard_grad_kernel(parts, place_ref, *refs):
    *pairs, near_ref, away_ref, total_ref = refs
    half = len(pairs) // 2
    total = contract(pairs[0][...], pairs[half][...], 0, 0)
    for left, right in zip(pairs[1:half], pairs[half + 1 :]):
        total += contract(left[...], right[...], 0, 0)
    total_ref[...] = total.astype(LOW)
    own, core = place_ref[0], place_ref[1]
    planes = near_ref.shape[0]
    for plane in range(planes):
        for side in range(2):
            to_row = 0
            for first, rows in parts:
                block = total_ref[pl.ds(first + (2 * plane + side) * rows, rows)]

                @pl.when(core == side)
                def _():
                    near_ref[plane ^ own, pl.ds(to_row, rows)] = block

                @pl.when(core != side)
                def _():
                    away_ref[plane ^ own, pl.ds(to_row, rows)] = block

                to_row += rows


def shard_grad_call(left, right, parts, place, planes):
    width, model = left[0].shape[1], right[0].shape[1]
    rows = sum(part[1] for part in parts)
    shape = jax.ShapeDtypeStruct((planes, rows, model), LOW)
    return pl.pallas_call(
        functools.partial(shard_grad_kernel, parts),
        in_specs=[pl.BlockSpec(memory_space=pltpu.SMEM)]
        + [pl.BlockSpec(memory_space=pltpu.VMEM)] * (len(left) + len(right)),
        out_specs=[pl.BlockSpec(memory_space=pltpu.VMEM)] * 2,
        out_shape=(shape, shape),
        scratch_shapes=[pltpu.VMEM((width, model), LOW)],
        compiler_params=params(),
        cost_estimate=COST,
    )(place, *left, *right)


def tie(value, *others):
    return lax.optimization_barrier((value, others))[0]


def choose(flag, one, two):
    return jnp.where(flag, one, two)


def nothing(*others):
    return ()


def shift(value, step):
    count = lax.axis_size("line")
    return lax.ppermute(value, "line", [(at, (at + step) % count) for at in range(count)])


def line_gather(block, work, while_first=nothing):
    half = block.shape[0] // 2
    up, down = shift(block, 1), shift(block, -1)
    done = while_first(lambda value: tie(value, block))
    up, down, done_first = lax.optimization_barrier((up, down, done))
    far_low, far_high = shift(down[:half], -1), shift(up[half:], 1)
    first = work(0, jnp.concatenate([block, up], axis=0))
    far_low, far_high = tie((far_low, far_high), first)
    second = work(1, jnp.concatenate([down, far_low, far_high], axis=0))
    return first, second, done_first


def line_order():
    turns = jnp.array([0, 3, 1, 2], jnp.int32)
    return lax.rem(lax.axis_index("line").astype(jnp.int32) + turns, 4)


def line_scatter(late, work, while_last=nothing, low_far=None):
    rows = late.shape[0] // 2
    half = rows // 2
    following, far = late[:rows], late[rows:]
    low_far = far.astype(LOW) if low_far is None else low_far
    for_following, for_former = shift(low_far[:half], 1), shift(low_far[half:], -1)
    for_following, for_former, (early, done_first) = lax.optimization_barrier(
        (for_following, for_former, work())
    )
    own, former = early[:rows], early[rows:]
    sends = lax.optimization_barrier(
        (
            (following + jnp.pad(for_following, ((0, half), (0, 0))).astype(WIDE)).astype(LOW),
            (former + jnp.pad(for_former, ((half, 0), (0, 0))).astype(WIDE)).astype(LOW),
        )
    )
    terms = shift(sends[0], 1), shift(sends[1], -1)
    done = while_last(lambda value: tie(value, *sends), done_first)
    terms, done_last = lax.optimization_barrier((terms, done))
    return own + sum(term.astype(WIDE) for term in terms), done_first, done_last


def swap(value, bits):
    count = lax.axis_size("plane")
    return lax.ppermute(value, "plane", [(b, b ^ bits) for b in range(count)])


def plane_order():
    count = lax.axis_size("plane")
    if count == 4:
        own = lax.axis_index("plane")
        return [own, own ^ 1, own ^ 2, own ^ 3]
    return list(range(count))


def plane_gather(block):
    if lax.axis_size("plane") != 4:
        return lax.all_gather(block, "plane", axis=0, tiled=True)
    half = block.shape[0] // 2
    one, two = swap(block, 1), swap(block, 2)
    first, second = swap(two[:half], 1), swap(one[half:], 2)
    return jnp.concatenate([block, one, two, first, second], axis=0)


def plane_scatter_far(total):
    count = lax.axis_size("plane")
    rows = total.shape[0] // count
    half = rows // 2
    own, one, two, far = [total[i * rows : (i + 1) * rows] for i in range(count)]
    one, two = one.astype(WIDE), two.astype(WIDE)
    low_far = far.astype(LOW)
    for_two = swap(low_far[:half], 1).astype(WIDE)
    for_one = swap(low_far[half:], 2).astype(WIDE)
    send_one = (one + jnp.pad(for_one, ((half, 0), (0, 0)))).astype(LOW)
    send_two = (two + jnp.pad(for_two, ((0, half), (0, 0)))).astype(LOW)
    return own, send_one, send_two


def plane_scatter(total):
    if lax.axis_size("plane") != 4:
        summed = lax.psum_scatter(total, "plane", scatter_dimension=0, tiled=True)
        empty = jnp.zeros(summed.shape, LOW)
        return summed, empty, empty
    own, send_one, send_two = plane_scatter_far(total)
    return own, swap(send_one, 1), swap(send_two, 2)


def sibling(value):
    return lax.ppermute(value, "fsdp", [(0, 1), (1, 0)])


def shards(
    tokens,
    cotangent,
    pair_table,
    query_weight,
    key_weight,
    value_weight,
    output_weight,
    gate_weight,
    up_weight,
    down_weight,
    norm_scales,
):
    line_count = lax.axis_size("line")
    plane_count = lax.axis_size("plane")
    fsdp_count = lax.axis_size("fsdp")
    sharers = plane_count * fsdp_count
    line_place = lax.axis_index("line")
    plane_place = lax.axis_index("plane")
    core = lax.axis_index("fsdp")
    devices = line_count * plane_count
    model = tokens.shape[2]
    row_count = tokens.shape[1]
    half_rows = row_count // 2
    span = 2 * row_count
    group_size = HEADS // KV_HEADS
    query_local = query_weight.shape[1]
    key_local = key_weight.shape[1]
    ff_local = gate_weight.shape[1]
    query_width = query_local * sharers
    key_width = key_local * sharers
    chunks = range(2)

    attn_local = jnp.concatenate(
        [jnp.concatenate([query_weight, key_weight, value_weight], axis=1).T, output_weight], axis=0
    )
    attn_flat = lax.all_gather(attn_local, ("plane", "fsdp"), axis=0, tiled=False)
    core_ref = core.astype(jnp.int32)[None]
    place_ref = jnp.stack([plane_place, core]).astype(jnp.int32)
    paired_local = jnp.concatenate([gate_weight.T, up_weight.T], axis=0)
    paired_all = lax.all_gather(paired_local, ("fsdp", "plane"), axis=0, tiled=True)
    down_all = lax.all_gather(down_weight, ("fsdp", "plane"), axis=0, tiled=True)

    edge_one = query_local
    edge_two = edge_one + key_local
    edge_three = edge_two + key_local
    edge_four = edge_three + output_weight.shape[0]
    pair_ids = jnp.arange(devices, dtype=jnp.int32)
    order = line_order()

    def places(members, chunk):
        lines = order[2 * chunk : 2 * chunk + 2]
        index = (lines[None, :] * plane_count + members[:, None]).reshape(-1)
        pair = jnp.sum(
            jnp.where(index[:, None] == pair_ids[None, :], pair_table[None, :], 0), axis=1
        )
        offsets = jnp.arange(row_count, dtype=jnp.int32)
        return jnp.where(
            offsets[None, :] < half_rows,
            pair[:, None] * half_rows + offsets[None, :],
            (2 * devices - 1 - pair[:, None]) * half_rows + offsets[None, :] - half_rows,
        ).reshape(-1)

    members = jnp.stack([jnp.asarray(member, jnp.int32) for member in plane_order()])
    positions = [places(plane_place[None], c) for c in chunks]
    key_positions = jnp.concatenate([places(members, c) for c in chunks])
    tables = [rope_tables(positions[c]) for c in chunks]
    key_bases = key_positions.reshape(-1, half_rows)[:, 0]
    tables, key_bases = lax.optimization_barrier((tables, key_bases))
    scales = norm_scales.astype(WIDE)

    tokens_own = tokens[0]
    tokens_line, normed_first, queries = [None] * 2, [None] * 2, [None] * 2

    def packed(held):
        return jnp.concatenate(
            [
                held[:, :edge_one].reshape(-1, model),
                held[:, edge_one:edge_two].reshape(-1, model),
                held[:, edge_two:edge_three].reshape(-1, model),
            ],
            axis=0,
        )

    def project(c, rows):
        tokens_line[c] = rows
        weights = attn_flat if plane_count == 4 else packed(attn_flat)
        normed_first[c], queries[c], both = project_call(
            rows, weights, scales[0:1], *tables[c], query_width, key_width
        )
        return plane_gather(both)

    pair_all = jnp.concatenate(line_gather(tokens_own, project)[:2], axis=0)
    attn_held = tie(attn_flat, queries[1])
    output_all = attn_held[:, edge_three:].reshape(-1, model)

    attn_full, attn_low, inverse_sums = [None] * 2, [None] * 2, [None] * 2

    def attend(c):
        attn_full[c], attn_low[c], inverse_sums[c] = attend_call(
            queries[c], pair_all, positions[c][:, None], key_positions[None, :], group_size
        )
        return contract(attn_low[c], output_all, 1, 0)

    def reorder(gate, _):
        return packed(gate(attn_flat))

    branch_out, _, projection = line_scatter(
        attend(1), lambda: (attend(0), ()), while_last=reorder
    )

    inputs = tokens_own.astype(WIDE)
    inverse_two = inverse_root(branch_out)
    hidden = inputs + branch_out * inverse_two * scales[1]
    inverse_three = inverse_root(hidden)

    normed_second, mixed, mixed_away = [None] * 2, [None] * 2, [None] * 2
    bent, slope = [None] * 2, [None] * 2

    def widen(c, rows):
        normed_second[c] = rows
        mixed[c], mixed_away[c], bent[c], slope[c] = widen_call(rows, paired_all, core_ref, sharers)
        return mixed[c]

    line_gather((hidden * inverse_three * scales[2]).astype(LOW), widen)

    mixed_theirs = [sibling(part) for part in mixed_away]
    second_theirs = [sibling(part) for part in normed_second]
    mixed[1] = tie(mixed[1], mixed_theirs, second_theirs)
    ffn_out, _, _ = line_scatter(
        contract(mixed[1], down_all, 0, 0), lambda: (contract(mixed[0], down_all, 0, 0), ())
    )

    inverse_four = inverse_root(ffn_out)
    result = hidden + ffn_out * inverse_four * scales[3]
    upstream = cotangent[0].astype(WIDE)
    ffn_grad = norm_back(ffn_out, inverse_four, scales[3], upstream)

    ffn_grad_low, pair_grad, pair_away = [None] * 2, [None] * 2, [None] * 2

    def narrow_back(c, rows):
        ffn_grad_low[c] = rows
        pair_grad[c], pair_away[c] = narrow_back_call(
            rows, down_all, bent[c], slope[c], core_ref, sharers
        )
        return pair_grad[c]

    line_gather(ffn_grad.astype(LOW), narrow_back)

    pair_theirs = [sibling(part) for part in pair_away]
    grad_theirs = [sibling(part) for part in ffn_grad_low]
    second_part = contract(jnp.concatenate(pair_grad, axis=1), paired_all, 0, 0)

    def give_down():
        return second_part[:span], weight_grad_call(
            [tie(part, second_part) for part in mixed],
            mixed_theirs,
            ffn_grad_low + grad_theirs,
            core_ref,
        )

    def give_paired(gate, _):
        return weight_grad_call(
            [gate(part) for part in pair_grad], pair_theirs, normed_second + second_theirs, core_ref
        )

    second_grad, down_grad, paired_grad = line_scatter(
        second_part[span:], give_down, while_last=give_paired
    )
    down_share = lax.psum_scatter(down_grad, "plane", scatter_dimension=0, tiled=True)
    paired_share = lax.psum_scatter(paired_grad, "plane", scatter_dimension=0, tiled=True)

    hidden_part = norm_back(hidden, inverse_three, scales[2], second_grad)
    hidden_grad = upstream + hidden_part
    branch_grad = norm_back(branch_out, inverse_two, scales[1], hidden_grad)

    branch_grad_low, query_raw_low, prior = [None] * 2, [None] * 2, [None] * 2

    def attend_back(c, rows):
        branch_grad_low[c] = rows
        grads = contract(rows, output_all, 1, 1).astype(LOW)
        query_raw_low[c], prior[c] = attend_back_call(
            queries[c],
            grads,
            attn_full[c],
            pair_all,
            inverse_sums[c],
            positions[c][None, :],
            key_bases,
            *tables[c],
            prior[0],
            group_size,
        )
        return query_raw_low[c], prior[c]

    def give_three(gate):
        sums = [
            jnp.sum(hidden_grad * gate(branch_out) * inverse_two, axis=0),
            jnp.sum(second_grad * gate(hidden) * inverse_three, axis=0),
            jnp.sum(upstream * gate(ffn_out) * inverse_four, axis=0),
        ]
        return jnp.stack(sums, axis=0)

    _, _, scale_three = line_gather(branch_grad.astype(LOW), attend_back, while_first=give_three)

    per_chunk = plane_count * span
    both_grads = jnp.concatenate(
        [prior[1][c * per_chunk : (c + 1) * per_chunk].reshape(plane_count, span, -1) for c in chunks],
        axis=1,
    ).reshape(2 * per_chunk, -1)
    own_terms = plane_scatter(both_grads)

    def shard_parts(left, right, parts):
        if plane_count == 4:
            return shard_grad_call(left, right, parts, place_ref, plane_count)
        grad = contract(
            jnp.concatenate(left, axis=0), jnp.concatenate(right, axis=0), 0, 0
        ).astype(LOW)
        blocks = [
            grad[first : first + rows * sharers].reshape(sharers, rows, model)
            for first, rows in parts
        ]
        blocks = jnp.concatenate(blocks, axis=1).reshape(plane_count, fsdp_count, -1, model)
        near = lax.dynamic_index_in_dim(blocks, core, 1, keepdims=False)
        return near, lax.dynamic_index_in_dim(blocks, 1 - core, 1, keepdims=False)

    output_near, output_away = shard_parts(
        [tie(part, prior[1]) for part in attn_low], branch_grad_low, [(0, edge_four - edge_three)]
    )
    own_terms = tie(own_terms, output_near)

    raw_low, first_part, low_part = [None] * 2, [None] * 2, [None] * 2

    def project_back(c):
        terms = [term[c * span : (c + 1) * span] for term in own_terms]
        raw_low[c], first_part[c], low_part[c] = project_back_call(
            query_raw_low[c], *terms, projection, *tables[c]
        )
        return first_part[c]

    all_count = devices * fsdp_count

    def give_projection():
        early = project_back(0)
        parts = shard_parts(
            [tie(part, early) for part in raw_low],
            normed_first,
            [
                (0, query_local),
                (query_width, key_local),
                (query_width + key_width, key_local),
            ],
        )
        return early, parts

    def give_far(gate, parts):
        near, away = parts
        total = jnp.concatenate(
            [
                near.astype(WIDE) + sibling(gate(away)).astype(WIDE),
                output_near.astype(WIDE) + sibling(gate(output_away)).astype(WIDE),
            ],
            axis=1,
        ).reshape(-1, model)
        scale_one = 0.0
        for c in chunks:
            wide_line = gate(tokens_line[c]).astype(WIDE)
            scale_one += jnp.sum(first_part[c] * (wide_line * inverse_root(wide_line)), axis=0)
        scale_grads = jnp.concatenate([scale_one[None], scale_three], axis=0)
        scale_cut = (
            scale_grads.reshape(4, all_count, -1).transpose(1, 0, 2).reshape(all_count, -1)
        )
        if plane_count == 4:
            return scale_cut, plane_scatter_far(total)
        return scale_cut, total

    first_grad, _, (scale_cut, attn_sends) = line_scatter(
        project_back(1), give_projection, while_last=give_far, low_far=low_part[1]
    )
    if plane_count == 4:
        own, send_one, send_two = attn_sends
        one, two = swap(send_one, 1), swap(send_two, 2)
    else:
        own, one, two = plane_scatter(attn_sends)

    input_part = norm_back(inputs, inverse_root(inputs), scales[0], first_grad)
    input_grad = hidden_grad + input_part

    gate_share = paired_share[:ff_local].T.astype(WIDE)
    up_share = paired_share[ff_local:].T.astype(WIDE)
    down_share = down_share.astype(WIDE)
    scale_cut = tie(scale_cut, gate_share, up_share, down_share)
    scale_cut = lax.all_to_all(scale_cut, EVERY, 0, 0, tiled=True)
    scale_share = jnp.sum(scale_cut, axis=0).reshape(4, -1)
    one, two = tie((one, two), input_grad, gate_share, up_share, down_share)
    attn_share = own + one.astype(WIDE) + two.astype(WIDE)

    return (
        result.astype(LOW)[None],
        input_grad.astype(LOW)[None],
        attn_share[:edge_one].T,
        attn_share[edge_one:edge_two].T,
        attn_share[edge_two:edge_three].T,
        attn_share[edge_three:],
        gate_share,
        up_share,
        down_share,
        scale_share,
    )


def solution(mesh):
    devices, fsdp_count = mesh.devices.shape
    inner = Mesh(
        mesh.devices.reshape(KV_HEADS, devices // KV_HEADS, fsdp_count), EVERY
    )
    rows = P("fsdp", ("line", "plane"), None)
    return jax.shard_map(
        shards,
        mesh=inner,
        in_specs=(
            rows,
            rows,
            P(),
            P(None, EVERY),
            P(None, EVERY),
            P(None, EVERY),
            P(EVERY, None),
            P(None, EVERY),
            P(None, EVERY),
            P(EVERY, None),
            P(),
        ),
        out_specs=(
            rows,
            rows,
            P(None, EVERY),
            P(None, EVERY),
            P(None, EVERY),
            P(EVERY, None),
            P(None, EVERY),
            P(None, EVERY),
            P(EVERY, None),
            P(None, EVERY),
        ),
        check_vma=False,
    )
```
